256 devices in a mesh: tm: 64 (over y, z, core), space: 4 (over x).
Axes of the slice: x: 4, y: 4, z: 8, core: 2. Of those that a mesh axis runs over, the one named last changes fastest.
Arguments:
- frames: bfloat16 [256, 32, 24, 384], P('tm', 'space'), may hold values from -6 to 6
- conv_weight: bfloat16 [27, 384, 384], replicated, may hold values from -0.0625 to 0.0625
- head_weight: bfloat16 [384, 32], replicated, may hold values from -0.3125 to 0.3125
- clip_len: int32 [21], replicated, may hold values from 1 to 21, 256 in all
Outputs:
- latent: float32 [256, 32, 24, 32], P('tm', 'space')
- loss: float32 [], replicated
- weight_grad: float32 [27, 384, 384], P(None, 'tm', 'space')
- head_grad: float32 [384, 32], P('tm', 'space')
The draws below stay inside these ranges and needn't reach their ends.
Inputs may be any that keep to these rules, and one draw needn't show every extreme that they name: `clip_len`: the lengths sum to 256; the longest clip has exactly 21 frames.
All inputs are finite; a program needn't handle non-finite values.
Results may differ from the reference program's by a relative error of at most 0.003.
Values may be sent and summed in bfloat16 or wider, within the bound.
No kernel may reach another device: no remote copies, remote signals or barrier semaphores. Data moves between devices by JAX's collectives and lax.ppermute only.
A program may use at most 256 MiB of HBM per device.

```python
import math
import jax
import jax.numpy as jnp
import numpy as np
from jax import lax

C = 384
Z = 16
NW = 24
CLIP_MOST = 21
NF = 256
NH = 32
NCLIP = 21


def level_of(own_key, shape, pieces, low, high):
    def one(dim, blocks):
        draws = jax.random.uniform(jax.random.fold_in(jax.random.fold_in(own_key, 6), dim), (blocks,), jnp.float32, low / len(pieces), high / len(pieces))
        return jnp.repeat(jnp.exp(draws), shape[dim] // blocks).reshape((-1,) + (1,) * (len(shape) - dim - 1))

    gain = one(*pieces[0])
    for cut in pieces[1:]:
        gain = gain * one(*cut)
    return gain


def length_profile(number_of, total, reach, skew):
    loads = [(1 << 20) // math.isqrt(standing ** skew) + 1 for standing in range(2, number_of + 1)]
    rest, given = total - reach - (number_of - 1), [1] * (number_of - 1)
    while rest > 0:
        free = [i for i in range(number_of - 1) if given[i] < reach]
        whole, remaining = sum([loads[i] for i in free]), rest
        for i in free:
            extra = min(reach - given[i], max(1, remaining * loads[i] // whole), rest)
            given[i] = given[i] + extra
            rest = rest - extra
    return np.array([reach] + given)


def ragged(own_key, number_of, total, limit, lean):
    if number_of == 2:
        one = jax.random.randint(own_key, (), max(1, total - limit), min(limit, total - 1) + 1)
        return jnp.stack([one, total - one])
    sizes = jnp.asarray(length_profile(number_of, total, limit, lean), jnp.int32)
    twos = (number_of - 1) // 2
    donor, taker = sizes[1:1 + 2 * twos:2], sizes[2:2 + 2 * twos:2]
    margin = jnp.minimum(donor - 1, limit - taker)
    passed = jax.random.randint(jax.random.fold_in(own_key, 1), (twos,), 0, 1 << 20) % (margin + 1)
    sizes = sizes.at[1:1 + 2 * twos:2].set(donor - passed).at[2:2 + 2 * twos:2].set(taker + passed)
    return sizes[jax.random.permutation(jax.random.fold_in(own_key, 2), number_of)]


def noise(stream_key, dims, spread, limit, shards=(), kind=jnp.bfloat16):
    result = spread * jax.random.normal(stream_key, dims, jnp.float32)
    if shards:
        result = result * level_of(stream_key, dims, shards, -0.22, 0.18)
    return jnp.clip(result, -limit, limit).astype(kind)


def setup_inputs(seed: int = 0) -> dict:
    streams_of = jax.random.split(jax.random.key(seed), 5)
    frames = noise(streams_of[0], (NF, NH, NW, C), 1.0, 6.0, ((0, 64), (1, 4)))
    conv_weight = noise(streams_of[1], (27, C, C), (27 * C) ** -0.5, 0.0625)
    head_weight = noise(streams_of[2], (C, 2 * Z), C ** -0.5, 0.3125)
    clip_len = ragged(streams_of[3], NCLIP, NF, CLIP_MOST, 2).astype(jnp.int32)
    return dict(frames=frames, conv_weight=conv_weight, head_weight=head_weight, clip_len=clip_len)


def clip_tables(clip_len, total):
    ends = jnp.cumsum(clip_len).astype(jnp.int32)
    starts = (ends - clip_len).astype(jnp.int32)
    frame_ids = jnp.arange(total, dtype=jnp.int32)
    member = (frame_ids[:, None] >= starts[None, :]) & (frame_ids[:, None] < ends[None, :])
    member_int = member.astype(jnp.int32)
    pos = frame_ids - jnp.sum(member_int * starts[None, :], axis=1).astype(jnp.int32)
    return member.astype(jnp.float32), pos


def reference(frames, conv_weight, head_weight, clip_len):
    nframe, nrow, ncol, chans = frames.shape
    member, pos = clip_tables(clip_len, nframe)
    padded = jnp.pad(frames, ((2, 0), (1, 1), (1, 1), (0, 0)))
    cells = nframe * nrow * ncol

    def tap_input(tap):
        dt, dh, dw = tap // 9, (tap // 3) % 3, tap % 3
        piece = padded[dt:dt + nframe, dh:dh + nrow, dw:dw + ncol, :]
        keep = (pos >= 2 - dt).astype(frames.dtype)
        return (piece * keep[:, None, None, None]).reshape(cells, chans)

    pre = jnp.zeros((cells, chans), jnp.float32)
    for tap in range(27):
        pre = pre + jnp.dot(tap_input(tap), conv_weight[tap], preferred_element_type=jnp.float32)
    act = jax.nn.silu(pre).astype(jnp.bfloat16)
    latent = jnp.dot(act, head_weight, preferred_element_type=jnp.float32)
    zdim = latent.shape[1] // 2
    mean, logvar = latent[:, :zdim], latent[:, zdim:]
    kcell = 0.5 * jnp.sum(mean * mean + jnp.exp(logvar) - 1.0 - logvar, axis=1)
    kframe = jnp.sum(kcell.reshape(nframe, nrow * ncol), axis=1)
    totals = jnp.sum(member * kframe[:, None], axis=0)
    lens = clip_len.astype(jnp.float32)
    per_frame = float(nrow * ncol)
    loss = jnp.sum(lens * jnp.log1p(totals / (lens * per_frame)))
    gclip = lens / (lens * per_frame + totals)
    gframe = jnp.sum(member * gclip[None, :], axis=1)
    gcell = jnp.repeat(gframe, nrow * ncol)[:, None]
    dlat = jnp.concatenate([gcell * mean, gcell * 0.5 * (jnp.exp(logvar) - 1.0)], axis=1).astype(jnp.bfloat16)
    head_grad = lax.dot_general(act, dlat, (((0,), (0,)), ((), ())), preferred_element_type=jnp.float32)
    dact = lax.dot_general(dlat, head_weight, (((1,), (1,)), ((), ())), preferred_element_type=jnp.float32)
    sig = jax.nn.sigmoid(pre)
    dpre = (dact * sig * (1.0 + pre * (1.0 - sig))).astype(jnp.bfloat16)
    grads = []
    for tap in range(27):
        grads.append(lax.dot_general(tap_input(tap), dpre, (((0,), (0,)), ((), ())), preferred_element_type=jnp.float32))
    weight_grad = jnp.stack(grads, axis=0)
    return latent.reshape(nframe, nrow, ncol, 2 * zdim), loss, weight_grad, head_grad
```

```python
import functools

import jax
import jax.numpy as jnp
import numpy as np
from jax import lax
from jax.experimental import pallas as pl
from jax.experimental.pallas import tpu as pltpu
from jax.sharding import PartitionSpec as P

F32 = jnp.float32
B16 = jnp.bfloat16
COLS = 24
LIMIT = 56 * 1024 * 1024
NT = (((1,), (1,)), ((), ()))
TN = (((0,), (0,)), ((), ()))


def dot(a, b, dims=None):
    if dims is None:
        return jnp.dot(a, b, preferred_element_type=F32)
    return lax.dot_general(a, b, dims, preferred_element_type=F32)


def call(kernel, outs, scratch=(), **kw):
    params = pltpu.CompilerParams(vmem_limit_bytes=LIMIT)
    return pl.pallas_call(kernel, out_shape=outs, scratch_shapes=list(scratch), compiler_params=params, **kw)


def smem():
    return pl.BlockSpec(memory_space=pltpu.SMEM)


def vmem():
    return pl.BlockSpec(memory_space=pltpu.VMEM)


def pack_tables(chans, run, ny, nz):
    half = chans // 2
    lane = np.arange(half)
    into = np.zeros((2, 2, chans, chans), np.float32)
    for core in range(2):
        channel = (lane // run) * 2 * run + core * run + lane % run
        for side in range(2):
            into[core, side, channel, side * half + lane] = 1
    block = wide(run) * nz
    place = (lane // run // nz) * block + (lane % run) * nz + lane // run % nz
    back = np.zeros((2, chans, ny * block), np.float32)
    for side in range(2):
        back[side, side * half + lane, place] = 1
    direct = np.zeros((2, chans, ny * block), np.float32)
    for core in range(2):
        direct[core, (lane // run) * 2 * run + core * run + lane % run, place] = 1
    return into, back, direct


def wide(run):
    return -(-run // 8) * 8


def first_kernel(at_ref, x_ref, into_ref, own_ref, oth_ref, tail_ref, past_ref, top_ref, bot_ref, ptop_ref, pbot_ref):
    c = at_ref[0]
    nf, band, chans = x_ref.shape
    for pair in range(nf // 2):
        a, b = x_ref[2 * pair], x_ref[2 * pair + 1]
        own_ref[pair] = (dot(a, into_ref[c, 0]) + dot(b, into_ref[c, 1])).astype(B16)
        oth_ref[pair] = (dot(a, into_ref[1 - c, 0]) + dot(b, into_ref[1 - c, 1])).astype(B16)
    tail_ref[0] = own_ref[nf // 2 - 1]
    past_ref[...] = x_ref[nf - 2 :]
    for f in range(nf):
        wide_frame = x_ref[f].astype(F32)
        top = wide_frame[:COLS].astype(B16)
        bot = wide_frame[band - COLS :].astype(B16)
        top_ref[f] = top
        bot_ref[f] = bot
        if f >= nf - 2:
            ptop_ref[f - nf + 2] = top
            pbot_ref[f - nf + 2] = bot


def merge_kernel(at_ref, own_ref, got_ref, past_ref, sent_ref, into_ref, out_ref):
    c = at_ref[0]

    @pl.when(c == 0)
    def _():
        out_ref[0] = (dot(past_ref[0], into_ref[0, 0]) + dot(past_ref[1], into_ref[0, 1])).astype(B16)
        out_ref[1:3] = own_ref[...]
        out_ref[3:5] = got_ref[...]

    @pl.when(c == 1)
    def _():
        out_ref[0] = sent_ref[0]
        out_ref[1:3] = got_ref[...]
        out_ref[3:5] = own_ref[...]


def unpack_kernel(at_ref, a0, a1, a2, a3, back_ref, out_ref):
    x = at_ref[1]
    pair = pl.program_id(0)
    band = a0.shape[1]
    for d, ref in enumerate((a0, a1, a2, a3)):
        at = pl.multiple_of(lax.rem(x - d + 4, 4) * band, band)
        for side in range(2):
            out_ref[side, pl.ds(at, band), :] = dot(ref[0], back_ref[side]).astype(B16)


def forward_kernel(at_ref, pos_ref, x_ref, past_ref, top_ref, bot_ref, ptop_ref, pbot_ref, w_ref, hw_ref,
                   pre_ref, lat_ref, kf_ref, wide_ref):
    step = pl.program_id(0)
    nf, band, chans = x_ref.shape
    rows = band + 2 * COLS

    @pl.when(step == 0)
    def _():
        col = lax.rem(lax.broadcasted_iota(jnp.int32, (rows, 1), 0), COLS)
        for f in range(nf + 2):
            if f < 2:
                parts = (ptop_ref[f], past_ref[f], pbot_ref[f])
            else:
                parts = (top_ref[f - 2], x_ref[f - 2], bot_ref[f - 2])
            v = jnp.concatenate([p.astype(F32) for p in parts], axis=0)
            for dw in range(3):
                if dw == 0:
                    s = jnp.where(col > 0, pltpu.roll(v, 1, 0), 0.0)
                elif dw == 2:
                    s = jnp.where(col < COLS - 1, pltpu.roll(v, rows - 1, 0), 0.0)
                else:
                    s = v
                for dh in range(3):
                    wide_ref[dh, f * band : (f + 1) * band, dw * chans : (dw + 1) * chans] = s[
                        dh * COLS : dh * COLS + band
                    ].astype(B16)

    dt, dh = step // 3, lax.rem(step, 3)
    part = dot(wide_ref[dh, pl.ds(pl.multiple_of(dt * band, band), nf * band), :], w_ref[0])
    for f in range(nf):
        keep = jnp.where(pos_ref[f] >= 2 - dt, 1.0, 0.0)
        piece = keep * part[f * band : (f + 1) * band]

        @pl.when(step == 0)
        def _():
            pre_ref[f * band : (f + 1) * band] = piece

        @pl.when(step > 0)
        def _():
            pre_ref[f * band : (f + 1) * band] += piece

    @pl.when(step == 8)
    def _():
        zdim = lat_ref.shape[1] // 2
        row = lax.broadcasted_iota(jnp.int32, kf_ref.shape, 0)
        kf = jnp.zeros(kf_ref.shape, F32)
        for f in range(nf):
            pre = pre_ref[f * band : (f + 1) * band]
            act = (pre * (1.0 / (1.0 + jnp.exp(-pre)))).astype(B16)
            lat = dot(act, hw_ref[...])
            lat_ref[f * band : (f + 1) * band] = lat
            lane = lax.broadcasted_iota(jnp.int32, lat.shape, 1)
            term = jnp.where(lane < zdim, lat * lat, jnp.exp(lat) - 1.0 - lat)
            kf = jnp.where(row == at_ref[0] * nf + f, 0.5 * jnp.sum(term), kf)
        kf_ref[...] = kf


def back_kernel(per_frame, at_ref, pre_ref, lat_ref, hw_ref, left_ref, mid_ref, right_ref, same_ref, lens_ref,
                d0, d1, d2, d3, k_ref, g_ref, grad_ref, turned_ref, head_ref):
    c, x = at_ref[0], at_ref[1]
    cells, chans = pre_ref.shape
    nf = g_ref.shape[0] // 2
    band = cells // nf
    per = g_ref.shape[0]
    window = jnp.concatenate(
        [left_ref[0], left_ref[1], left_ref[2], mid_ref[...], right_ref[0], right_ref[1], right_ref[2]], axis=0
    )
    row = lax.broadcasted_iota(jnp.int32, g_ref.shape, 0)
    total = jnp.zeros(g_ref.shape, F32)
    for f in range(per):
        total = jnp.where(row == f, jnp.sum(same_ref[:, f : f + 1] * window, axis=0, keepdims=True), total)
    k_ref[...] = total
    g_ref[...] = lens_ref[...] / (lens_ref[...] * per_frame + total)
    head = jnp.zeros(head_ref.shape, F32)
    for f in range(nf):
        at = slice(f * band, (f + 1) * band)
        lat = lat_ref[at]
        zdim = lat.shape[1] // 2
        g = g_ref[pl.ds(c * nf + f, 1), :][:, : 2 * zdim]
        lane = lax.broadcasted_iota(jnp.int32, lat.shape, 1)
        dlat = (g * jnp.where(lane < zdim, lat, 0.5 * (jnp.exp(lat) - 1.0))).astype(B16)
        dact = dot(dlat, hw_ref[...], NT)
        pre = pre_ref[at]
        sig = 1.0 / (1.0 + jnp.exp(-pre))
        dpre = (dact * sig * (1.0 + pre * (1.0 - sig))).astype(B16)
        act = (pre * sig).astype(B16)
        head = head + dot(dlat, act, TN)
        grad_ref[at] = dpre.astype(F32)
    head_ref[...] = head
    turned_ref[...] = jnp.transpose(grad_ref[...], (1, 0)).astype(B16)
    block = chans // 4
    hblock = head_ref.shape[0] // 4
    for d, ref in enumerate((d0, d1, d2, d3)):
        to = lax.rem(x + d, 4)
        ref[:block] = turned_ref[pl.ds(pl.multiple_of(to * block, block), block), :]
        part = head_ref[pl.ds(pl.multiple_of(to * hblock, hblock), hblock), :]
        high = part.astype(B16).astype(F32)
        both = jnp.concatenate([high, part - high], axis=0)
        if cells > chans:
            both = jnp.concatenate([both, jnp.zeros((2 * hblock, cells - chans), F32)], axis=1)
        ref[block:] = both.astype(B16)


def weight_kernel(ny, at_ref, keep_ref, loss_ref, a0, a1, a2, a3, b0, b1, b2, b3, x_ref, direct_ref,
                  *refs):
    sends, (held_ref, taps_ref, acc_ref, out_ref) = refs[:ny], refs[ny:]
    c, x, y = at_ref[0], at_ref[1], at_ref[2]
    full = x_ref.shape[1]
    band = full // 4
    block = taps_ref.shape[0] // 9
    chans = direct_ref.shape[1]
    lanes = acc_ref.shape[2]
    hsum = jnp.zeros((2 * ((held_ref.shape[2] - block) // 2), chans), F32)
    for core, given in ((c, (a0, a1, a2, a3)), (1 - c, (b0, b1, b2, b3))):
        for d, ref in enumerate(given):
            held_ref[core, lax.rem(x - d + 4, 4)] = ref[...]
            hsum = hsum + ref[block:, :chans].astype(F32)
    hblock = hsum.shape[0] // 2
    acc_ref[...] = jnp.zeros(acc_ref.shape, F32)
    lane = lax.broadcasted_iota(jnp.int32, (1, full), 1)
    col = lax.rem(lane, COLS)
    line = lane // COLS

    def core_frames(core, carry):
        for lf in range(4):
            frame = jnp.zeros((block, full), F32)
            for xs in range(4):
                v = held_ref[core, xs, :block, :].astype(F32)
                shift = ((xs - lf) * band) % full
                if shift:
                    v = pltpu.roll(v, shift, 1)
                frame = jnp.where(lane // band == xs, v, frame)
            for dw in range(3):
                if dw == 0:
                    v = jnp.where(col < COLS - 1, pltpu.roll(frame, full - 1, 1), 0.0)
                elif dw == 2:
                    v = jnp.where(col > 0, pltpu.roll(frame, 1, 1), 0.0)
                else:
                    v = frame
                for dh in range(3):
                    if dh == 0:
                        s = jnp.where(line < full // COLS - 1, pltpu.roll(v, full - COLS, 1), 0.0)
                    elif dh == 2:
                        s = jnp.where(line > 0, pltpu.roll(v, COLS, 1), 0.0)
                    else:
                        s = v
                    q = dh * 3 + dw
                    taps_ref[q * block : (q + 1) * block, :] = s.astype(B16)
            f = core * 4 + lf
            for dt in range(3):
                acc_ref[dt, : 9 * block] += keep_ref[f * 3 + dt] * dot(taps_ref[...], x_ref[f + dt])
        return carry

    lax.fori_loop(0, 2, core_frames, 0)
    direct = direct_ref[c]
    both = hsum[:hblock] + hsum[hblock:]
    high = both.astype(B16)
    low = (both - high.astype(F32)).astype(B16)
    acc_ref[0, 9 * block : 9 * block + hblock] = dot(high, direct) + dot(low, direct)
    loss = jnp.full((8, lanes), loss_ref[0], F32)
    top = loss.astype(B16).astype(F32)
    mid = (loss - top).astype(B16).astype(F32)
    acc_ref[1, 9 * block : 9 * block + 8] = top
    acc_ref[1, 9 * block + 8 : 9 * block + 16] = mid
    acc_ref[1, 9 * block + 16 : 9 * block + 24] = loss - top - mid
    rows = sends[0].shape[1]
    ystep = lanes // ny
    for dt in range(3):
        out_ref[...] = jnp.transpose(acc_ref[dt], (1, 0))
        for d, ref in enumerate(sends):
            to = lax.rem(y + d, ny)
            ref[dt] = out_ref[pl.ds(pl.multiple_of(to * ystep, 8), rows), :].astype(ref.dtype)


def add_kernel(ny, nz, run, at_ref, *refs):
    gets, sends, (sum_ref, part_ref) = refs[:ny], refs[ny : ny + nz], refs[ny + nz :]
    total = gets[0][...]
    for ref in gets[1:]:
        total = total + ref[...].astype(F32)
    chunk = sum_ref.shape[3]
    for i in range(sum_ref.shape[0]):
        sum_ref[i] = total[:, :, i * chunk : (i + 1) * chunk]
    part_ref[...] = jnp.zeros(part_ref.shape, F32)
    step = part_ref.shape[1] // 3
    for z in range(nz):
        for dt in range(3):
            for i in range(sum_ref.shape[0]):
                part_ref[z, dt * step : dt * step + run, i * chunk : (i + 1) * chunk] = sum_ref[
                    i, dt, pl.ds(z, run, stride=nz), :
                ]
    for d, ref in enumerate(sends):
        ref[...] = part_ref[lax.rem(at_ref[3] + d, nz)].astype(ref.dtype)


def last_kernel(*refs):
    total = refs[0][...]
    for ref in refs[1:-1]:
        total = total + ref[...].astype(F32)
    refs[-1][...] = total


def body(frames, conv_weight, head_weight, clip_len):
    nf, nrow, ncol, chans = frames.shape
    band = nrow * ncol
    cells = nf * band
    count = lax.axis_size("tm")
    ny = 4 if count == 64 else 2
    nz = count // 2 // ny
    run = chans // count
    chip = 2 * nf
    t, x = lax.axis_index("tm"), lax.axis_index("space")
    c, k = t % 2, t // 2
    y, z = k // nz, k % nz
    at = jnp.stack([c, x, y, z]).astype(jnp.int32)
    shape = jax.ShapeDtypeStruct

    def index(yy, zz, cc):
        return ((yy % ny) * nz + zz % nz) * 2 + cc

    every = [(yy, zz, cc) for yy in range(ny) for zz in range(nz) for cc in range(2)]

    def over_core(v):
        return lax.ppermute(v, "tm", [(i, i ^ 1) for i in range(count)])

    def over_chip(v, d):
        return lax.ppermute(v, "tm", [(i, (i + 2 * d) % count) for i in range(count)])

    def over_x(v, d):
        return lax.ppermute(v, "space", [(i, (i + d) % 4) for i in range(4)])

    def over_y(v, d):
        return lax.ppermute(v, "tm", [(index(a, b, e), index(a + d, b, e)) for a, b, e in every])

    def over_z(v, d):
        return lax.ppermute(v, "tm", [(index(a, b, e), index(a, b + d, e)) for a, b, e in every])

    nclip = clip_len.shape[0]
    order = jnp.arange(nclip)
    ends = jnp.sum(jnp.where(order[None, :] <= order[:, None], clip_len[None, :], 0), axis=1)
    ids = chip * k + jnp.arange(-3 * chip, 4 * chip)
    clip = jnp.where(ids < 0, -1, jnp.sum(ends[None, :] <= ids[:, None], axis=1))
    mine = clip[3 * chip : 4 * chip]
    same = (clip[:, None] == mine[None, :]).astype(F32)
    member = mine[:, None] == order[None, :]
    lens = jnp.sum(jnp.where(member, clip_len[None, :], 0), axis=1)
    pos = ids[3 * chip : 4 * chip] - jnp.sum(jnp.where(member, (ends - clip_len)[None, :], 0), axis=1)
    lens = lens.astype(F32)
    keep = (pos[:, None] >= jnp.array([2, 1, 0])[None, :]).astype(F32).reshape(-1)
    own_pos = lax.dynamic_slice_in_dim(pos, c * nf, nf).astype(jnp.int32)

    into, back, direct = (jnp.asarray(v, B16) for v in pack_tables(chans, run, ny, nz))
    flat = frames.reshape(nf, band, chans)
    pairs = nf // 2
    own, oth, tail, past, top, bot, ptop, pbot = call(
        first_kernel,
        [shape((pairs, band, chans), B16)] * 2
        + [shape((1, band, chans), B16), shape((2, band, chans), B16)]
        + [shape((nf, ncol, chans), B16)] * 2
        + [shape((2, ncol, chans), B16)] * 2,
        in_specs=[smem(), vmem(), vmem()],
        name="first",
    )(at, flat, into)
    both = ("tm", "space")
    past = lax.ppermute(past, "tm", [(i, i + 1) for i in range(count - 1)])
    top, bot = (
        lax.ppermute(bot, "space", [(i, i + 1) for i in range(3)]),
        lax.ppermute(top, "space", [(i + 1, i) for i in range(3)]),
    )
    ptop, pbot = (
        lax.ppermute(pbot, both, [(4 * i + j, 4 * (i + 1) + j + 1) for i in range(count - 1) for j in range(3)]),
        lax.ppermute(ptop, both, [(4 * i + j + 1, 4 * (i + 1) + j) for i in range(count - 1) for j in range(3)]),
    )
    got = over_core(oth)
    sent = lax.ppermute(tail, "tm", [(i, i + 2) for i in range(1, count - 2, 2)])
    five = call(
        merge_kernel,
        shape((5, band, chans), B16),
        in_specs=[smem()] + [vmem()] * 5,
        name="merge",
    )(at, own, got, past, sent, into)
    fives = [five] + [over_x(five, d) for d in (1, 2, 3)]

    whole = lambda *dims: pl.BlockSpec(dims, lambda i: (0,) * len(dims))
    zlat = head_weight.shape[1]
    pre, latent, kframe = call(
        forward_kernel,
        [shape((cells, chans), F32), shape((cells, zlat), F32), shape((chip, 128), F32)],
        [pltpu.VMEM((3, (nf + 2) * band, 3 * chans), B16)],
        grid=(9,),
        in_specs=[smem(), smem()]
        + [whole(*v.shape) for v in (flat, past, top, bot, ptop, pbot)]
        + [pl.BlockSpec((1, 3 * chans, chans), lambda i: (i, 0, 0)), whole(chans, zlat)],
        out_specs=[whole(cells, chans), whole(cells, zlat), whole(chip, 128)],
        name="forward",
    )(at, own_pos, flat, past, top, bot, ptop, pbot, conv_weight.reshape(9, 3 * chans, chans), head_weight)

    xs = call(
        unpack_kernel,
        shape((10, 4 * band, back.shape[2]), B16),
        grid=(5,),
        in_specs=[smem()] + [pl.BlockSpec((1, band, chans), lambda i: (i, 0, 0))] * 4 + [whole(*back.shape)],
        out_specs=pl.BlockSpec((2, 4 * band, back.shape[2]), lambda i: (i, 0, 0)),
        name="unpack",
    )(at, *fives, back)

    kchip = kframe + over_core(kframe)
    kchip = kchip + over_x(kchip, 1) + over_x(kchip, 2) + over_x(kchip, 3)
    triple = jnp.stack([over_chip(kchip, 1), kchip, over_chip(kchip, -1)])
    left, right = over_chip(triple, 2), over_chip(triple, -2)
    per_frame = float(4 * band)
    hblock = zlat // 4
    block = chans // 4
    message = shape((block + 2 * hblock, cells), B16)
    lens_rows = jnp.broadcast_to(lens[:, None], (chip, 128))
    *mine_d, totals = call(
        functools.partial(back_kernel, per_frame),
        [message] * 4 + [shape((chip, 128), F32)],
        [
            pltpu.VMEM((chip, 128), F32),
            pltpu.VMEM((cells, chans), F32),
            pltpu.VMEM((chans, cells), B16),
            pltpu.VMEM((zlat, chans), F32),
        ],
        in_specs=[smem()] + [vmem()] * 8,
        name="back",
    )(at, pre, latent, head_weight, left, kchip, right, same, lens_rows)
    first = (pos == 0).astype(F32)
    loss_part = jnp.sum(first * lens * jnp.log1p(totals[:, 0] / (lens * per_frame)))
    mine_d = [mine_d[0]] + [over_x(mine_d[d], d) for d in (1, 2, 3)]
    core_d = [over_core(v) for v in mine_d]

    lanes = back.shape[2]
    rows = run * nz
    wrow = 9 * block + 32
    sends = call(
        functools.partial(weight_kernel, ny),
        [shape((3, rows, wrow), F32)] + [shape((3, rows, wrow), B16)] * (ny - 1),
        [
            pltpu.VMEM((2, 4) + message.shape, B16),
            pltpu.VMEM((9 * block, 4 * band), B16),
            pltpu.VMEM((3, wrow, lanes), F32),
            pltpu.VMEM((lanes, wrow), F32),
        ],
        in_specs=[smem()] * 3 + [vmem()] * 10,
        name="weight",
    )(at, keep, loss_part[None], *mine_d, *core_d, xs, direct)
    gets = [sends[0]] + [over_y(sends[d], d) for d in range(1, ny)]
    step = wide(run)
    chunk = 128 if wrow % 128 == 0 else wrow
    parts = call(
        functools.partial(add_kernel, ny, nz, run),
        [shape((3 * step, wrow), F32)] * nz,
        [pltpu.VMEM((wrow // chunk, 3, rows, chunk), F32), pltpu.VMEM((nz, 3 * step, wrow), F32)],
        in_specs=[smem()] + [vmem()] * ny,
        name="add",
    )(at, *gets)
    parts = [parts[0]] + [over_z(parts[d], d) for d in range(1, nz)]
    total = call(last_kernel, shape((3 * step, wrow), F32), name="last")(*parts)
    total = total.reshape(3, step, wrow)
    weight_grad = total[:, :run, : 9 * block].reshape(3, run, 9, block).transpose(0, 2, 1, 3).reshape(27, run, block)
    base = 9 * block
    head_grad = total[0, :run, base : base + hblock]
    loss = total[1, 0, base] + total[1, 0, base + 8] + total[1, 0, base + 16]
    return latent.reshape(nf, nrow, ncol, zlat), loss, weight_grad, head_grad


def solution(mesh):
    in_specs = (P("tm", "space", None, None), P(), P(), P())
    out_specs = (P("tm", "space", None, None), P(), P(None, "tm", "space"), P("tm", "space"))
    return jax.shard_map(body, mesh=mesh, in_specs=in_specs, out_specs=out_specs, check_vma=False)
```

```python
import functools

import jax
import jax.numpy as jnp
import numpy as np
from jax import lax
from jax.experimental import pallas as pl
from jax.experimental.pallas import tpu as pltpu
from jax.sharding import PartitionSpec as P

F32 = jnp.float32
B16 = jnp.bfloat16
COLS = 24
LIMIT = 56 * 1024 * 1024
NT = (((1,), (1,)), ((), ()))
TN = (((0,), (0,)), ((), ()))


def dot(a, b, dims=None):
    if dims is None:
        return jnp.dot(a, b, preferred_element_type=F32)
    return lax.dot_general(a, b, dims, preferred_element_type=F32)


def call(kernel, outs, scratch=(), **kw):
    params = pltpu.CompilerParams(vmem_limit_bytes=LIMIT)
    return pl.pallas_call(kernel, out_shape=outs, scratch_shapes=list(scratch), compiler_params=params, **kw)


def smem():
    return pl.BlockSpec(memory_space=pltpu.SMEM)


def vmem():
    return pl.BlockSpec(memory_space=pltpu.VMEM)


def half_table(chans, run, ny, nz):
    lane = np.arange(chans // 2)
    block = wide(run) * nz
    place = (lane // run // nz) * block + (lane % run) * nz + lane // run % nz
    table = np.zeros((2, chans, ny * block), np.float32)
    for core in range(2):
        table[core, (lane // run) * 2 * run + core * run + lane % run, place] = 1
    return table


def wide(run):
    return -(-run // 8) * 8


def first_kernel(x_ref, past_ref, last_ref, top_ref, bot_ref, ptop_ref, pbot_ref):
    nf, band, chans = x_ref.shape
    past_ref[...] = x_ref[nf - 2 :]
    last_ref[0] = x_ref[nf - 1]
    for f in range(nf):
        wide_frame = x_ref[f].astype(F32)
        top = wide_frame[:COLS].astype(B16)
        bot = wide_frame[band - COLS :].astype(B16)
        top_ref[f] = top
        bot_ref[f] = bot
        if f >= nf - 2:
            ptop_ref[f - nf + 2] = top
            pbot_ref[f - nf + 2] = bot


def choose_kernel(at_ref, frames_ref, p0, p1, p2, p3, table_ref, own_ref, oth_ref):
    c = at_ref[0]
    band = frames_ref.shape[2]

    @pl.when(pl.program_id(0) == 0)
    def _():
        for d, ref in enumerate((p0, p1, p2, p3)):
            at = pl.ds(pl.multiple_of(lax.rem(at_ref[1] - d + 4, 4) * band, band), band)
            own_ref[0, at] = dot(ref[0], table_ref[c]).astype(B16)
            oth_ref[0, at] = dot(ref[0], table_ref[1 - c]).astype(B16)

    @pl.when(pl.program_id(0) > 0)
    def _():
        for xs in range(4):
            at = slice(xs * band, (xs + 1) * band)
            own_ref[0, at] = dot(frames_ref[xs, 0], table_ref[c]).astype(B16)
            oth_ref[0, at] = dot(frames_ref[xs, 0], table_ref[1 - c]).astype(B16)


def forward_kernel(at_ref, pos_ref, x_ref, past_ref, top_ref, bot_ref, ptop_ref, pbot_ref, w_ref, hw_ref,
                   lat_ref, kf_ref, d0, d1, d2, d3, pre_ref, wide_ref, turned_ref, head_ref):
    step = pl.program_id(0)
    nf, band, chans = x_ref.shape
    rows = band + 2 * COLS

    @pl.when(step == 0)
    def _():
        col = lax.rem(lax.broadcasted_iota(jnp.int32, (rows, 1), 0), COLS)
        for f in range(nf + 2):
            if f < 2:
                parts = (ptop_ref[f], past_ref[f], pbot_ref[f])
            else:
                parts = (top_ref[f - 2], x_ref[f - 2], bot_ref[f - 2])
            v = jnp.concatenate([p.astype(F32) for p in parts], axis=0)
            for dw in range(3):
                if dw == 0:
                    s = jnp.where(col > 0, pltpu.roll(v, 1, 0), 0.0)
                elif dw == 2:
                    s = jnp.where(col < COLS - 1, pltpu.roll(v, rows - 1, 0), 0.0)
                else:
                    s = v
                for dh in range(3):
                    wide_ref[dh, f * band : (f + 1) * band, dw * chans : (dw + 1) * chans] = s[
                        dh * COLS : dh * COLS + band
                    ].astype(B16)

    dt, dh = step // 3, lax.rem(step, 3)
    part = dot(wide_ref[dh, pl.ds(pl.multiple_of(dt * band, band), nf * band), :], w_ref[0])
    for f in range(nf):
        keep = jnp.where(pos_ref[f] >= 2 - dt, 1.0, 0.0)
        piece = keep * part[f * band : (f + 1) * band]

        @pl.when(step == 0)
        def _():
            pre_ref[f * band : (f + 1) * band] = piece

        @pl.when(step > 0)
        def _():
            pre_ref[f * band : (f + 1) * band] += piece

    @pl.when(step == 8)
    def _():
        zdim = lat_ref.shape[1] // 2
        row = lax.broadcasted_iota(jnp.int32, kf_ref.shape, 0)
        kf = jnp.zeros(kf_ref.shape, F32)
        for f in range(nf):
            at = slice(f * band, (f + 1) * band)
            pre = pre_ref[at]
            sig = 1.0 / (1.0 + jnp.exp(-pre))
            act = (pre * sig).astype(B16)
            lat = dot(act, hw_ref[...])
            lat_ref[at] = lat
            lane = lax.broadcasted_iota(jnp.int32, lat.shape, 1)
            grow = jnp.exp(lat) - 1.0
            term = jnp.where(lane < zdim, lat * lat, grow - lat)
            kf = jnp.where(row == at_ref[0] * nf + f, 0.5 * jnp.sum(term), kf)
            dlat = jnp.where(lane < zdim, lat, 0.5 * grow).astype(B16)
            dact = dot(dlat, hw_ref[...], NT)
            pre_ref[at] = (dact * sig * (1.0 + pre * (1.0 - sig))).astype(B16).astype(F32)
            head_ref[f] = dot(dlat, act, TN)
        kf_ref[...] = kf
        turned_ref[...] = jnp.transpose(pre_ref[...], (1, 0)).astype(B16)
        block = chans // 4
        hblock = 2 * zdim // 4
        for d, ref in enumerate((d0, d1, d2, d3)):
            to = lax.rem(at_ref[1] + d, 4)
            ref[:block] = turned_ref[pl.ds(pl.multiple_of(to * block, block), block), :]
            heads = [head_ref[f, pl.ds(pl.multiple_of(to * hblock, hblock), hblock), :] for f in range(nf)]
            pad = ref.shape[1] - 2 * chans
            if pad:
                heads = [jnp.concatenate([h, jnp.zeros((hblock, pad // 2), F32)], axis=1) for h in heads]
            both = jnp.concatenate(
                [jnp.concatenate(heads[:2], axis=1), jnp.concatenate(heads[2:], axis=1)], axis=0
            )
            ref[block:] = both.astype(B16)


def weight_kernel(ny, at_ref, keep_ref, g_ref, loss_ref, a0, a1, a2, a3, b0, b1, b2, b3, x_ref, xo_ref, direct_ref,
                  *refs):
    sends, (held_ref, taps_ref, acc_ref, out_ref, xs_ref, sem) = refs[:ny], refs[ny:]
    c, x, y = at_ref[0], at_ref[1], at_ref[2]
    copies = []
    for core, ref, s in ((c, x_ref, 0), (1 - c, xo_ref, 1)):
        copies.append(pltpu.make_async_copy(ref.at[0:1], xs_ref.at[pl.ds(core, 1)], sem.at[s, 0]))
        copies.append(pltpu.make_async_copy(ref.at[1:5], xs_ref.at[pl.ds(2 + 4 * core, 4)], sem.at[s, 1]))
    for copy in copies:
        copy.start()
    full = x_ref.shape[1]
    band = full // 4
    block = taps_ref.shape[0] // 9
    chans = direct_ref.shape[1]
    lanes = acc_ref.shape[2]
    hblock = (held_ref.shape[2] - block) // 2
    half = full // 2
    hsum = jnp.zeros((hblock, chans), F32)
    for core, given in ((c, (a0, a1, a2, a3)), (1 - c, (b0, b1, b2, b3))):
        for d, ref in enumerate(given):
            held_ref[core, lax.rem(x - d + 4, 4)] = ref[...]
            tail = ref[block:, :].astype(F32)
            for f in range(4):
                part = tail[(f // 2) * hblock : (f // 2 + 1) * hblock, (f % 2) * half : (f % 2) * half + chans]
                hsum = hsum + g_ref[core * 4 + f] * part
    acc_ref[...] = jnp.zeros(acc_ref.shape, F32)
    lane = lax.broadcasted_iota(jnp.int32, (1, full), 1)
    col = lax.rem(lane, COLS)
    line = lane // COLS

    for copy in copies:
        copy.wait()

    def core_frames(core, carry):
        for lf in range(4):
            frame = jnp.zeros((block, full), F32)
            for xs in range(4):
                v = held_ref[core, xs, :block, :].astype(F32)
                shift = ((xs - lf) * band) % full
                if shift:
                    v = pltpu.roll(v, shift, 1)
                frame = jnp.where(lane // band == xs, v, frame)
            for dw in range(3):
                if dw == 0:
                    v = jnp.where(col < COLS - 1, pltpu.roll(frame, full - 1, 1), 0.0)
                elif dw == 2:
                    v = jnp.where(col > 0, pltpu.roll(frame, 1, 1), 0.0)
                else:
                    v = frame
                for dh in range(3):
                    if dh == 0:
                        s = jnp.where(line < full // COLS - 1, pltpu.roll(v, full - COLS, 1), 0.0)
                    elif dh == 2:
                        s = jnp.where(line > 0, pltpu.roll(v, COLS, 1), 0.0)
                    else:
                        s = v
                    q = dh * 3 + dw
                    taps_ref[q * block : (q + 1) * block, :] = s.astype(B16)
            f = core * 4 + lf
            for dt in range(3):
                acc_ref[dt, : 9 * block] += keep_ref[f * 3 + dt] * dot(taps_ref[...], xs_ref[f + dt])
        return carry

    lax.fori_loop(0, 2, core_frames, 0)
    direct = direct_ref[c]
    high = hsum.astype(B16)
    low = (hsum - high.astype(F32)).astype(B16)
    acc_ref[0, 9 * block : 9 * block + hblock] = dot(high, direct) + dot(low, direct)
    loss = jnp.full((8, lanes), loss_ref[0], F32)
    top = loss.astype(B16).astype(F32)
    mid = (loss - top).astype(B16).astype(F32)
    acc_ref[1, 9 * block : 9 * block + 8] = top
    acc_ref[1, 9 * block + 8 : 9 * block + 16] = mid
    acc_ref[1, 9 * block + 16 : 9 * block + 24] = loss - top - mid
    rows = sends[0].shape[1]
    ystep = lanes // ny
    for dt in range(3):
        out_ref[...] = jnp.transpose(acc_ref[dt], (1, 0))
        for d, ref in enumerate(sends):
            to = lax.rem(y + d, ny)
            ref[dt] = out_ref[pl.ds(pl.multiple_of(to * ystep, 8), rows), :].astype(ref.dtype)


def add_kernel(ny, nz, run, at_ref, *refs):
    gets, sends, (sum_ref, part_ref) = refs[:ny], refs[ny : ny + nz], refs[ny + nz :]
    total = gets[0][...]
    for ref in gets[1:]:
        total = total + ref[...].astype(F32)
    chunk = sum_ref.shape[3]
    for i in range(sum_ref.shape[0]):
        sum_ref[i] = total[:, :, i * chunk : (i + 1) * chunk]
    part_ref[...] = jnp.zeros(part_ref.shape, F32)
    step = part_ref.shape[1] // 3
    for z in range(nz):
        for dt in range(3):
            for i in range(sum_ref.shape[0]):
                part_ref[z, dt * step : dt * step + run, i * chunk : (i + 1) * chunk] = sum_ref[
                    i, dt, pl.ds(z, run, stride=nz), :
                ]
    for d, ref in enumerate(sends):
        ref[...] = part_ref[lax.rem(at_ref[3] + d, nz)].astype(ref.dtype)


def last_kernel(count, *refs):
    parts, (weight_ref, head_ref, loss_ref) = refs[:count], refs[count:]
    total = parts[0][...]
    for ref in parts[1:]:
        total = total + ref[...].astype(F32)
    run, block = weight_ref.shape[1:]
    step = total.shape[0] // 3
    for dt in range(3):
        for q in range(9):
            weight_ref[dt * 9 + q] = total[dt * step : dt * step + run, q * block : (q + 1) * block]
    base = 9 * block
    head_ref[...] = total[:run, base : base + head_ref.shape[1]]
    loss = total[step : step + 1, base : base + 1]
    loss = loss + total[step : step + 1, base + 8 : base + 9]
    loss_ref[...] = loss + total[step : step + 1, base + 16 : base + 17]


def body(frames, conv_weight, head_weight, clip_len):
    nf, nrow, ncol, chans = frames.shape
    band = nrow * ncol
    cells = nf * band
    count = lax.axis_size("tm")
    ny = 4 if count == 64 else 2
    nz = count // 2 // ny
    run = chans // count
    chip = 2 * nf
    t, x = lax.axis_index("tm"), lax.axis_index("space")
    c, k = t % 2, t // 2
    y, z = k // nz, k % nz
    at = jnp.stack([c, x, y, z]).astype(jnp.int32)
    shape = jax.ShapeDtypeStruct

    def index(yy, zz, cc):
        return ((yy % ny) * nz + zz % nz) * 2 + cc

    every = [(yy, zz, cc) for yy in range(ny) for zz in range(nz) for cc in range(2)]

    def over_core(v):
        return lax.ppermute(v, "tm", [(i, i ^ 1) for i in range(count)])

    def over_chip(v, d):
        return lax.ppermute(v, "tm", [(i, (i + 2 * d) % count) for i in range(count)])

    def over_x(v, d):
        return lax.ppermute(v, "space", [(i, (i + d) % 4) for i in range(4)])

    def over_y(v, d):
        return lax.ppermute(v, "tm", [(index(a, b, e), index(a + d, b, e)) for a, b, e in every])

    def over_z(v, d):
        return lax.ppermute(v, "tm", [(index(a, b, e), index(a, b + d, e)) for a, b, e in every])

    nclip = clip_len.shape[0]
    order = jnp.arange(nclip)
    ends = jnp.sum(jnp.where(order[None, :] <= order[:, None], clip_len[None, :], 0), axis=1)
    ids = chip * k + jnp.arange(-3 * chip, 4 * chip)
    clip = jnp.where(ids < 0, -1, jnp.sum(ends[None, :] <= ids[:, None], axis=1))
    mine = clip[3 * chip : 4 * chip]
    same = (clip[:, None] == mine[None, :]).astype(F32)
    member = mine[:, None] == order[None, :]
    lens = jnp.sum(jnp.where(member, clip_len[None, :], 0), axis=1)
    pos = ids[3 * chip : 4 * chip] - jnp.sum(jnp.where(member, (ends - clip_len)[None, :], 0), axis=1)
    lens = lens.astype(F32)
    keep = (pos[:, None] >= jnp.array([2, 1, 0])[None, :]).astype(F32).reshape(-1)
    own_pos = lax.dynamic_slice_in_dim(pos, c * nf, nf).astype(jnp.int32)

    table = jnp.asarray(half_table(chans, run, ny, nz), B16)
    flat = frames.reshape(nf, band, chans)
    gathered = lax.all_gather(flat, "space", axis=0)
    past, last, top, bot, ptop, pbot = call(
        first_kernel,
        [shape((2, band, chans), B16), shape((1, band, chans), B16)]
        + [shape((nf, ncol, chans), B16)] * 2
        + [shape((2, ncol, chans), B16)] * 2,
        name="first",
    )(flat)
    both = ("tm", "space")
    top, bot = (
        lax.ppermute(bot, "space", [(i, i + 1) for i in range(3)]),
        lax.ppermute(top, "space", [(i + 1, i) for i in range(3)]),
    )
    past = lax.ppermute(past, "tm", [(i, i + 1) for i in range(count - 1)])
    ptop, pbot = (
        lax.ppermute(pbot, both, [(4 * i + j, 4 * (i + 1) + j + 1) for i in range(count - 1) for j in range(3)]),
        lax.ppermute(ptop, both, [(4 * i + j + 1, 4 * (i + 1) + j) for i in range(count - 1) for j in range(3)]),
    )
    last = lax.ppermute(last, "tm", [(i, i + 2) for i in range(1, count - 2, 2)])
    before = jnp.where(c == 0, past[:1], last)
    before, flat = lax.optimization_barrier((before, flat))
    befores = [before] + [over_x(before, d) for d in (1, 2, 3)]

    whole = lambda *dims: pl.BlockSpec(dims, lambda i: (0,) * len(dims))
    zlat = head_weight.shape[1]
    hblock = zlat // 4
    block = chans // 4
    message = shape((block + 2 * hblock, cells), B16)
    latent, kframe, *mine_d = call(
        forward_kernel,
        [shape((cells, zlat), F32), shape((chip, 128), F32)] + [message] * 4,
        [
            pltpu.VMEM((cells, chans), F32),
            pltpu.VMEM((3, (nf + 2) * band, 3 * chans), B16),
            pltpu.VMEM((chans, cells), B16),
            pltpu.VMEM((nf, zlat, chans), F32),
        ],
        grid=(9,),
        in_specs=[smem(), smem()]
        + [whole(*v.shape) for v in (flat, past, top, bot, ptop, pbot)]
        + [pl.BlockSpec((1, 3 * chans, chans), lambda i: (i, 0, 0)), whole(chans, zlat)],
        out_specs=[whole(cells, zlat), whole(chip, 128)] + [whole(*message.shape)] * 4,
        name="forward",
    )(at, own_pos, flat, past, top, bot, ptop, pbot, conv_weight.reshape(9, 3 * chans, chans), head_weight)
    mine_d = [mine_d[0]] + [over_x(mine_d[d], d) for d in (1, 2, 3)]

    kchip = kframe + over_core(kframe)
    gathered, befores, kchip = lax.optimization_barrier((gathered, befores, kchip))
    kchip, mine_d = lax.optimization_barrier((kchip, mine_d))
    kchip = kchip + over_x(kchip, 1) + over_x(kchip, 2) + over_x(kchip, 3)
    core_d = [over_core(v) for v in mine_d]
    triple = jnp.stack([over_chip(kchip, 1), kchip, over_chip(kchip, -1)])
    left, right = over_chip(triple, 2), over_chip(triple, -2)
    window = jnp.concatenate([left, kchip[None], right])[:, :, 0].reshape(-1)
    per_frame = float(4 * band)
    totals = jnp.sum(same * window[:, None], axis=0)
    gain = lens / (lens * per_frame + totals)
    first = (pos == 0).astype(F32)
    loss_part = jnp.sum(first * lens * jnp.log1p(totals / (lens * per_frame)))
    scale = (keep.reshape(chip, 3) * gain[:, None]).reshape(-1)

    lanes = table.shape[2]
    chosen = shape((5, 4 * band, lanes), B16)
    spec = pl.BlockSpec((1, 4 * band, lanes), lambda i: (i, 0, 0))
    xown, xoth = call(
        choose_kernel,
        [chosen, chosen],
        grid=(5,),
        in_specs=[
            smem(),
            pl.BlockSpec((4, 1, band, chans), lambda i: (0, jnp.maximum(i - 1, 0), 0, 0)),
        ]
        + [whole(1, band, chans)] * 4
        + [
            whole(*table.shape),
        ],
        out_specs=[spec, spec],
        name="choose",
    )(at, gathered, *befores, table)
    xoth = over_core(xoth)

    rows = run * nz
    wrow = 9 * block + 32
    sends = call(
        functools.partial(weight_kernel, ny),
        [shape((3, rows, wrow), F32)] + [shape((3, rows, wrow), B16)] * (ny - 1),
        [
            pltpu.VMEM((2, 4) + message.shape, B16),
            pltpu.VMEM((9 * block, 4 * band), B16),
            pltpu.VMEM((3, wrow, lanes), F32),
            pltpu.VMEM((lanes, wrow), F32),
            pltpu.VMEM((10, 4 * band, lanes), B16),
            pltpu.SemaphoreType.DMA((2, 2)),
        ],
        in_specs=[smem()] * 4 + [vmem()] * 8 + [pl.BlockSpec(memory_space=pl.ANY)] * 2 + [vmem()],
        name="weight",
    )(at, scale, gain, loss_part[None], *mine_d, *core_d, xown, xoth, table)
    gets = [sends[0]] + [over_y(sends[d], d) for d in range(1, ny)]
    step = wide(run)
    chunk = 128 if wrow % 128 == 0 else wrow
    parts = call(
        functools.partial(add_kernel, ny, nz, run),
        [shape((3 * step, wrow), F32)] + [shape((3 * step, wrow), B16)] * (nz - 1),
        [pltpu.VMEM((wrow // chunk, 3, rows, chunk), F32), pltpu.VMEM((nz, 3 * step, wrow), F32)],
        in_specs=[smem()] + [vmem()] * ny,
        name="add",
    )(at, *gets)
    parts = [parts[0]] + [over_z(parts[d], d) for d in range(1, nz)]
    weight_grad, head_grad, loss = call(
        functools.partial(last_kernel, nz),
        [shape((27, run, block), F32), shape((run, hblock), F32), shape((1, 1), F32)],
        name="last",
    )(*parts)
    return latent.reshape(nf, nrow, ncol, zlat), loss[0, 0], weight_grad, head_grad


def solution(mesh):
    in_specs = (P("tm", "space", None, None), P(), P(), P())
    out_specs = (P("tm", "space", None, None), P(), P(None, "tm", "space"), P("tm", "space"))
    return jax.shard_map(body, mesh=mesh, in_specs=in_specs, out_specs=out_specs, check_vma=False)
```

```python
import functools

import jax
import jax.numpy as jnp
import numpy as np
from jax import lax
from jax.experimental import pallas as pl
from jax.experimental.pallas import tpu as pltpu
from jax.sharding import PartitionSpec as P

F32 = jnp.float32
B16 = jnp.bfloat16
COLS = 24
LIMIT = 56 * 1024 * 1024
NT = (((1,), (1,)), ((), ()))
TN = (((0,), (0,)), ((), ()))


def dot(a, b, dims=None):
    if dims is None:
        return jnp.dot(a, b, preferred_element_type=F32)
    return lax.dot_general(a, b, dims, preferred_element_type=F32)


def call(kernel, outs, scratch=(), **kw):
    params = pltpu.CompilerParams(vmem_limit_bytes=LIMIT)
    return pl.pallas_call(kernel, out_shape=outs, scratch_shapes=list(scratch), compiler_params=params, **kw)


def smem():
    return pl.BlockSpec(memory_space=pltpu.SMEM)


def vmem():
    return pl.BlockSpec(memory_space=pltpu.VMEM)


def half_table(chans, run, ny, nz):
    lane = np.arange(chans // 2)
    block = wide(run) * nz
    place = (lane // run // nz) * block + (lane % run) * nz + lane // run % nz
    table = np.zeros((2, chans, ny * block), np.float32)
    for core in range(2):
        table[core, (lane // run) * 2 * run + core * run + lane % run, place] = 1
    return table


def wide(run):
    return -(-run // 8) * 8


def first_kernel(x_ref, past_ref, last_ref, top_ref, bot_ref, ptop_ref, pbot_ref):
    nf, band, chans = x_ref.shape
    past_ref[...] = x_ref[nf - 2 :]
    last_ref[0] = x_ref[nf - 1]
    for f in range(nf):
        wide_frame = x_ref[f].astype(F32)
        top = wide_frame[:COLS].astype(B16)
        bot = wide_frame[band - COLS :].astype(B16)
        top_ref[f] = top
        bot_ref[f] = bot
        if f >= nf - 2:
            ptop_ref[f - nf + 2] = top
            pbot_ref[f - nf + 2] = bot


def choose_kernel(at_ref, frames_ref, p0, p1, p2, p3, table_ref, own_ref, oth_ref, past_ref):
    c = at_ref[0]
    band = frames_ref.shape[2]

    def put(v):
        own_ref[0] = dot(v, table_ref[c]).astype(B16)
        oth_ref[0] = dot(v, table_ref[1 - c]).astype(B16)

    @pl.when(pl.program_id(0) == 0)
    def _():
        for d, ref in enumerate((p0, p1, p2, p3)):
            at = pl.ds(pl.multiple_of(lax.rem(at_ref[1] - d + 4, 4) * band, band), band)
            past_ref[at] = ref[0]
        put(past_ref[...])

    @pl.when(pl.program_id(0) > 0)
    def _():
        put(jnp.concatenate([frames_ref[xs, 0] for xs in range(4)], axis=0))


def forward_kernel(at_ref, pos_ref, x_ref, past_ref, top_ref, bot_ref, ptop_ref, pbot_ref, w_ref, hw_ref,
                   lat_ref, kf_ref, d0, d1, d2, d3, pre_ref, wide_ref, turned_ref, head_ref):
    step = pl.program_id(0)
    nf, band, chans = x_ref.shape
    rows = band + 2 * COLS

    @pl.when(step == 0)
    def _():
        col = lax.rem(lax.broadcasted_iota(jnp.int32, (rows, 1), 0), COLS)
        for f in range(nf + 2):
            if f < 2:
                parts = (ptop_ref[f], past_ref[f], pbot_ref[f])
            else:
                parts = (top_ref[f - 2], x_ref[f - 2], bot_ref[f - 2])
            v = jnp.concatenate([p.astype(F32) for p in parts], axis=0)
            for dw in range(3):
                if dw == 0:
                    s = jnp.where(col > 0, pltpu.roll(v, 1, 0), 0.0)
                elif dw == 2:
                    s = jnp.where(col < COLS - 1, pltpu.roll(v, rows - 1, 0), 0.0)
                else:
                    s = v
                for dh in range(3):
                    q = dh * 3 + dw
                    wide_ref[f * band : (f + 1) * band, q * chans : (q + 1) * chans] = s[
                        dh * COLS : dh * COLS + band
                    ].astype(B16)

    dt = step
    part = dot(wide_ref[pl.ds(pl.multiple_of(dt * band, band), nf * band), :], w_ref[0])
    for f in range(nf):
        keep = jnp.where(pos_ref[f] >= 2 - dt, 1.0, 0.0)
        piece = keep * part[f * band : (f + 1) * band]

        @pl.when(step == 0)
        def _():
            pre_ref[f * band : (f + 1) * band] = piece

        @pl.when(step > 0)
        def _():
            pre_ref[f * band : (f + 1) * band] += piece

    @pl.when(step == 2)
    def _():
        zdim = lat_ref.shape[1] // 2
        row = lax.broadcasted_iota(jnp.int32, kf_ref.shape, 0)
        kf = jnp.zeros(kf_ref.shape, F32)
        for f in range(nf):
            at = slice(f * band, (f + 1) * band)
            pre = pre_ref[at]
            sig = 1.0 / (1.0 + jnp.exp(-pre))
            act = (pre * sig).astype(B16)
            lat = dot(act, hw_ref[...], NT)
            lat_ref[at] = lat
            lane = lax.broadcasted_iota(jnp.int32, lat.shape, 1)
            grow = jnp.exp(lat) - 1.0
            term = jnp.where(lane < zdim, lat * lat, grow - lat)
            kf = jnp.where(row == at_ref[0] * nf + f, 0.5 * jnp.sum(term), kf)
            dlat = jnp.where(lane < zdim, lat, 0.5 * grow).astype(B16)
            dact = dot(dlat, hw_ref[...])
            pre_ref[at] = (dact * sig * (1.0 + pre * (1.0 - sig))).astype(B16).astype(F32)
            head_ref[f] = dot(dlat, act, TN)
        kf_ref[...] = kf
        turned_ref[...] = jnp.transpose(pre_ref[...], (1, 0)).astype(B16)
        block = chans // 4
        hblock = 2 * zdim // 4
        for d, ref in enumerate((d0, d1, d2, d3)):
            to = lax.rem(at_ref[1] + d, 4)
            ref[:block] = turned_ref[pl.ds(pl.multiple_of(to * block, block), block), :]
            heads = [head_ref[f, pl.ds(pl.multiple_of(to * hblock, hblock), hblock), :] for f in range(nf)]
            pad = ref.shape[1] - 2 * chans
            if pad:
                heads = [jnp.concatenate([h, jnp.zeros((hblock, pad // 2), F32)], axis=1) for h in heads]
            both = jnp.concatenate(
                [jnp.concatenate(heads[:2], axis=1), jnp.concatenate(heads[2:], axis=1)], axis=0
            )
            ref[block:] = both.astype(B16)


def weight_kernel(ny, per_frame, at_ref, keep_ref, left_ref, mid_ref, right_ref, same_ref, lens_ref, first_ref,
                  a0, a1, a2, a3, b0, b1, b2, b3, x_ref, xo_ref, direct_ref,
                  *refs):
    sends, (held_ref, taps_ref, acc_ref, out_ref, xs_ref, g_ref, sem) = refs[:ny], refs[ny:]
    c, x, y = at_ref[0], at_ref[1], at_ref[2]
    copies = []
    for core, ref, s in ((c, x_ref, 0), (1 - c, xo_ref, 1)):
        copies.append(pltpu.make_async_copy(ref.at[0:1], xs_ref.at[pl.ds(core, 1)], sem.at[s, 0]))
        copies.append(pltpu.make_async_copy(ref.at[1:5], xs_ref.at[pl.ds(2 + 4 * core, 4)], sem.at[s, 1]))
    for copy in copies:
        copy.start()
    full = x_ref.shape[1]
    band = full // 4
    block = taps_ref.shape[1] // 9
    chans = direct_ref.shape[1]
    lanes = acc_ref.shape[2]
    hblock = (held_ref.shape[2] - block) // 2
    half = full // 2
    window = jnp.concatenate(
        [left_ref[0], left_ref[1], left_ref[2], mid_ref[...], right_ref[0], right_ref[1], right_ref[2]], axis=0
    )
    row = lax.broadcasted_iota(jnp.int32, g_ref.shape, 0)
    total = jnp.zeros(g_ref.shape, F32)
    for f in range(g_ref.shape[0]):
        total = jnp.where(row == f, jnp.sum(same_ref[:, f : f + 1] * window, axis=0, keepdims=True), total)
    lens = lens_ref[...]
    g_ref[...] = lens / (lens * per_frame + total)
    loss = jnp.sum(first_ref[...] * lens * jnp.log1p(total / (lens * per_frame)), axis=0, keepdims=True)
    hsum = jnp.zeros((hblock, chans), F32)
    for core, given in ((c, (a0, a1, a2, a3)), (1 - c, (b0, b1, b2, b3))):
        for d, ref in enumerate(given):
            held_ref[core, lax.rem(x - d + 4, 4)] = ref[...]
            tail = ref[block:, :].astype(F32)
            for f in range(4):
                part = tail[(f // 2) * hblock : (f // 2 + 1) * hblock, (f % 2) * half : (f % 2) * half + chans]
                hsum = hsum + g_ref[pl.ds(core * 4 + f, 1), :][:, :1] * part
    acc_ref[...] = jnp.zeros(acc_ref.shape, F32)
    lane = lax.broadcasted_iota(jnp.int32, (1, full), 1)
    col = lax.rem(lane, COLS)
    line = lane // COLS

    def build(f):
        core, lf = f // 4, f % 4
        frame = jnp.zeros((block, full), F32)
        for xs in range(4):
            v = held_ref[core, xs, :block, :].astype(F32)
            shift = ((xs - lf) * band) % full
            if shift:
                v = pltpu.roll(v, shift, 1)
            frame = jnp.where(lane // band == xs, v, frame)
        for dw in range(3):
            if dw == 0:
                v = jnp.where(col < COLS - 1, pltpu.roll(frame, full - 1, 1), 0.0)
            elif dw == 2:
                v = jnp.where(col > 0, pltpu.roll(frame, 1, 1), 0.0)
            else:
                v = frame
            for dh in range(3):
                if dh == 0:
                    s = jnp.where(line < full // COLS - 1, pltpu.roll(v, full - COLS, 1), 0.0)
                elif dh == 2:
                    s = jnp.where(line > 0, pltpu.roll(v, COLS, 1), 0.0)
                else:
                    s = v
                q = dh * 3 + dw
                taps_ref[f % 2, q * block : (q + 1) * block, :] = s.astype(B16)

    build(0)
    for copy in copies:
        copy.wait()
    for f in range(8):
        if f < 7:
            build(f + 1)
        for dt in range(3):
            scale = keep_ref[f * 3 + dt] * g_ref[f : f + 1, :1]
            acc_ref[dt, : 9 * block] += scale * dot(taps_ref[f % 2], xs_ref[f + dt])
    direct = direct_ref[c]
    high = hsum.astype(B16)
    low = (hsum - high.astype(F32)).astype(B16)
    acc_ref[0, 9 * block : 9 * block + hblock] = dot(high, direct) + dot(low, direct)
    loss = jnp.broadcast_to(loss[:, :1], (8, lanes))
    top = loss.astype(B16).astype(F32)
    mid = (loss - top).astype(B16).astype(F32)
    acc_ref[1, 9 * block : 9 * block + 8] = top
    acc_ref[1, 9 * block + 8 : 9 * block + 16] = mid
    acc_ref[1, 9 * block + 16 : 9 * block + 24] = loss - top - mid
    rows = sends[0].shape[1]
    ystep = lanes // ny
    for dt in range(3):
        out_ref[...] = jnp.transpose(acc_ref[dt], (1, 0))
        for d, ref in enumerate(sends):
            to = lax.rem(y + d, ny)
            ref[dt] = out_ref[pl.ds(pl.multiple_of(to * ystep, 8), rows), :].astype(ref.dtype)


def add_kernel(ny, nz, run, at_ref, *refs):
    gets, sends, (sum_ref, part_ref) = refs[:ny], refs[ny : ny + nz], refs[ny + nz :]
    total = gets[0][...]
    for ref in gets[1:]:
        total = total + ref[...].astype(F32)
    chunk = sum_ref.shape[3]
    for i in range(sum_ref.shape[0]):
        sum_ref[i] = total[:, :, i * chunk : (i + 1) * chunk]
    part_ref[...] = jnp.zeros(part_ref.shape, F32)
    step = part_ref.shape[1] // 3
    for z in range(nz):
        for dt in range(3):
            for i in range(sum_ref.shape[0]):
                part_ref[z, dt * step : dt * step + run, i * chunk : (i + 1) * chunk] = sum_ref[
                    i, dt, pl.ds(z, run, stride=nz), :
                ]
    for d, ref in enumerate(sends):
        ref[...] = part_ref[lax.rem(at_ref[3] + d, nz)].astype(ref.dtype)


def last_kernel(count, *refs):
    parts, (weight_ref, head_ref, loss_ref) = refs[:count], refs[count:]
    total = parts[0][...]
    for ref in parts[1:]:
        total = total + ref[...].astype(F32)
    run, _, block = weight_ref.shape
    step = total.shape[0] // 3
    for dt in range(3):
        for q in range(9):
            weight_ref[:, dt * 9 + q, :] = total[dt * step : dt * step + run, q * block : (q + 1) * block]
    base = 9 * block
    head_ref[...] = total[:run, base : base + head_ref.shape[1]]
    loss = total[step : step + 1, base : base + 1]
    loss = loss + total[step : step + 1, base + 8 : base + 9]
    loss_ref[...] = loss + total[step : step + 1, base + 16 : base + 17]


def body(frames, conv_weight, head_weight, clip_len):
    nf, nrow, ncol, chans = frames.shape
    band = nrow * ncol
    cells = nf * band
    count = lax.axis_size("tm")
    ny = 4 if count == 64 else 2
    nz = count // 2 // ny
    run = chans // count
    chip = 2 * nf
    t, x = lax.axis_index("tm"), lax.axis_index("space")
    c, k = t % 2, t // 2
    y, z = k // nz, k % nz
    at = jnp.stack([c, x, y, z]).astype(jnp.int32)
    shape = jax.ShapeDtypeStruct

    def index(yy, zz, cc):
        return ((yy % ny) * nz + zz % nz) * 2 + cc

    every = [(yy, zz, cc) for yy in range(ny) for zz in range(nz) for cc in range(2)]

    def over_core(v):
        return lax.ppermute(v, "tm", [(i, i ^ 1) for i in range(count)])

    def over_chip(v, d):
        return lax.ppermute(v, "tm", [(i, (i + 2 * d) % count) for i in range(count)])

    def over_x(v, d):
        return lax.ppermute(v, "space", [(i, (i + d) % 4) for i in range(4)])

    def over_y(v, d):
        return lax.ppermute(v, "tm", [(index(a, b, e), index(a + d, b, e)) for a, b, e in every])

    def over_z(v, d):
        return lax.ppermute(v, "tm", [(index(a, b, e), index(a, b + d, e)) for a, b, e in every])

    nclip = clip_len.shape[0]
    order = jnp.arange(nclip)
    ends = jnp.sum(jnp.where(order[None, :] <= order[:, None], clip_len[None, :], 0), axis=1)
    ids = chip * k + jnp.arange(-3 * chip, 4 * chip)
    clip = jnp.where(ids < 0, -1, jnp.sum(ends[None, :] <= ids[:, None], axis=1))
    mine = clip[3 * chip : 4 * chip]
    same = (clip[:, None] == mine[None, :]).astype(F32)
    member = mine[:, None] == order[None, :]
    lens = jnp.sum(jnp.where(member, clip_len[None, :], 0), axis=1)
    pos = ids[3 * chip : 4 * chip] - jnp.sum(jnp.where(member, (ends - clip_len)[None, :], 0), axis=1)
    lens = lens.astype(F32)
    keep = (pos[:, None] >= jnp.array([2, 1, 0])[None, :]).astype(F32).reshape(-1)
    own_pos = lax.dynamic_slice_in_dim(pos, c * nf, nf).astype(jnp.int32)

    table = jnp.asarray(half_table(chans, run, ny, nz), B16)
    flat = frames.reshape(nf, band, chans)
    past, last, top, bot, ptop, pbot = call(
        first_kernel,
        [shape((2, band, chans), B16), shape((1, band, chans), B16)]
        + [shape((nf, ncol, chans), B16)] * 2
        + [shape((2, ncol, chans), B16)] * 2,
        name="first",
    )(flat)
    both = ("tm", "space")
    top, bot = (
        lax.ppermute(bot, "space", [(i, i + 1) for i in range(3)]),
        lax.ppermute(top, "space", [(i + 1, i) for i in range(3)]),
    )
    past = lax.ppermute(past, "tm", [(i, i + 1) for i in range(count - 1)])
    ptop, pbot = (
        lax.ppermute(pbot, both, [(4 * i + j, 4 * (i + 1) + j + 1) for i in range(count - 1) for j in range(3)]),
        lax.ppermute(ptop, both, [(4 * i + j + 1, 4 * (i + 1) + j) for i in range(count - 1) for j in range(3)]),
    )
    flat, last, top, bot = lax.optimization_barrier((flat, last, top, bot))
    gathered = lax.all_gather(flat, "space", axis=0)
    last = lax.ppermute(last, "tm", [(i, i + 2) for i in range(1, count - 2, 2)])
    before = jnp.where(c == 0, past[:1], last)
    befores = [before] + [over_x(before, d) for d in (1, 2, 3)]

    whole = lambda *dims: pl.BlockSpec(dims, lambda i: (0,) * len(dims))
    zlat = head_weight.shape[1]
    hblock = zlat // 4
    block = chans // 4
    message = shape((block + 2 * hblock, cells), B16)
    latent, kframe, *mine_d = call(
        forward_kernel,
        [shape((cells, zlat), F32), shape((chip, 128), F32)] + [message] * 4,
        [
            pltpu.VMEM((cells, chans), F32),
            pltpu.VMEM(((nf + 2) * band, 9 * chans), B16),
            pltpu.VMEM((chans, cells), B16),
            pltpu.VMEM((nf, zlat, chans), F32),
        ],
        grid=(3,),
        in_specs=[smem(), smem()]
        + [whole(*v.shape) for v in (flat, past, top, bot, ptop, pbot)]
        + [pl.BlockSpec((1, 9 * chans, chans), lambda i: (i, 0, 0)), whole(zlat, chans)],
        out_specs=[whole(cells, zlat), whole(chip, 128)] + [whole(*message.shape)] * 4,
        name="forward",
    )(at, own_pos, flat, past, top, bot, ptop, pbot, conv_weight.reshape(3, 9 * chans, chans), head_weight.T)
    mine_d = [mine_d[0]] + [over_x(mine_d[d], d) for d in (1, 2, 3)]

    kchip = kframe + over_core(kframe)
    kchip, mine_d = lax.optimization_barrier((kchip, mine_d))
    kchip = kchip + over_x(kchip, 1) + over_x(kchip, 2) + over_x(kchip, 3)
    core_d = [over_core(v) for v in mine_d]
    triple = jnp.stack([over_chip(kchip, 1), kchip, over_chip(kchip, -1)])
    gathered, befores, triple = lax.optimization_barrier((gathered, befores, triple))
    left, right = over_chip(triple, 2), over_chip(triple, -2)
    lens_rows = jnp.broadcast_to(lens[:, None], (chip, 128))
    first_rows = jnp.broadcast_to((pos == 0).astype(F32)[:, None], (chip, 128))

    lanes = table.shape[2]
    chosen = shape((5, 4 * band, lanes), B16)
    spec = pl.BlockSpec((1, 4 * band, lanes), lambda i: (i, 0, 0))
    xown, xoth = call(
        choose_kernel,
        [chosen, chosen],
        [pltpu.VMEM((4 * band, chans), B16)],
        grid=(5,),
        in_specs=[
            smem(),
            pl.BlockSpec((4, 1, band, chans), lambda i: (0, jnp.maximum(i - 1, 0), 0, 0)),
        ]
        + [whole(1, band, chans)] * 4
        + [
            whole(*table.shape),
        ],
        out_specs=[spec, spec],
        name="choose",
    )(at, gathered, *befores, table)
    xoth = over_core(xoth)

    rows = run * nz
    wrow = 9 * block + 32
    sends = call(
        functools.partial(weight_kernel, ny, float(4 * band)),
        [shape((3, rows, wrow), F32)] + [shape((3, rows, wrow), B16)] * (ny - 1),
        [
            pltpu.VMEM((2, 4) + message.shape, B16),
            pltpu.VMEM((2, 9 * block, 4 * band), B16),
            pltpu.VMEM((3, wrow, lanes), F32),
            pltpu.VMEM((lanes, wrow), F32),
            pltpu.VMEM((10, 4 * band, lanes), B16),
            pltpu.VMEM((chip, 128), F32),
            pltpu.SemaphoreType.DMA((2, 2)),
        ],
        in_specs=[smem()] * 2 + [vmem()] * 14 + [pl.BlockSpec(memory_space=pl.ANY)] * 2 + [vmem()],
        name="weight",
    )(at, keep, left, kchip, right, same, lens_rows, first_rows, *mine_d, *core_d, xown, xoth, table)
    gets = [sends[0]] + [over_y(sends[d], d) for d in range(1, ny)]
    step = wide(run)
    chunk = 128 if wrow % 128 == 0 else wrow
    parts = call(
        functools.partial(add_kernel, ny, nz, run),
        [shape((3 * step, wrow), F32)] + [shape((3 * step, wrow), B16)] * (nz - 1),
        [pltpu.VMEM((wrow // chunk, 3, rows, chunk), F32), pltpu.VMEM((nz, 3 * step, wrow), F32)],
        in_specs=[smem()] + [vmem()] * ny,
        name="add",
    )(at, *gets)
    parts = [parts[0]] + [over_z(parts[d], d) for d in range(1, nz)]
    weight_grad, head_grad, loss = call(
        functools.partial(last_kernel, nz),
        [shape((run, 27, block), F32), shape((run, hblock), F32), shape((1, 1), F32)],
        name="last",
    )(*parts)
    return latent.reshape(nf, nrow, ncol, zlat), loss[0, 0], weight_grad.transpose(1, 0, 2), head_grad


def solution(mesh):
    in_specs = (P("tm", "space", None, None), P(), P(), P())
    out_specs = (P("tm", "space", None, None), P(), P(None, "tm", "space"), P("tm", "space"))
    return jax.shard_map(body, mesh=mesh, in_specs=in_specs, out_specs=out_specs, check_vma=False)
```

```python
import functools

import jax
import jax.numpy as jnp
import numpy as np
from jax import lax
from jax.experimental import pallas as pl
from jax.experimental.pallas import tpu as pltpu
from jax.sharding import PartitionSpec as P

F32 = jnp.float32
B16 = jnp.bfloat16
COLS = 24
LIMIT = 56 * 1024 * 1024
NT = (((1,), (1,)), ((), ()))
TN = (((0,), (0,)), ((), ()))


def dot(a, b, dims=None):
    if dims is None:
        return jnp.dot(a, b, preferred_element_type=F32)
    return lax.dot_general(a, b, dims, preferred_element_type=F32)


def call(kernel, outs, scratch=(), **kw):
    params = pltpu.CompilerParams(vmem_limit_bytes=LIMIT)
    return pl.pallas_call(kernel, out_shape=outs, scratch_shapes=list(scratch), compiler_params=params, **kw)


def smem():
    return pl.BlockSpec(memory_space=pltpu.SMEM)


def vmem():
    return pl.BlockSpec(memory_space=pltpu.VMEM)


def place(nz):
    t = lax.axis_index("tm")
    k = lax.div(t, 2)
    return lax.rem(t, 2), lax.axis_index("space"), lax.div(k, nz), lax.rem(k, nz), k


def half_table(chans, run, ny, nz):
    lane = np.arange(chans // 2)
    block = wide(run) * nz
    spot = (lane // run // nz) * block + (lane % run) * nz + lane // run % nz
    table = np.zeros((2, chans, ny * block), np.float32)
    for core in range(2):
        table[core, (lane // run) * 2 * run + core * run + lane % run, spot] = 1
    return table


def wide(run):
    return -(-run // 8) * 8


def first_kernel(x_ref, top_ref, bot_ref):
    nf, band, chans = x_ref.shape
    for f in range(nf):
        wide_frame = x_ref[f].astype(F32)
        top_ref[f] = wide_frame[:COLS].astype(B16)
        bot_ref[f] = wide_frame[band - COLS :].astype(B16)


def frame_of(top, mid, bot):
    return jnp.concatenate([top.astype(F32), mid.astype(F32), bot.astype(F32)], axis=0)


def ends_kernel(x_ref, top_ref, bot_ref, ends_ref, last_ref):
    nf = x_ref.shape[0]
    for f in range(2):
        g = nf - 2 + f
        ends_ref[f] = frame_of(top_ref[g], x_ref[g], bot_ref[g]).astype(B16)
    last_ref[0] = x_ref[nf - 1]


def choose_kernel(f0, f1, f2, f3, p0, p1, p2, p3, table_ref, own_ref, oth_ref, wide_ref):
    c, x = lax.rem(lax.axis_index("tm"), 2), lax.axis_index("space")
    band = f0.shape[1]

    def put(refs):
        for d, ref in enumerate(refs):
            wide_ref[pl.ds(pl.multiple_of(lax.rem(x - d + 4, 4) * band, band), band)] = ref[0]

    @pl.when(pl.program_id(0) == 0)
    def _():
        put((p0, p1, p2, p3))

    @pl.when(pl.program_id(0) > 0)
    def _():
        put((f0, f1, f2, f3))

    both = dot(wide_ref[...], table_ref[...]).astype(B16)
    lanes = own_ref.shape[2]

    @pl.when(c == 0)
    def _():
        own_ref[0] = both[:, :lanes]
        oth_ref[0] = both[:, lanes:]

    @pl.when(c == 1)
    def _():
        own_ref[0] = both[:, lanes:]
        oth_ref[0] = both[:, :lanes]


def forward_kernel(len_ref, x_ref, ends_ref, last_ref, top_ref, bot_ref, w_ref, hw_ref,
                   lat_ref, before_ref, d0, d1, d2, d3, pre_ref, wide_ref, turned_ref, head_ref):
    step = pl.program_id(0)
    nf, band, chans = x_ref.shape
    rows = band + 2 * COLS

    @pl.when(step == 0)
    def _():
        col = lax.rem(lax.broadcasted_iota(jnp.int32, (rows, 1), 0), COLS)
        for f in range(nf + 2):
            if f < 2:
                v = ends_ref[f].astype(F32)
            else:
                v = frame_of(top_ref[f - 2], x_ref[f - 2], bot_ref[f - 2])
            if f == 0:
                core = jnp.broadcast_to(lax.rem(lax.axis_index("tm"), 2), (1, 1))
                before_ref[0] = jnp.where(core == 0, v[COLS : COLS + band], last_ref[0].astype(F32)).astype(B16)
            for dw in range(3):
                if dw == 0:
                    s = jnp.where(col > 0, pltpu.roll(v, 1, 0), 0.0)
                elif dw == 2:
                    s = jnp.where(col < COLS - 1, pltpu.roll(v, rows - 1, 0), 0.0)
                else:
                    s = v
                for dh in range(3):
                    q = dh * 3 + dw
                    wide_ref[f * band : (f + 1) * band, q * chans : (q + 1) * chans] = s[
                        dh * COLS : dh * COLS + band
                    ].astype(B16)

    t, xs = lax.axis_index("tm"), lax.axis_index("space")
    pos = [jnp.int32(0)] * nf
    start = jnp.int32(0)
    for j in range(len_ref.shape[0]):
        for f in range(nf):
            pos[f] = jnp.where(t * nf + f >= start, t * nf + f - start, pos[f])
        start = start + len_ref[j]
    dt = step
    part = dot(wide_ref[pl.ds(pl.multiple_of(dt * band, band), nf * band), :], w_ref[0])
    for f in range(nf):
        keep = jnp.where(pos[f] >= 2 - dt, 1.0, 0.0)
        piece = keep * part[f * band : (f + 1) * band]

        @pl.when(step == 0)
        def _():
            pre_ref[f * band : (f + 1) * band] = piece

        @pl.when(step > 0)
        def _():
            pre_ref[f * band : (f + 1) * band] += piece

    @pl.when(step == 2)
    def _():
        zdim = lat_ref.shape[1] // 2
        row = lax.broadcasted_iota(jnp.int32, (16, 128), 0)
        kf = jnp.zeros((16, 128), F32)
        for f in range(nf):
            at = slice(f * band, (f + 1) * band)
            pre = pre_ref[at]
            sig = 1.0 / (1.0 + jnp.exp(-pre))
            act = (pre * sig).astype(B16)
            lat = dot(act, hw_ref[...], NT)
            lat_ref[at] = lat
            lane = lax.broadcasted_iota(jnp.int32, lat.shape, 1)
            grow = jnp.exp(lat) - 1.0
            term = jnp.where(lane < zdim, lat * lat, grow - lat)
            kf = jnp.where(lax.rem(row, nf) == f, 0.5 * jnp.sum(term), kf)
            dlat = jnp.where(lane < zdim, lat, 0.5 * grow).astype(B16)
            dact = dot(dlat, hw_ref[...])
            pre_ref[at] = (dact * sig * (1.0 + pre * (1.0 - sig))).astype(B16).astype(F32)
            head_ref[f] = dot(dlat, act, TN)
        high = kf.astype(B16).astype(F32)
        mid = (kf - high).astype(B16).astype(F32)
        kf = jnp.where(row < nf, high, jnp.where(row < 2 * nf, mid, jnp.where(row < 3 * nf, kf - high - mid, 0.0)))
        turned_ref[...] = jnp.transpose(pre_ref[...], (1, 0)).astype(B16)
        block = chans // 4
        hblock = 2 * zdim // 4
        for d, ref in enumerate((d0, d1, d2, d3)):
            to = lax.rem(xs + d, 4)
            ref[:16, :128] = kf.astype(B16)
            ref[:16, 128:] = jnp.zeros((16, ref.shape[1] - 128), B16)
            ref[32:] = turned_ref[pl.ds(pl.multiple_of(to * block, block), block), :]
            heads = [head_ref[f, pl.ds(pl.multiple_of(to * hblock, hblock), hblock), :] for f in range(nf)]
            pad = ref.shape[1] - 2 * chans
            if pad:
                heads = [jnp.concatenate([h, jnp.zeros((hblock, pad // 2), F32)], axis=1) for h in heads]
            both = jnp.concatenate(
                [jnp.concatenate(heads[:2], axis=1), jnp.concatenate(heads[2:], axis=1)], axis=0
            )
            ref[16:32] = both.astype(B16)


def clip_kernel(*refs):
    c = lax.rem(lax.axis_index("tm"), 2)
    sums = []
    for given in (refs[:4], refs[4:8]):
        v = given[0][...].astype(F32)
        for ref in given[1:]:
            v = v + ref[...].astype(F32)
        sums.append(v[:4] + v[4:8] + v[8:12])
    own, oth = sums

    @pl.when(c == 0)
    def _():
        refs[8][...] = jnp.concatenate([own, oth], axis=0)

    @pl.when(c == 1)
    def _():
        refs[8][...] = jnp.concatenate([oth, own], axis=0)


def weight_kernel(ny, nz, per_frame, len_ref, left_ref, mid_ref, right_ref, a0, a1, a2, a3, b0, b1, b2, b3,
                  x_ref, xo_ref, table_ref, *refs):
    sends, (held_ref, taps_ref, acc_ref, out_ref, xs_ref, g_ref, keep_ref, sem) = refs[:ny], refs[ny:]
    c, x, y, _, k = place(nz)
    copies = []
    for core, ref, s in ((c, x_ref, 0), (1 - c, xo_ref, 1)):
        copies.append(pltpu.make_async_copy(ref.at[0:1], xs_ref.at[pl.ds(core, 1)], sem.at[s, 0]))
        copies.append(pltpu.make_async_copy(ref.at[1:5], xs_ref.at[pl.ds(2 + 4 * core, 4)], sem.at[s, 1]))
    for copy in copies:
        copy.start()
    full = x_ref.shape[1]
    band = full // 4
    block = taps_ref.shape[1] // 9
    chans = table_ref.shape[0]
    lanes = acc_ref.shape[2]
    hblock = 8
    half = full // 2
    window = jnp.concatenate(
        [left_ref[0], left_ref[1], left_ref[2], mid_ref[...], right_ref[0], right_ref[1], right_ref[2]], axis=0
    )
    chip = g_ref.shape[0]
    wids = chip * (k - 3) + lax.broadcasted_iota(jnp.int32, window.shape, 0)
    ids = chip * k + lax.broadcasted_iota(jnp.int32, g_ref.shape, 0)
    total = jnp.zeros(g_ref.shape, F32)
    lens = jnp.ones(g_ref.shape, F32)
    pos = ids
    start = jnp.int32(0)
    for j in range(len_ref.shape[0]):
        size = len_ref[j]
        inside = jnp.where((wids >= start) & (wids < start + size), window, 0.0)
        mine = (ids >= start) & (ids < start + size)
        total = jnp.where(mine, jnp.sum(inside, axis=0, keepdims=True), total)
        lens = jnp.where(mine, size.astype(F32), lens)
        pos = jnp.where(mine, ids - start, pos)
        start = start + size
    gain = lens / (lens * per_frame + total)
    g_ref[...] = gain
    for dt in range(3):
        keep_ref[dt] = jnp.where(pos >= 2 - dt, gain, 0.0)
    loss = jnp.where(pos == 0, lens * jnp.log1p(total / (lens * per_frame)), 0.0)
    loss = jnp.sum(loss, axis=0, keepdims=True)
    hsum = jnp.zeros((hblock, chans), F32)
    for core, given in ((c, (a0, a1, a2, a3)), (1 - c, (b0, b1, b2, b3))):
        for d, ref in enumerate(given):
            held_ref[core, lax.rem(x - d + 4, 4)] = ref[...]
            tail = ref[16:32, :].astype(F32)
            for f in range(4):
                part = tail[(f // 2) * hblock : (f // 2 + 1) * hblock, (f % 2) * half : (f % 2) * half + chans]
                hsum = hsum + g_ref[pl.ds(core * 4 + f, 1), :][:, :1] * part
    acc_ref[...] = jnp.zeros(acc_ref.shape, F32)
    lane = lax.broadcasted_iota(jnp.int32, (1, full), 1)
    col = lax.rem(lane, COLS)
    line = lane // COLS

    def build(f):
        core, lf = f // 4, f % 4
        frame = jnp.zeros((block, full), F32)
        for xs in range(4):
            v = held_ref[core, xs, 32:, :].astype(F32)
            shift = ((xs - lf) * band) % full
            if shift:
                v = pltpu.roll(v, shift, 1)
            frame = jnp.where(lane // band == xs, v, frame)
        for dw in range(3):
            if dw == 0:
                v = jnp.where(col < COLS - 1, pltpu.roll(frame, full - 1, 1), 0.0)
            elif dw == 2:
                v = jnp.where(col > 0, pltpu.roll(frame, 1, 1), 0.0)
            else:
                v = frame
            for dh in range(3):
                if dh == 0:
                    s = jnp.where(line < full // COLS - 1, pltpu.roll(v, full - COLS, 1), 0.0)
                elif dh == 2:
                    s = jnp.where(line > 0, pltpu.roll(v, COLS, 1), 0.0)
                else:
                    s = v
                q = dh * 3 + dw
                taps_ref[f % 2, q * block : (q + 1) * block, :] = s.astype(B16)

    build(0)
    for copy in copies:
        copy.wait()
    for f in range(8):
        if f < 7:
            build(f + 1)
        for dt in range(3):
            scale = keep_ref[dt, f : f + 1, :1]
            acc_ref[dt, : 9 * block] += scale * dot(taps_ref[f % 2], xs_ref[f + dt])
    direct = jnp.where(c == 0, table_ref[:, :lanes].astype(F32), table_ref[:, lanes:].astype(F32)).astype(B16)
    high = hsum.astype(B16)
    low = (hsum - high.astype(F32)).astype(B16)
    acc_ref[0, 9 * block : 9 * block + hblock] = dot(high, direct) + dot(low, direct)
    loss = jnp.broadcast_to(loss[:, :1], (8, lanes))
    top = loss.astype(B16).astype(F32)
    mid = (loss - top).astype(B16).astype(F32)
    acc_ref[1, 9 * block : 9 * block + 8] = top
    acc_ref[1, 9 * block + 8 : 9 * block + 16] = mid
    acc_ref[1, 9 * block + 16 : 9 * block + 24] = loss - top - mid
    rows = sends[0].shape[1]
    ystep = lanes // ny
    for dt in range(3):
        out_ref[...] = jnp.transpose(acc_ref[dt], (1, 0))
        for d, ref in enumerate(sends):
            to = lax.rem(y + d, ny)
            ref[dt] = out_ref[pl.ds(pl.multiple_of(to * ystep, 8), rows), :].astype(ref.dtype)


def add_kernel(ny, nz, run, *refs):
    gets, sends, (sum_ref, part_ref) = refs[:ny], refs[ny : ny + nz], refs[ny + nz :]
    total = gets[0][...]
    for ref in gets[1:]:
        total = total + ref[...].astype(F32)
    chunk = sum_ref.shape[3]
    for i in range(sum_ref.shape[0]):
        sum_ref[i] = total[:, :, i * chunk : (i + 1) * chunk]
    part_ref[...] = jnp.zeros(part_ref.shape, F32)
    step = part_ref.shape[1] // 3
    for z in range(nz):
        for dt in range(3):
            for i in range(sum_ref.shape[0]):
                part_ref[z, dt * step : dt * step + run, i * chunk : (i + 1) * chunk] = sum_ref[
                    i, dt, pl.ds(z, run, stride=nz), :
                ]
    for d, ref in enumerate(sends):
        ref[...] = part_ref[lax.rem(place(nz)[3] + d, nz)].astype(ref.dtype)


def last_kernel(count, *refs):
    parts, (weight_ref, head_ref, loss_ref) = refs[:count], refs[count:]
    total = parts[0][...]
    for ref in parts[1:]:
        total = total + ref[...].astype(F32)
    run, _, block = weight_ref.shape
    step = total.shape[0] // 3
    for dt in range(3):
        for q in range(9):
            weight_ref[:, dt * 9 + q, :] = total[dt * step : dt * step + run, q * block : (q + 1) * block]
    base = 9 * block
    head_ref[...] = total[:run, base : base + head_ref.shape[1]]
    loss = total[step : step + 1, base : base + 1]
    loss = loss + total[step : step + 1, base + 8 : base + 9]
    loss_ref[...] = loss + total[step : step + 1, base + 16 : base + 17]


def body(frames, conv_weight, head_weight, clip_len):
    nf, nrow, ncol, chans = frames.shape
    band = nrow * ncol
    cells = nf * band
    count = lax.axis_size("tm")
    ny = 4 if count == 64 else 2
    nz = count // 2 // ny
    run = chans // count
    chip = 2 * nf
    shape = jax.ShapeDtypeStruct

    def index(yy, zz, cc):
        return ((yy % ny) * nz + zz % nz) * 2 + cc

    every = [(yy, zz, cc) for yy in range(ny) for zz in range(nz) for cc in range(2)]

    def over_core(v):
        return lax.ppermute(v, "tm", [(i, i ^ 1) for i in range(count)])

    def over_chip(v, d):
        return lax.ppermute(v, "tm", [(i, (i + 2 * d) % count) for i in range(count)])

    def over_x(v, d):
        return lax.ppermute(v, "space", [(i, (i + d) % 4) for i in range(4)])

    def over_y(v, d):
        return lax.ppermute(v, "tm", [(index(a, b, e), index(a + d, b, e)) for a, b, e in every])

    def over_z(v, d):
        return lax.ppermute(v, "tm", [(index(a, b, e), index(a, b + d, e)) for a, b, e in every])

    table = half_table(chans, run, ny, nz)
    lanes = table.shape[2]
    table = jnp.asarray(np.concatenate([table[0], table[1]], axis=1), B16)
    flat = frames.reshape(nf, band, chans)
    edge = shape((nf, ncol, chans), B16)
    top, bot = call(first_kernel, [edge, edge], name="first")(flat)
    top, bot = (
        lax.ppermute(bot, "space", [(i, i + 1) for i in range(3)]),
        lax.ppermute(top, "space", [(i + 1, i) for i in range(3)]),
    )
    flat, top, bot = lax.optimization_barrier((flat, top, bot))
    flats = [flat] + [over_x(flat, d) for d in (1, 2, 3)]
    ends, last = call(
        ends_kernel, [shape((2, band + 2 * ncol, chans), B16), shape((1, band, chans), B16)], name="ends"
    )(flat, top, bot)
    ends = lax.ppermute(ends, "tm", [(i, i + 1) for i in range(count - 1)])
    last = lax.ppermute(last, "tm", [(i, i + 2) for i in range(1, count - 2, 2)])

    whole = lambda *dims: pl.BlockSpec(dims, lambda i: (0,) * len(dims))
    zlat = head_weight.shape[1]
    hblock = zlat // 4
    block = chans // 4
    message = shape((32 + block, cells), B16)
    latent, before, *mine_d = call(
        forward_kernel,
        [shape((cells, zlat), F32), shape((1, band, chans), B16)] + [message] * 4,
        [
            pltpu.VMEM((cells, chans), F32),
            pltpu.VMEM(((nf + 2) * band, 9 * chans), B16),
            pltpu.VMEM((chans, cells), B16),
            pltpu.VMEM((nf, zlat, chans), F32),
        ],
        grid=(3,),
        in_specs=[smem()]
        + [whole(*v.shape) for v in (flat, ends, last, top, bot)]
        + [pl.BlockSpec((1, 9 * chans, chans), lambda i: (i, 0, 0)), whole(zlat, chans)],
        out_specs=[whole(cells, zlat), whole(1, band, chans)] + [whole(*message.shape)] * 4,
        name="forward",
    )(clip_len, flat, ends, last, top, bot, conv_weight.reshape(3, 9 * chans, chans), head_weight.T)
    mine_d, flats = lax.optimization_barrier((mine_d, flats))
    mine_d = [mine_d[0]] + [over_x(mine_d[d], d) for d in (1, 2, 3)]

    befores = [before] + [over_x(before, d) for d in (1, 2, 3)]
    core_d = [over_core(v) for v in mine_d]

    corner = pl.BlockSpec((16, 128), lambda i: (0, 0))
    kchip = call(
        clip_kernel,
        shape((chip, 128), F32),
        grid=(1,),
        in_specs=[corner] * 8,
        out_specs=whole(chip, 128),
        name="clip",
    )(*mine_d, *core_d)
    chosen = shape((5, 4 * band, lanes), B16)
    spec = pl.BlockSpec((1, 4 * band, lanes), lambda i: (i, 0, 0))
    befores, kchip = lax.optimization_barrier((befores, kchip))
    xown, xoth = call(
        choose_kernel,
        [chosen, chosen],
        [pltpu.VMEM((4 * band, chans), B16)],
        grid=(5,),
        in_specs=[pl.BlockSpec((1, band, chans), lambda i: (jnp.maximum(i - 1, 0), 0, 0))] * 4
        + [whole(1, band, chans)] * 4
        + [whole(*table.shape)],
        out_specs=[spec, spec],
        name="choose",
    )(*flats, *befores, table)
    xoth = over_core(xoth)
    triple = jnp.stack([over_chip(kchip, 1), kchip, over_chip(kchip, -1)])
    left, right = over_chip(triple, 2), over_chip(triple, -2)


    rows = run * nz
    wrow = 9 * block + 32
    sends = call(
        functools.partial(weight_kernel, ny, nz, float(4 * band)),
        [shape((3, rows, wrow), F32)] + [shape((3, rows, wrow), B16)] * (ny - 1),
        [
            pltpu.VMEM((2, 4) + message.shape, B16),
            pltpu.VMEM((2, 9 * block, 4 * band), B16),
            pltpu.VMEM((3, wrow, lanes), F32),
            pltpu.VMEM((lanes, wrow), F32),
            pltpu.VMEM((10, 4 * band, lanes), B16),
            pltpu.VMEM((chip, 128), F32),
            pltpu.VMEM((3, chip, 128), F32),
            pltpu.SemaphoreType.DMA((2, 2)),
        ],
        in_specs=[smem()] + [vmem()] * 11 + [pl.BlockSpec(memory_space=pl.ANY)] * 2 + [vmem()],
        name="weight",
    )(clip_len, left, kchip, right, *mine_d, *core_d, xown, xoth, table)
    gets = [sends[0]] + [over_y(sends[d], d) for d in range(1, ny)]
    step = wide(run)
    chunk = 128 if wrow % 128 == 0 else wrow
    parts = call(
        functools.partial(add_kernel, ny, nz, run),
        [shape((3 * step, wrow), F32)] + [shape((3 * step, wrow), B16)] * (nz - 1),
        [pltpu.VMEM((wrow // chunk, 3, rows, chunk), F32), pltpu.VMEM((nz, 3 * step, wrow), F32)],
        name="add",
    )(*gets)
    parts = [parts[0]] + [over_z(parts[d], d) for d in range(1, nz)]
    weight_grad, head_grad, loss = call(
        functools.partial(last_kernel, nz),
        [shape((run, 27, block), F32), shape((run, hblock), F32), shape((1, 1), F32)],
        name="last",
    )(*parts)
    return latent.reshape(nf, nrow, ncol, zlat), loss[0, 0], weight_grad.transpose(1, 0, 2), head_grad


def solution(mesh):
    in_specs = (P("tm", "space", None, None), P(), P(), P())
    out_specs = (P("tm", "space", None, None), P(), P(None, "tm", "space"), P("tm", "space"))
    return jax.shard_map(body, mesh=mesh, in_specs=in_specs, out_specs=out_specs, check_vma=False)
```

```python
import functools

import jax
import jax.numpy as jnp
import numpy as np
from jax import lax
from jax.experimental import pallas as pl
from jax.experimental.pallas import tpu as pltpu
from jax.sharding import PartitionSpec as P

F32 = jnp.float32
B16 = jnp.bfloat16
COLS = 24
LIMIT = 56 * 1024 * 1024
NT = (((1,), (1,)), ((), ()))
TN = (((0,), (0,)), ((), ()))


def dot(a, b, dims=None):
    if dims is None:
        return jnp.dot(a, b, preferred_element_type=F32)
    return lax.dot_general(a, b, dims, preferred_element_type=F32)


def call(kernel, outs, scratch=(), **kw):
    params = pltpu.CompilerParams(vmem_limit_bytes=LIMIT)
    return pl.pallas_call(kernel, out_shape=outs, scratch_shapes=list(scratch), compiler_params=params, **kw)


def smem():
    return pl.BlockSpec(memory_space=pltpu.SMEM)


def vmem():
    return pl.BlockSpec(memory_space=pltpu.VMEM)


def place(nz):
    t = lax.axis_index("tm")
    k = lax.div(t, 2)
    return lax.rem(t, 2), lax.axis_index("space"), lax.div(k, nz), lax.rem(k, nz), k


def half_table(chans, run, ny, nz):
    lane = np.arange(chans // 2)
    block = wide(run) * nz
    spot = (lane // run // nz) * block + (lane % run) * nz + lane // run % nz
    table = np.zeros((2, chans, ny * block), np.float32)
    for core in range(2):
        table[core, (lane // run) * 2 * run + core * run + lane % run, spot] = 1
    return table


def wide(run):
    return -(-run // 8) * 8


def first_kernel(x_ref, top_ref, bot_ref):
    nf, band, chans = x_ref.shape
    for f in range(nf):
        wide_frame = x_ref[f].astype(F32)
        top_ref[f] = wide_frame[:COLS].astype(B16)
        bot_ref[f] = wide_frame[band - COLS :].astype(B16)


def frame_of(top, mid, bot):
    return jnp.concatenate([top.astype(F32), mid.astype(F32), bot.astype(F32)], axis=0)


def ends_kernel(x_ref, top_ref, bot_ref, ends_ref, last_ref):
    nf = x_ref.shape[0]
    for f in range(2):
        g = nf - 2 + f
        ends_ref[f] = frame_of(top_ref[g], x_ref[g], bot_ref[g]).astype(B16)
    last_ref[0] = x_ref[nf - 1]


def choose_kernel(f0, f1, f2, f3, p0, p1, p2, p3, table_ref, own_ref, oth_ref, wide_ref):
    c, x = lax.rem(lax.axis_index("tm"), 2), lax.axis_index("space")
    band = f0.shape[1]

    def put(refs):
        for d, ref in enumerate(refs):
            wide_ref[pl.ds(pl.multiple_of(lax.rem(x - d + 4, 4) * band, band), band)] = ref[0]

    @pl.when(pl.program_id(0) == 0)
    def _():
        put((p0, p1, p2, p3))

    @pl.when(pl.program_id(0) > 0)
    def _():
        put((f0, f1, f2, f3))

    both = dot(wide_ref[...], table_ref[c]).astype(B16)
    lanes = own_ref.shape[2]
    own_ref[0] = both[:, :lanes]
    oth_ref[0] = both[:, lanes:]


def forward_kernel(len_ref, x_ref, ends_ref, last_ref, top_ref, bot_ref, w_ref, hw_ref,
                   lat_ref, before_ref, d0, d1, d2, d3, pre_ref, wide_ref, turned_ref, head_ref, held_ref, sem):
    nf, band, chans = x_ref.shape
    rows = band + 2 * COLS
    loads = [pltpu.make_async_copy(w_ref.at[dt], held_ref.at[dt], sem.at[dt]) for dt in range(3)]
    for load in loads:
        load.start()
    col = lax.rem(lax.broadcasted_iota(jnp.int32, (rows, 1), 0), COLS)
    for f in range(nf + 2):
        if f < 2:
            v = ends_ref[f].astype(F32)
        else:
            v = frame_of(top_ref[f - 2], x_ref[f - 2], bot_ref[f - 2])
        if f == 0:
            core = jnp.broadcast_to(lax.rem(lax.axis_index("tm"), 2), (1, 1))
            before_ref[0] = jnp.where(core == 0, v[COLS : COLS + band], last_ref[0].astype(F32)).astype(B16)
        for dw in range(3):
            if dw == 0:
                s = jnp.where(col > 0, pltpu.roll(v, 1, 0), 0.0)
            elif dw == 2:
                s = jnp.where(col < COLS - 1, pltpu.roll(v, rows - 1, 0), 0.0)
            else:
                s = v
            for dh in range(3):
                q = dh * 3 + dw
                wide_ref[f * band : (f + 1) * band, q * chans : (q + 1) * chans] = s[
                    dh * COLS : dh * COLS + band
                ].astype(B16)

    t, xs = lax.axis_index("tm"), lax.axis_index("space")
    pos = [jnp.int32(0)] * nf
    start = jnp.int32(0)
    for j in range(len_ref.shape[0]):
        for f in range(nf):
            pos[f] = jnp.where(t * nf + f >= start, t * nf + f - start, pos[f])
        start = start + len_ref[j]
    for dt in range(3):
        loads[dt].wait()
        part = dot(wide_ref[dt * band : (dt + nf) * band, :], held_ref[dt])
        for f in range(nf):
            keep = jnp.where(pos[f] >= 2 - dt, 1.0, 0.0)
            piece = keep * part[f * band : (f + 1) * band]
            if dt == 0:
                pre_ref[f * band : (f + 1) * band] = piece
            else:
                pre_ref[f * band : (f + 1) * band] += piece

    zdim = lat_ref.shape[1] // 2
    row = lax.broadcasted_iota(jnp.int32, (16, 128), 0)
    kf = jnp.zeros((16, 128), F32)
    for f in range(nf):
        at = slice(f * band, (f + 1) * band)
        pre = pre_ref[at]
        sig = 1.0 / (1.0 + jnp.exp(-pre))
        act = (pre * sig).astype(B16)
        lat = dot(act, hw_ref[...], NT)
        lat_ref[at] = lat
        lane = lax.broadcasted_iota(jnp.int32, lat.shape, 1)
        grow = jnp.exp(lat) - 1.0
        term = jnp.where(lane < zdim, lat * lat, grow - lat)
        kf = jnp.where(lax.rem(row, nf) == f, 0.5 * jnp.sum(term), kf)
        dlat = jnp.where(lane < zdim, lat, 0.5 * grow).astype(B16)
        dact = dot(dlat, hw_ref[...])
        pre_ref[at] = (dact * sig * (1.0 + pre * (1.0 - sig))).astype(B16).astype(F32)
        head_ref[f] = dot(dlat, act, TN)
    high = kf.astype(B16).astype(F32)
    mid = (kf - high).astype(B16).astype(F32)
    kf = jnp.where(row < nf, high, jnp.where(row < 2 * nf, mid, jnp.where(row < 3 * nf, kf - high - mid, 0.0)))
    turned_ref[...] = jnp.transpose(pre_ref[...], (1, 0)).astype(B16)
    block = chans // 4
    hblock = 2 * zdim // 4
    for d, ref in enumerate((d0, d1, d2, d3)):
        to = lax.rem(xs + d, 4)
        ref[:16, :128] = kf.astype(B16)
        ref[:16, 128:] = jnp.zeros((16, ref.shape[1] - 128), B16)
        ref[32:] = turned_ref[pl.ds(pl.multiple_of(to * block, block), block), :]
        heads = [head_ref[f, pl.ds(pl.multiple_of(to * hblock, hblock), hblock), :] for f in range(nf)]
        pad = ref.shape[1] - 2 * chans
        if pad:
            heads = [jnp.concatenate([h, jnp.zeros((hblock, pad // 2), F32)], axis=1) for h in heads]
        both = jnp.concatenate(
            [jnp.concatenate(heads[:2], axis=1), jnp.concatenate(heads[2:], axis=1)], axis=0
        )
        ref[16:32] = both.astype(B16)


def relay_kernel(a0, a1, a2, a3, out_ref):
    x = lax.axis_index("space")
    for d, ref in enumerate((a0, a1, a2, a3)):
        out_ref[lax.rem(x - d + 4, 4)] = ref[...]


def clip_kernel(*refs):
    c = lax.rem(lax.axis_index("tm"), 2)
    sums = []
    for ref in refs[:2]:
        v = ref[0].astype(F32)
        for xs in range(1, 4):
            v = v + ref[xs].astype(F32)
        sums.append(v[:4] + v[4:8] + v[8:12])
    own, oth = sums

    @pl.when(c == 0)
    def _():
        refs[2][...] = jnp.concatenate([own, oth], axis=0)

    @pl.when(c == 1)
    def _():
        refs[2][...] = jnp.concatenate([oth, own], axis=0)


def weight_kernel(ny, nz, per_frame, len_ref, k0, k1, k2, k3, k4, k5, k6, a_ref, b_ref, x_ref, xo_ref, table_ref, *refs):
    sends, (held_ref, taps_ref, acc_ref, out_ref, xs_ref, g_ref, keep_ref, sem) = refs[:ny], refs[ny:]
    c, x, y, _, k = place(nz)
    copies = []
    for core, ref, s in ((c, x_ref, 0), (1 - c, xo_ref, 1)):
        copies.append(pltpu.make_async_copy(ref.at[0:1], xs_ref.at[pl.ds(core, 1)], sem.at[s, 0]))
        copies.append(pltpu.make_async_copy(ref.at[1:5], xs_ref.at[pl.ds(2 + 4 * core, 4)], sem.at[s, 1]))
    copies.append(pltpu.make_async_copy(a_ref, held_ref.at[c], sem.at[2, 0]))
    copies.append(pltpu.make_async_copy(b_ref, held_ref.at[1 - c], sem.at[2, 1]))
    for copy in copies[::-1]:
        copy.start()
    full = x_ref.shape[1]
    band = full // 4
    block = taps_ref.shape[1] // 9
    chans = table_ref.shape[1]
    lanes = acc_ref.shape[2]
    hblock = 8
    half = full // 2
    window = jnp.concatenate([ref[...] for ref in (k0, k1, k2, k3, k4, k5, k6)], axis=0)
    chip = g_ref.shape[0]
    wids = chip * (k - 3) + lax.broadcasted_iota(jnp.int32, window.shape, 0)
    ids = chip * k + lax.broadcasted_iota(jnp.int32, g_ref.shape, 0)
    total = jnp.zeros(g_ref.shape, F32)
    lens = jnp.ones(g_ref.shape, F32)
    pos = ids
    start = jnp.int32(0)
    for j in range(len_ref.shape[0]):
        size = len_ref[j]
        inside = jnp.where((wids >= start) & (wids < start + size), window, 0.0)
        mine = (ids >= start) & (ids < start + size)
        total = jnp.where(mine, jnp.sum(inside, axis=0, keepdims=True), total)
        lens = jnp.where(mine, size.astype(F32), lens)
        pos = jnp.where(mine, ids - start, pos)
        start = start + size
    gain = lens / (lens * per_frame + total)
    g_ref[...] = gain
    for dt in range(3):
        keep_ref[dt] = jnp.where(pos >= 2 - dt, gain, 0.0)
    loss = jnp.where(pos == 0, lens * jnp.log1p(total / (lens * per_frame)), 0.0)
    loss = jnp.sum(loss, axis=0, keepdims=True)
    hsum = jnp.zeros((hblock, chans), F32)
    for copy in copies[4:]:
        copy.wait()
    for core in range(2):
        for xs in range(4):
            tail = held_ref[core, xs, 16:32, :].astype(F32)
            for f in range(4):
                part = tail[(f // 2) * hblock : (f // 2 + 1) * hblock, (f % 2) * half : (f % 2) * half + chans]
                hsum = hsum + g_ref[core * 4 + f : core * 4 + f + 1, :1] * part
    acc_ref[...] = jnp.zeros(acc_ref.shape, F32)
    lane = lax.broadcasted_iota(jnp.int32, (1, full), 1)
    col = lax.rem(lane, COLS)
    line = lane // COLS

    def build(f):
        core, lf = f // 4, f % 4
        frame = jnp.zeros((block, full), F32)
        for xs in range(4):
            v = held_ref[core, xs, 32:, :].astype(F32)
            shift = ((xs - lf) * band) % full
            if shift:
                v = pltpu.roll(v, shift, 1)
            frame = jnp.where(lane // band == xs, v, frame)
        for dw in range(3):
            if dw == 0:
                v = jnp.where(col < COLS - 1, pltpu.roll(frame, full - 1, 1), 0.0)
            elif dw == 2:
                v = jnp.where(col > 0, pltpu.roll(frame, 1, 1), 0.0)
            else:
                v = frame
            for dh in range(3):
                if dh == 0:
                    s = jnp.where(line < full // COLS - 1, pltpu.roll(v, full - COLS, 1), 0.0)
                elif dh == 2:
                    s = jnp.where(line > 0, pltpu.roll(v, COLS, 1), 0.0)
                else:
                    s = v
                q = dh * 3 + dw
                taps_ref[f % 2, q * block : (q + 1) * block, :] = s.astype(B16)

    build(0)
    for copy in copies[:4]:
        copy.wait()
    for f in range(8):
        if f < 7:
            build(f + 1)
        for dt in range(3):
            scale = keep_ref[dt, f : f + 1, :1]
            acc_ref[dt, : 9 * block] += scale * dot(taps_ref[f % 2], xs_ref[f + dt])
    direct = table_ref[c, :, :lanes]
    high = hsum.astype(B16)
    low = (hsum - high.astype(F32)).astype(B16)
    acc_ref[0, 9 * block : 9 * block + hblock] = dot(high, direct) + dot(low, direct)
    loss = jnp.broadcast_to(loss[:, :1], (8, lanes))
    top = loss.astype(B16).astype(F32)
    mid = (loss - top).astype(B16).astype(F32)
    acc_ref[1, 9 * block : 9 * block + 8] = top
    acc_ref[1, 9 * block + 8 : 9 * block + 16] = mid
    acc_ref[1, 9 * block + 16 : 9 * block + 24] = loss - top - mid
    rows = sends[0].shape[1]
    ystep = lanes // ny
    for dt in range(3):
        out_ref[...] = jnp.transpose(acc_ref[dt], (1, 0))
        for d, ref in enumerate(sends):
            to = lax.rem(y + d, ny)
            ref[dt] = out_ref[pl.ds(pl.multiple_of(to * ystep, 8), rows), :].astype(ref.dtype)


def add_kernel(ny, nz, run, *refs):
    gets, sends, (sum_ref, part_ref) = refs[:ny], refs[ny : ny + nz], refs[ny + nz :]
    total = gets[0][...]
    for ref in gets[1:]:
        total = total + ref[...].astype(F32)
    chunk = sum_ref.shape[3]
    for i in range(sum_ref.shape[0]):
        sum_ref[i] = total[:, :, i * chunk : (i + 1) * chunk]
    part_ref[...] = jnp.zeros(part_ref.shape, F32)
    step = part_ref.shape[1] // 3
    for z in range(nz):
        for dt in range(3):
            for i in range(sum_ref.shape[0]):
                part_ref[z, dt * step : dt * step + run, i * chunk : (i + 1) * chunk] = sum_ref[
                    i, dt, pl.ds(z, run, stride=nz), :
                ]
    for d, ref in enumerate(sends):
        ref[...] = part_ref[lax.rem(place(nz)[3] + d, nz)].astype(ref.dtype)


def last_kernel(count, *refs):
    parts, (weight_ref, head_ref, loss_ref) = refs[:count], refs[count:]
    total = parts[0][...]
    for ref in parts[1:]:
        total = total + ref[...].astype(F32)
    run, _, block = weight_ref.shape
    step = total.shape[0] // 3
    for dt in range(3):
        for q in range(9):
            weight_ref[:, dt * 9 + q, :] = total[dt * step : dt * step + run, q * block : (q + 1) * block]
    base = 9 * block
    head_ref[...] = total[:run, base : base + head_ref.shape[1]]
    loss = total[step : step + 1, base : base + 1]
    loss = loss + total[step : step + 1, base + 8 : base + 9]
    loss_ref[...] = loss + total[step : step + 1, base + 16 : base + 17]


def body(frames, conv_weight, head_weight, clip_len):
    nf, nrow, ncol, chans = frames.shape
    band = nrow * ncol
    cells = nf * band
    count = lax.axis_size("tm")
    ny = 4 if count == 64 else 2
    nz = count // 2 // ny
    run = chans // count
    chip = 2 * nf
    shape = jax.ShapeDtypeStruct

    def index(yy, zz, cc):
        return ((yy % ny) * nz + zz % nz) * 2 + cc

    every = [(yy, zz, cc) for yy in range(ny) for zz in range(nz) for cc in range(2)]

    def over_core(v):
        return lax.ppermute(v, "tm", [(i, i ^ 1) for i in range(count)])

    def over_chip(v, d):
        return lax.ppermute(v, "tm", [(i, (i + 2 * d) % count) for i in range(count)])

    def over_x(v, d):
        return lax.ppermute(v, "space", [(i, (i + d) % 4) for i in range(4)])

    def over_y(v, d):
        return lax.ppermute(v, "tm", [(index(a, b, e), index(a + d, b, e)) for a, b, e in every])

    def over_z(v, d):
        return lax.ppermute(v, "tm", [(index(a, b, e), index(a, b + d, e)) for a, b, e in every])

    table = half_table(chans, run, ny, nz)
    lanes = table.shape[2]
    table = np.concatenate([table, table[::-1]], axis=2)
    table = jnp.asarray(table, B16)
    flat = frames.reshape(nf, band, chans)
    edge = shape((nf, ncol, chans), B16)
    top, bot = call(first_kernel, [edge, edge], name="first")(flat)
    top, bot = (
        lax.ppermute(bot, "space", [(i, i + 1) for i in range(3)]),
        lax.ppermute(top, "space", [(i + 1, i) for i in range(3)]),
    )
    flat, top, bot = lax.optimization_barrier((flat, top, bot))
    flats = [flat] + [over_x(flat, d) for d in (1, 2, 3)]
    ends, last = call(
        ends_kernel, [shape((2, band + 2 * ncol, chans), B16), shape((1, band, chans), B16)], name="ends"
    )(flat, top, bot)
    ends = lax.ppermute(ends, "tm", [(i, i + 1) for i in range(count - 1)])
    last = lax.ppermute(last, "tm", [(i, i + 2) for i in range(1, count - 2, 2)])

    whole = lambda *dims: pl.BlockSpec(dims, lambda i: (0,) * len(dims))
    zlat = head_weight.shape[1]
    hblock = zlat // 4
    block = chans // 4
    message = shape((32 + block, cells), B16)
    latent, before, *mine_d = call(
        forward_kernel,
        [shape((cells, zlat), F32), shape((1, band, chans), B16)] + [message] * 4,
        [
            pltpu.VMEM((cells, chans), F32),
            pltpu.VMEM(((nf + 2) * band, 9 * chans), B16),
            pltpu.VMEM((chans, cells), B16),
            pltpu.VMEM((nf, zlat, chans), F32),
            pltpu.VMEM((3, 9 * chans, chans), B16),
            pltpu.SemaphoreType.DMA((3,)),
        ],
        grid=(1,),
        in_specs=[smem()]
        + [whole(*v.shape) for v in (flat, ends, last, top, bot)]
        + [pl.BlockSpec(memory_space=pl.ANY), whole(zlat, chans)],
        out_specs=[whole(cells, zlat), whole(1, band, chans)] + [whole(*message.shape)] * 4,
        name="forward",
    )(clip_len, flat, ends, last, top, bot, conv_weight.reshape(3, 9 * chans, chans), head_weight.T)
    mine_d, flats = lax.optimization_barrier((mine_d, flats))
    mine_d = [mine_d[0]] + [over_x(mine_d[d], d) for d in (1, 2, 3)]

    befores = [before] + [over_x(before, d) for d in (1, 2, 3)]
    mine_d = call(relay_kernel, shape((4,) + message.shape, B16), name="relay")(*mine_d)
    core_d = over_core(mine_d)

    corner = pl.BlockSpec((4, 16, 128), lambda i: (0, 0, 0))
    kchip = call(
        clip_kernel,
        shape((chip, 128), F32),
        grid=(1,),
        in_specs=[corner] * 2,
        out_specs=whole(chip, 128),
        name="clip",
    )(mine_d, core_d)
    chosen = shape((5, 4 * band, lanes), B16)
    spec = pl.BlockSpec((1, 4 * band, lanes), lambda i: (i, 0, 0))
    befores, kchip = lax.optimization_barrier((befores, kchip))
    window = [over_chip(kchip, d) for d in (1, -1, 2, -2, 3, -3)]
    window = [window[i] for i in (4, 2, 0)] + [kchip] + [window[i] for i in (1, 3, 5)]
    xown, xoth = call(
        choose_kernel,
        [chosen, chosen],
        [pltpu.VMEM((4 * band, chans), B16)],
        grid=(5,),
        in_specs=[pl.BlockSpec((1, band, chans), lambda i: (jnp.maximum(i - 1, 0), 0, 0))] * 4
        + [whole(1, band, chans)] * 4
        + [whole(*table.shape)],
        out_specs=[spec, spec],
        name="choose",
    )(*flats, *befores, table)
    xoth = over_core(xoth)
    rows = run * nz
    wrow = 9 * block + 32
    sends = call(
        functools.partial(weight_kernel, ny, nz, float(4 * band)),
        [shape((3, rows, wrow), F32)] + [shape((3, rows, wrow), B16)] * (ny - 1),
        [
            pltpu.VMEM((2, 4) + message.shape, B16),
            pltpu.VMEM((2, 9 * block, 4 * band), B16),
            pltpu.VMEM((3, wrow, lanes), F32),
            pltpu.VMEM((lanes, wrow), F32),
            pltpu.VMEM((10, 4 * band, lanes), B16),
            pltpu.VMEM((chip, 128), F32),
            pltpu.VMEM((3, chip, 128), F32),
            pltpu.SemaphoreType.DMA((3, 2)),
        ],
        in_specs=[smem()] + [vmem()] * 7 + [pl.BlockSpec(memory_space=pl.ANY)] * 4 + [vmem()],
        name="weight",
    )(clip_len, *window, mine_d, core_d, xown, xoth, table)
    gets = [sends[0]] + [over_y(sends[d], d) for d in range(1, ny)]
    step = wide(run)
    chunk = 128 if wrow % 128 == 0 else wrow
    parts = call(
        functools.partial(add_kernel, ny, nz, run),
        [shape((3 * step, wrow), F32)] + [shape((3 * step, wrow), B16)] * (nz - 1),
        [pltpu.VMEM((wrow // chunk, 3, rows, chunk), F32), pltpu.VMEM((nz, 3 * step, wrow), F32)],
        name="add",
    )(*gets)
    parts = [parts[0]] + [over_z(parts[d], d) for d in range(1, nz)]
    weight_grad, head_grad, loss = call(
        functools.partial(last_kernel, nz),
        [shape((run, 27, block), F32), shape((run, hblock), F32), shape((1, 1), F32)],
        name="last",
    )(*parts)
    return latent.reshape(nf, nrow, ncol, zlat), loss[0, 0], weight_grad.transpose(1, 0, 2), head_grad


def solution(mesh):
    in_specs = (P("tm", "space", None, None), P(), P(), P())
    out_specs = (P("tm", "space", None, None), P(), P(None, "tm", "space"), P("tm", "space"))
    return jax.shard_map(body, mesh=mesh, in_specs=in_specs, out_specs=out_specs, check_vma=False)
```

```python
import functools

import jax
import jax.numpy as jnp
import numpy as np
from jax import lax
from jax.experimental import pallas as pl
from jax.experimental.pallas import tpu as pltpu
from jax.sharding import PartitionSpec as P

F32 = jnp.float32
B16 = jnp.bfloat16
COLS = 24
LIMIT = 56 * 1024 * 1024
NT = (((1,), (1,)), ((), ()))
TN = (((0,), (0,)), ((), ()))


def dot(a, b, dims=None):
    if dims is None:
        return jnp.dot(a, b, preferred_element_type=F32)
    return lax.dot_general(a, b, dims, preferred_element_type=F32)


def call(kernel, outs, scratch=(), **kw):
    params = pltpu.CompilerParams(vmem_limit_bytes=LIMIT)
    return pl.pallas_call(kernel, out_shape=outs, scratch_shapes=list(scratch), compiler_params=params, **kw)


def smem():
    return pl.BlockSpec(memory_space=pltpu.SMEM)


def vmem():
    return pl.BlockSpec(memory_space=pltpu.VMEM)


def place(nz):
    t = lax.axis_index("tm")
    k = lax.div(t, 2)
    return lax.rem(t, 2), lax.axis_index("space"), lax.div(k, nz), lax.rem(k, nz), k


def half_table(chans, run, ny, nz):
    lane = np.arange(chans // 2)
    block = wide(run) * nz
    spot = (lane // run // nz) * block + (lane % run) * nz + lane // run % nz
    table = np.zeros((2, chans, ny * block), np.float32)
    for core in range(2):
        table[core, (lane // run) * 2 * run + core * run + lane % run, spot] = 1
    return table


def wide(run):
    return -(-run // 8) * 8


def first_kernel(x_ref, top_ref, bot_ref):
    nf, band, chans = x_ref.shape
    for f in range(nf):
        wide_frame = x_ref[f].astype(F32)
        top_ref[f] = wide_frame[:COLS].astype(B16)
        bot_ref[f] = wide_frame[band - COLS :].astype(B16)


def frame_of(top, mid, bot):
    return jnp.concatenate([top.astype(F32), mid.astype(F32), bot.astype(F32)], axis=0)


def ends_kernel(x_ref, top_ref, bot_ref, ends_ref):
    nf = x_ref.shape[0]
    for f in range(2):
        g = nf - 2 + f
        ends_ref[f] = frame_of(top_ref[g], x_ref[g], bot_ref[g]).astype(B16)


def choose_kernel(f0, f1, f2, f3, table_ref, own_ref, oth_ref, wide_ref):
    c, x = lax.rem(lax.axis_index("tm"), 2), lax.axis_index("space")
    band = f0.shape[1]

    for d, ref in enumerate((f0, f1, f2, f3)):
        wide_ref[pl.ds(pl.multiple_of(lax.rem(x - d + 4, 4) * band, band), band)] = ref[0]
    both = dot(wide_ref[...], table_ref[c]).astype(B16)
    lanes = own_ref.shape[2]
    own_ref[0] = both[:, :lanes]
    oth_ref[0] = both[:, lanes:]


def forward_kernel(len_ref, x_ref, ends_ref, top_ref, bot_ref, w_ref, hw_ref,
                   lat_ref, d0, d1, d2, d3, pre_ref, wide_ref, turned_ref, head_ref, held_ref, sem):
    nf, band, chans = x_ref.shape
    rows = band + 2 * COLS
    loads = [pltpu.make_async_copy(w_ref.at[dt], held_ref.at[dt], sem.at[dt]) for dt in range(3)]
    for load in loads:
        load.start()
    col = lax.rem(lax.broadcasted_iota(jnp.int32, (rows, 1), 0), COLS)
    for f in range(nf + 2):
        if f < 2:
            v = ends_ref[f].astype(F32)
        else:
            v = frame_of(top_ref[f - 2], x_ref[f - 2], bot_ref[f - 2])
        for dw in range(3):
            if dw == 0:
                s = jnp.where(col > 0, pltpu.roll(v, 1, 0), 0.0)
            elif dw == 2:
                s = jnp.where(col < COLS - 1, pltpu.roll(v, rows - 1, 0), 0.0)
            else:
                s = v
            for dh in range(3):
                q = dh * 3 + dw
                wide_ref[f * band : (f + 1) * band, q * chans : (q + 1) * chans] = s[
                    dh * COLS : dh * COLS + band
                ].astype(B16)

    t, xs = lax.axis_index("tm"), lax.axis_index("space")
    pos = [jnp.int32(0)] * nf
    start = jnp.int32(0)
    for j in range(len_ref.shape[0]):
        for f in range(nf):
            pos[f] = jnp.where(t * nf + f >= start, t * nf + f - start, pos[f])
        start = start + len_ref[j]
    for dt in range(3):
        loads[dt].wait()
        part = dot(wide_ref[dt * band : (dt + nf) * band, :], held_ref[dt])
        for f in range(nf):
            keep = jnp.where(pos[f] >= 2 - dt, 1.0, 0.0)
            piece = keep * part[f * band : (f + 1) * band]
            if dt == 0:
                pre_ref[f * band : (f + 1) * band] = piece
            else:
                pre_ref[f * band : (f + 1) * band] += piece

    zdim = lat_ref.shape[1] // 2
    row = lax.broadcasted_iota(jnp.int32, (16, 128), 0)
    kf = jnp.zeros((16, 128), F32)
    for f in range(nf):
        at = slice(f * band, (f + 1) * band)
        pre = pre_ref[at]
        sig = 1.0 / (1.0 + jnp.exp(-pre))
        act = (pre * sig).astype(B16)
        lat = dot(act, hw_ref[...], NT)
        lat_ref[at] = lat
        lane = lax.broadcasted_iota(jnp.int32, lat.shape, 1)
        grow = jnp.exp(lat) - 1.0
        term = jnp.where(lane < zdim, lat * lat, grow - lat)
        kf = jnp.where(lax.rem(row, nf) == f, 0.5 * jnp.sum(term), kf)
        dlat = jnp.where(lane < zdim, lat, 0.5 * grow).astype(B16)
        dact = dot(dlat, hw_ref[...])
        pre_ref[at] = (dact * sig * (1.0 + pre * (1.0 - sig))).astype(B16).astype(F32)
        head_ref[f] = dot(dlat, act, TN)
    high = kf.astype(B16).astype(F32)
    mid = (kf - high).astype(B16).astype(F32)
    kf = jnp.where(row < nf, high, jnp.where(row < 2 * nf, mid, jnp.where(row < 3 * nf, kf - high - mid, 0.0)))
    turned_ref[...] = jnp.transpose(pre_ref[...], (1, 0)).astype(B16)
    block = chans // 4
    hblock = 2 * zdim // 4
    for d, ref in enumerate((d0, d1, d2, d3)):
        to = lax.rem(xs + d, 4)
        ref[:16, :128] = kf.astype(B16)
        ref[:16, 128:] = jnp.zeros((16, ref.shape[1] - 128), B16)
        ref[32:] = turned_ref[pl.ds(pl.multiple_of(to * block, block), block), :]
        heads = [head_ref[f, pl.ds(pl.multiple_of(to * hblock, hblock), hblock), :] for f in range(nf)]
        pad = ref.shape[1] - 2 * chans
        if pad:
            heads = [jnp.concatenate([h, jnp.zeros((hblock, pad // 2), F32)], axis=1) for h in heads]
        both = jnp.concatenate(
            [jnp.concatenate(heads[:2], axis=1), jnp.concatenate(heads[2:], axis=1)], axis=0
        )
        ref[16:32] = both.astype(B16)


def clip_kernel(*refs):
    c, x = lax.rem(lax.axis_index("tm"), 2), lax.axis_index("space")
    given, (sums_ref, tail_ref) = (refs[:4], refs[4:8]), refs[8:]
    sums = []
    for four in given:
        v = four[0][:16, :128].astype(F32)
        for ref in four[1:]:
            v = v + ref[:16, :128].astype(F32)
        sums.append(v[:4] + v[4:8] + v[8:12])
    for core in range(2):

        @pl.when(c == core)
        def _():
            sums_ref[...] = jnp.concatenate([sums[core], sums[1 - core]], axis=0)
            for d in range(4):
                tail_ref[lax.rem(x - d + 4, 4)] = given[core][d][32:, :]


def weight_kernel(ny, nz, per_frame, len_ref, left_ref, mid_ref, right_ref, next_ref, a0, a1, a2, a3, b0, b1, b2, b3,
                  x_ref, xo_ref, table_ref, *refs):
    sends, (held_ref, taps_ref, acc_ref, out_ref, xs_ref, g_ref, keep_ref, sem) = refs[:ny], refs[ny:]
    c, x, y, _, k = place(nz)
    copies = []
    for core, given, s in ((c, (a0, a1, a2, a3), 0), (1 - c, (b0, b1, b2, b3), 1)):
        for d, ref in enumerate(given):
            copies.append(pltpu.make_async_copy(ref, held_ref.at[core, lax.rem(x - d + 4, 4)], sem.at[s, d]))
    for core, ref, s in ((c, x_ref, 0), (1 - c, xo_ref, 1)):
        copies.append(pltpu.make_async_copy(ref, xs_ref.at[pl.ds(4 * core, 4)], sem.at[2, s]))
    for copy in copies:
        copy.start()
    full = x_ref.shape[1]
    band = full // 4
    block = taps_ref.shape[1] // 9
    chans = table_ref.shape[1]
    lanes = acc_ref.shape[2]
    hblock = 8
    half = full // 2
    window = jnp.concatenate(
        [left_ref[0], left_ref[1], left_ref[2], mid_ref[...], right_ref[0], right_ref[1], right_ref[2]], axis=0
    )
    chip = mid_ref.shape[0]
    wids = chip * (k - 3) + lax.broadcasted_iota(jnp.int32, window.shape, 0)
    ids = chip * k + lax.broadcasted_iota(jnp.int32, g_ref.shape, 0)
    total = jnp.zeros(g_ref.shape, F32)
    lens = jnp.ones(g_ref.shape, F32)
    pos = jnp.full(g_ref.shape, -1, jnp.int32)
    start = jnp.int32(0)
    for j in range(len_ref.shape[0]):
        size = len_ref[j]
        inside = jnp.where((wids >= start) & (wids < start + size), window, 0.0)
        mine = (ids >= start) & (ids < start + size)
        total = jnp.where(mine, jnp.sum(inside, axis=0, keepdims=True), total)
        lens = jnp.where(mine, size.astype(F32), lens)
        pos = jnp.where(mine, ids - start, pos)
        start = start + size
    gain = lens / (lens * per_frame + total)
    g_ref[...] = gain
    for dt in range(3):
        keep_ref[dt] = jnp.where(pos >= 2 - dt, gain, 0.0)
    row = lax.broadcasted_iota(jnp.int32, g_ref.shape, 0)
    loss = jnp.where((pos == 0) & (row < chip), lens * jnp.log1p(total / (lens * per_frame)), 0.0)
    loss = jnp.sum(loss, axis=0, keepdims=True)
    hsum = jnp.zeros((hblock, chans), F32)
    for copy in copies[:8]:
        copy.wait()
    for core in range(2):
        for xs in range(4):
            tail = held_ref[core, xs, 16:32, :].astype(F32)
            for f in range(4):
                part = tail[(f // 2) * hblock : (f // 2 + 1) * hblock, (f % 2) * half : (f % 2) * half + chans]
                hsum = hsum + g_ref[core * 4 + f : core * 4 + f + 1, :1] * part
    acc_ref[...] = jnp.zeros(acc_ref.shape, F32)
    lane = lax.broadcasted_iota(jnp.int32, (1, full), 1)
    col = lax.rem(lane, COLS)
    line = lane // COLS

    def build(f):
        core, lf = f // 4 % 2, f % 4
        frame = jnp.zeros((block, full), F32)
        for xs in range(4):
            if f < 8:
                v = held_ref[core, xs, 32:, :].astype(F32)
            else:
                v = next_ref[xs].astype(F32)
                v = jnp.concatenate([v, jnp.zeros_like(v)], axis=1)
            shift = ((xs - lf) * band) % full
            if shift:
                v = pltpu.roll(v, shift, 1)
            frame = jnp.where(lane // band == xs, v, frame)
        for dw in range(3):
            if dw == 0:
                v = jnp.where(col < COLS - 1, pltpu.roll(frame, full - 1, 1), 0.0)
            elif dw == 2:
                v = jnp.where(col > 0, pltpu.roll(frame, 1, 1), 0.0)
            else:
                v = frame
            for dh in range(3):
                if dh == 0:
                    s = jnp.where(line < full // COLS - 1, pltpu.roll(v, full - COLS, 1), 0.0)
                elif dh == 2:
                    s = jnp.where(line > 0, pltpu.roll(v, COLS, 1), 0.0)
                else:
                    s = v
                q = dh * 3 + dw
                taps_ref[f % 2, q * block : (q + 1) * block, :] = s.astype(B16)

    build(0)
    for copy in copies[8:]:
        copy.wait()
    for f in range(10):
        if f < 9:
            build(f + 1)
        for dt in range(3):
            if 0 <= f - 2 + dt < 8:
                scale = keep_ref[dt, f : f + 1, :1]
                acc_ref[dt, : 9 * block] += scale * dot(taps_ref[f % 2], xs_ref[f - 2 + dt])
    direct = table_ref[c, :, :lanes]
    high = hsum.astype(B16)
    low = (hsum - high.astype(F32)).astype(B16)
    acc_ref[0, 9 * block : 9 * block + hblock] = dot(high, direct) + dot(low, direct)
    loss = jnp.broadcast_to(loss[:, :1], (8, lanes))
    top = loss.astype(B16).astype(F32)
    mid = (loss - top).astype(B16).astype(F32)
    acc_ref[1, 9 * block : 9 * block + 8] = top
    acc_ref[1, 9 * block + 8 : 9 * block + 16] = mid
    acc_ref[1, 9 * block + 16 : 9 * block + 24] = loss - top - mid
    rows = sends[0].shape[1]
    ystep = lanes // ny
    for dt in range(3):
        out_ref[...] = jnp.transpose(acc_ref[dt], (1, 0))
        for d, ref in enumerate(sends):
            to = lax.rem(y + d, ny)
            ref[dt] = out_ref[pl.ds(pl.multiple_of(to * ystep, 8), rows), :].astype(ref.dtype)


def add_kernel(ny, nz, run, *refs):
    gets, sends, (sum_ref, part_ref) = refs[:ny], refs[ny : ny + nz], refs[ny + nz :]
    total = gets[0][...]
    for ref in gets[1:]:
        total = total + ref[...].astype(F32)
    chunk = sum_ref.shape[3]
    for i in range(sum_ref.shape[0]):
        sum_ref[i] = total[:, :, i * chunk : (i + 1) * chunk]
    part_ref[...] = jnp.zeros(part_ref.shape, F32)
    step = part_ref.shape[1] // 3
    for z in range(nz):
        for dt in range(3):
            for i in range(sum_ref.shape[0]):
                part_ref[z, dt * step : dt * step + run, i * chunk : (i + 1) * chunk] = sum_ref[
                    i, dt, pl.ds(z, run, stride=nz), :
                ]
    for d, ref in enumerate(sends):
        ref[...] = part_ref[lax.rem(place(nz)[3] + d, nz)].astype(ref.dtype)


def last_kernel(count, *refs):
    parts, (weight_ref, head_ref, loss_ref) = refs[:count], refs[count:]
    total = parts[0][...]
    for ref in parts[1:]:
        total = total + ref[...].astype(F32)
    run, _, block = weight_ref.shape
    step = total.shape[0] // 3
    for dt in range(3):
        for q in range(9):
            weight_ref[:, dt * 9 + q, :] = total[dt * step : dt * step + run, q * block : (q + 1) * block]
    base = 9 * block
    head_ref[...] = total[:run, base : base + head_ref.shape[1]]
    loss = total[step : step + 1, base : base + 1]
    loss = loss + total[step : step + 1, base + 8 : base + 9]
    loss_ref[...] = loss + total[step : step + 1, base + 16 : base + 17]


def body(frames, conv_weight, head_weight, clip_len):
    nf, nrow, ncol, chans = frames.shape
    band = nrow * ncol
    cells = nf * band
    count = lax.axis_size("tm")
    ny = 4 if count == 64 else 2
    nz = count // 2 // ny
    run = chans // count
    chip = 2 * nf
    shape = jax.ShapeDtypeStruct

    def index(yy, zz, cc):
        return ((yy % ny) * nz + zz % nz) * 2 + cc

    every = [(yy, zz, cc) for yy in range(ny) for zz in range(nz) for cc in range(2)]

    def over_core(v):
        return lax.ppermute(v, "tm", [(i, i ^ 1) for i in range(count)])

    def over_chip(v, d):
        return lax.ppermute(v, "tm", [(i, (i + 2 * d) % count) for i in range(count)])

    def over_x(v, d):
        return lax.ppermute(v, "space", [(i, (i + d) % 4) for i in range(4)])

    def over_y(v, d):
        return lax.ppermute(v, "tm", [(index(a, b, e), index(a + d, b, e)) for a, b, e in every])

    def over_z(v, d):
        return lax.ppermute(v, "tm", [(index(a, b, e), index(a, b + d, e)) for a, b, e in every])

    table = half_table(chans, run, ny, nz)
    lanes = table.shape[2]
    table = np.concatenate([table, table[::-1]], axis=2)
    table = jnp.asarray(table, B16)
    flat = frames.reshape(nf, band, chans)
    edge = shape((nf, ncol, chans), B16)
    top, bot = call(first_kernel, [edge, edge], name="first")(flat)
    top, bot = (
        lax.ppermute(bot, "space", [(i, i + 1) for i in range(3)]),
        lax.ppermute(top, "space", [(i + 1, i) for i in range(3)]),
    )
    flat, top, bot = lax.optimization_barrier((flat, top, bot))
    flats = [flat] + [over_x(flat, d) for d in (1, 2, 3)]
    ends = call(ends_kernel, shape((2, band + 2 * ncol, chans), B16), name="ends")(flat, top, bot)
    ends = lax.ppermute(ends, "tm", [(i, i + 1) for i in range(count - 1)])

    whole = lambda *dims: pl.BlockSpec(dims, lambda i: (0,) * len(dims))
    zlat = head_weight.shape[1]
    hblock = zlat // 4
    block = chans // 4
    message = shape((32 + block, cells), B16)
    latent, *mine_d = call(
        forward_kernel,
        [shape((cells, zlat), F32)] + [message] * 4,
        [
            pltpu.VMEM((cells, chans), F32),
            pltpu.VMEM(((nf + 2) * band, 9 * chans), B16),
            pltpu.VMEM((chans, cells), B16),
            pltpu.VMEM((nf, zlat, chans), F32),
            pltpu.VMEM((3, 9 * chans, chans), B16),
            pltpu.SemaphoreType.DMA((3,)),
        ],
        grid=(1,),
        in_specs=[smem()]
        + [whole(*v.shape) for v in (flat, ends, top, bot)]
        + [pl.BlockSpec(memory_space=pl.ANY), whole(zlat, chans)],
        out_specs=[whole(cells, zlat)] + [whole(*message.shape)] * 4,
        name="forward",
    )(clip_len, flat, ends, top, bot, conv_weight.reshape(3, 9 * chans, chans), head_weight.T)
    mine_d, flats = lax.optimization_barrier((mine_d, flats))
    mine_d = [mine_d[0]] + [over_x(mine_d[d], d) for d in (1, 2, 3)]
    chosen = shape((4, 4 * band, lanes), B16)
    spec = pl.BlockSpec((1, 4 * band, lanes), lambda i: (i, 0, 0))
    xown, xoth = call(
        choose_kernel,
        [chosen, chosen],
        [pltpu.VMEM((4 * band, chans), B16)],
        grid=(4,),
        in_specs=[pl.BlockSpec((1, band, chans), lambda i: (i, 0, 0))] * 4 + [whole(*table.shape)],
        out_specs=[spec, spec],
        name="choose",
    )(*flats, table)
    mine_d, xoth = lax.optimization_barrier((mine_d, xoth))
    core_d = [over_core(v) for v in mine_d]
    xoth = over_core(xoth)

    front = pl.BlockSpec((message.shape[0], 2 * band), lambda i: (0, 0))
    kchip, tail = call(
        clip_kernel,
        [shape((chip, 128), F32), shape((4, block, 2 * band), B16)],
        grid=(1,),
        in_specs=[front] * 8,
        out_specs=[whole(chip, 128), whole(4, block, 2 * band)],
        name="clip",
    )(*mine_d, *core_d)
    tail = over_chip(tail, -1)
    triple = jnp.stack([over_chip(kchip, 1), kchip, over_chip(kchip, -1)])
    left, right = over_chip(triple, 2), over_chip(triple, -2)

    rows = run * nz
    wrow = 9 * block + 32
    sends = call(
        functools.partial(weight_kernel, ny, nz, float(4 * band)),
        [shape((3, rows, wrow), F32)] + [shape((3, rows, wrow), B16)] * (ny - 1),
        [
            pltpu.VMEM((2, 4) + message.shape, B16),
            pltpu.VMEM((2, 9 * block, 4 * band), B16),
            pltpu.VMEM((3, wrow, lanes), F32),
            pltpu.VMEM((lanes, wrow), F32),
            pltpu.VMEM((8, 4 * band, lanes), B16),
            pltpu.VMEM((2 * chip, 128), F32),
            pltpu.VMEM((3, 2 * chip, 128), F32),
            pltpu.SemaphoreType.DMA((3, 4)),
        ],
        in_specs=[smem()] + [vmem()] * 4 + [pl.BlockSpec(memory_space=pl.ANY)] * 10 + [vmem()],
        name="weight",
    )(clip_len, left, kchip, right, tail, *mine_d, *core_d, xown, xoth, table)
    gets = [sends[0]] + [over_y(sends[d], d) for d in range(1, ny)]
    step = wide(run)
    chunk = 128 if wrow % 128 == 0 else wrow
    parts = call(
        functools.partial(add_kernel, ny, nz, run),
        [shape((3 * step, wrow), F32)] + [shape((3 * step, wrow), B16)] * (nz - 1),
        [pltpu.VMEM((wrow // chunk, 3, rows, chunk), F32), pltpu.VMEM((nz, 3 * step, wrow), F32)],
        name="add",
    )(*gets)
    parts = [parts[0]] + [over_z(parts[d], d) for d in range(1, nz)]
    weight_grad, head_grad, loss = call(
        functools.partial(last_kernel, nz),
        [shape((run, 27, block), F32), shape((run, hblock), F32), shape((1, 1), F32)],
        name="last",
    )(*parts)
    return latent.reshape(nf, nrow, ncol, zlat), loss[0, 0], weight_grad.transpose(1, 0, 2), head_grad


def solution(mesh):
    in_specs = (P("tm", "space", None, None), P(), P(), P())
    out_specs = (P("tm", "space", None, None), P(), P(None, "tm", "space"), P("tm", "space"))
    return jax.shard_map(body, mesh=mesh, in_specs=in_specs, out_specs=out_specs, check_vma=False)
```

```python
import functools

import jax
import jax.numpy as jnp
import numpy as np
from jax import lax
from jax.experimental import pallas as pl
from jax.experimental.pallas import tpu as pltpu
from jax.sharding import PartitionSpec as P

F32 = jnp.float32
B16 = jnp.bfloat16
COLS = 24
LIMIT = 56 * 1024 * 1024
NT = (((1,), (1,)), ((), ()))
TN = (((0,), (0,)), ((), ()))


def dot(a, b, dims=None):
    if dims is None:
        return jnp.dot(a, b, preferred_element_type=F32)
    return lax.dot_general(a, b, dims, preferred_element_type=F32)


def call(kernel, outs, scratch=(), **kw):
    params = pltpu.CompilerParams(vmem_limit_bytes=LIMIT)
    return pl.pallas_call(kernel, out_shape=outs, scratch_shapes=list(scratch), compiler_params=params, **kw)


def smem():
    return pl.BlockSpec(memory_space=pltpu.SMEM)


def vmem():
    return pl.BlockSpec(memory_space=pltpu.VMEM)


def place(nz):
    t = lax.axis_index("tm")
    k = lax.div(t, 2)
    return lax.rem(t, 2), lax.axis_index("space"), lax.div(k, nz), lax.rem(k, nz), k


def half_table(chans, run, ny, nz):
    lane = np.arange(chans // 2)
    block = wide(run) * nz
    spot = (lane // run // nz) * block + (lane % run) * nz + lane // run % nz
    table = np.zeros((2, chans, ny * block), np.float32)
    for core in range(2):
        table[core, (lane // run) * 2 * run + core * run + lane % run, spot] = 1
    return table


def wide(run):
    return -(-run // 8) * 8


def first_kernel(x_ref, top_ref, bot_ref):
    nf, band, chans = x_ref.shape
    for f in range(nf):
        wide_frame = x_ref[f].astype(F32)
        top_ref[f] = wide_frame[:COLS].astype(B16)
        bot_ref[f] = wide_frame[band - COLS :].astype(B16)


def frame_of(top, mid, bot):
    return jnp.concatenate([top.astype(F32), mid.astype(F32), bot.astype(F32)], axis=0)


def ends_kernel(x_ref, top_ref, bot_ref, ends_ref):
    nf = x_ref.shape[0]
    for f in range(2):
        g = nf - 2 + f
        ends_ref[f] = frame_of(top_ref[g], x_ref[g], bot_ref[g]).astype(B16)


def choose_kernel(f0, f1, f2, f3, table_ref, own_ref, oth_ref, wide_ref):
    c, x = lax.rem(lax.axis_index("tm"), 2), lax.axis_index("space")
    band = f0.shape[1]

    for d, ref in enumerate((f0, f1, f2, f3)):
        wide_ref[pl.ds(pl.multiple_of(lax.rem(x - d + 4, 4) * band, band), band)] = ref[0]
    both = dot(wide_ref[...], table_ref[c]).astype(B16)
    lanes = own_ref.shape[2]
    own_ref[0] = both[:, :lanes]
    oth_ref[0] = both[:, lanes:]


def forward_kernel(len_ref, x_ref, ends_ref, top_ref, bot_ref, w_ref, hw_ref,
                   lat_ref, d0, d1, d2, d3, pre_ref, wide_ref, turned_ref, head_ref, held_ref, sem):
    nf, band, chans = x_ref.shape
    rows = band + 2 * COLS
    loads = [pltpu.make_async_copy(w_ref.at[dt], held_ref.at[dt], sem.at[dt]) for dt in range(3)]
    for load in loads:
        load.start()
    col = lax.rem(lax.broadcasted_iota(jnp.int32, (rows, 1), 0), COLS)
    for f in range(nf + 2):
        if f < 2:
            v = ends_ref[f].astype(F32)
        else:
            v = frame_of(top_ref[f - 2], x_ref[f - 2], bot_ref[f - 2])
        for dw in range(3):
            if dw == 0:
                s = jnp.where(col > 0, pltpu.roll(v, 1, 0), 0.0)
            elif dw == 2:
                s = jnp.where(col < COLS - 1, pltpu.roll(v, rows - 1, 0), 0.0)
            else:
                s = v
            for dh in range(3):
                q = dh * 3 + dw
                wide_ref[f * band : (f + 1) * band, q * chans : (q + 1) * chans] = s[
                    dh * COLS : dh * COLS + band
                ].astype(B16)

    t, xs = lax.axis_index("tm"), lax.axis_index("space")
    pos = [jnp.int32(0)] * nf
    start = jnp.int32(0)
    for j in range(len_ref.shape[0]):
        for f in range(nf):
            pos[f] = jnp.where(t * nf + f >= start, t * nf + f - start, pos[f])
        start = start + len_ref[j]
    for dt in range(3):
        loads[dt].wait()
        part = dot(wide_ref[dt * band : (dt + nf) * band, :], held_ref[dt])
        for f in range(nf):
            keep = jnp.where(pos[f] >= 2 - dt, 1.0, 0.0)
            piece = keep * part[f * band : (f + 1) * band]
            if dt == 0:
                pre_ref[f * band : (f + 1) * band] = piece
            else:
                pre_ref[f * band : (f + 1) * band] += piece

    zdim = lat_ref.shape[1] // 2
    row = lax.broadcasted_iota(jnp.int32, (16, 128), 0)
    kf = jnp.zeros((16, 128), F32)
    for f in range(nf):
        at = slice(f * band, (f + 1) * band)
        pre = pre_ref[at]
        sig = 1.0 / (1.0 + jnp.exp(-pre))
        act = (pre * sig).astype(B16)
        lat = dot(act, hw_ref[...], NT)
        lat_ref[at] = lat
        lane = lax.broadcasted_iota(jnp.int32, lat.shape, 1)
        grow = jnp.exp(lat) - 1.0
        term = jnp.where(lane < zdim, lat * lat, grow - lat)
        kf = jnp.where(lax.rem(row, nf) == f, 0.5 * jnp.sum(term), kf)
        dlat = jnp.where(lane < zdim, lat, 0.5 * grow).astype(B16)
        dact = dot(dlat, hw_ref[...])
        pre_ref[at] = (dact * sig * (1.0 + pre * (1.0 - sig))).astype(B16).astype(F32)
        head_ref[f] = dot(dlat, act, TN)
    high = kf.astype(B16).astype(F32)
    mid = (kf - high).astype(B16).astype(F32)
    kf = jnp.where(row < nf, high, jnp.where(row < 2 * nf, mid, jnp.where(row < 3 * nf, kf - high - mid, 0.0)))
    turned_ref[...] = jnp.transpose(pre_ref[...], (1, 0)).astype(B16)
    block = chans // 4
    hblock = 2 * zdim // 4
    for d, ref in enumerate((d0, d1, d2, d3)):
        to = lax.rem(xs + d, 4)
        ref[:16, :128] = kf.astype(B16)
        ref[:16, 128:] = jnp.zeros((16, ref.shape[1] - 128), B16)
        ref[32:] = turned_ref[pl.ds(pl.multiple_of(to * block, block), block), :]
        heads = [head_ref[f, pl.ds(pl.multiple_of(to * hblock, hblock), hblock), :] for f in range(nf)]
        pad = ref.shape[1] - 2 * chans
        if pad:
            heads = [jnp.concatenate([h, jnp.zeros((hblock, pad // 2), F32)], axis=1) for h in heads]
        both = jnp.concatenate(
            [jnp.concatenate(heads[:2], axis=1), jnp.concatenate(heads[2:], axis=1)], axis=0
        )
        ref[16:32] = both.astype(B16)


def clip_kernel(*refs):
    c, x = lax.rem(lax.axis_index("tm"), 2), lax.axis_index("space")
    given, (sums_ref, tail_ref) = (refs[:4], refs[4:8]), refs[8:]
    sums = []
    for four in given:
        v = four[0][:16, :128].astype(F32)
        for ref in four[1:]:
            v = v + ref[:16, :128].astype(F32)
        sums.append(v[:4] + v[4:8] + v[8:12])
    for core in range(2):

        @pl.when(c == core)
        def _():
            sums_ref[...] = jnp.concatenate([sums[core], sums[1 - core]], axis=0)
            for d in range(4):
                tail_ref[lax.rem(x - d + 4, 4)] = given[core][d][32:, :]


def weight_kernel(ny, nz, per_frame, len_ref, left_ref, mid_ref, right_ref, next_ref, a0, a1, a2, a3, b0, b1, b2, b3,
                  x_ref, xo_ref, table_ref, *refs):
    sends, (held_ref, taps_ref, acc_ref, out_ref, xs_ref, g_ref, keep_ref, sem) = refs[:ny], refs[ny:]
    c, x, y, _, k = place(nz)
    copies = []
    for core, given, s in ((c, (a0, a1, a2, a3), 0), (1 - c, (b0, b1, b2, b3), 1)):
        for d, ref in enumerate(given):
            copies.append(pltpu.make_async_copy(ref, held_ref.at[core, lax.rem(x - d + 4, 4)], sem.at[s, d]))
    for core, ref, s in ((c, x_ref, 0), (1 - c, xo_ref, 1)):
        copies.append(pltpu.make_async_copy(ref, xs_ref.at[pl.ds(4 * core, 4)], sem.at[2, s]))
    for copy in copies:
        copy.start()
    full = x_ref.shape[1]
    band = full // 4
    block = taps_ref.shape[1] // 9
    chans = table_ref.shape[1]
    lanes = acc_ref.shape[2]
    hblock = 8
    half = full // 2
    window = jnp.concatenate(
        [left_ref[0], left_ref[1], left_ref[2], mid_ref[...], right_ref[0], right_ref[1], right_ref[2]], axis=0
    )
    chip = mid_ref.shape[0]
    wids = chip * (k - 3) + lax.broadcasted_iota(jnp.int32, window.shape, 0)
    ids = chip * k + lax.broadcasted_iota(jnp.int32, g_ref.shape, 0)
    total = jnp.zeros(g_ref.shape, F32)
    lens = jnp.ones(g_ref.shape, F32)
    pos = jnp.full(g_ref.shape, -1, jnp.int32)
    start = jnp.int32(0)
    for j in range(len_ref.shape[0]):
        size = len_ref[j]
        inside = jnp.where((wids >= start) & (wids < start + size), window, 0.0)
        mine = (ids >= start) & (ids < start + size)
        total = jnp.where(mine, jnp.sum(inside, axis=0, keepdims=True), total)
        lens = jnp.where(mine, size.astype(F32), lens)
        pos = jnp.where(mine, ids - start, pos)
        start = start + size
    gain = lens / (lens * per_frame + total)
    g_ref[...] = gain
    for dt in range(3):
        keep_ref[dt] = jnp.where(pos >= 2 - dt, gain, 0.0)
    row = lax.broadcasted_iota(jnp.int32, g_ref.shape, 0)
    loss = jnp.where((pos == 0) & (row < chip), lens * jnp.log1p(total / (lens * per_frame)), 0.0)
    loss = jnp.sum(loss, axis=0, keepdims=True)
    hsum = jnp.zeros((hblock, chans), F32)
    for copy in copies[:8]:
        copy.wait()
    for core in range(2):
        for xs in range(4):
            tail = held_ref[core, xs, 16:32, :].astype(F32)
            for f in range(4):
                part = tail[(f // 2) * hblock : (f // 2 + 1) * hblock, (f % 2) * half : (f % 2) * half + chans]
                hsum = hsum + g_ref[core * 4 + f : core * 4 + f + 1, :1] * part
    acc_ref[...] = jnp.zeros(acc_ref.shape, F32)
    lane = lax.broadcasted_iota(jnp.int32, (1, full), 1)
    col = lax.rem(lane, COLS)
    line = lane // COLS

    def build(f):
        core, lf = f // 4 % 2, f % 4
        frame = jnp.zeros((block, full), F32)
        for xs in range(4):
            if f < 8:
                v = held_ref[core, xs, 32:, :].astype(F32)
            else:
                v = next_ref[xs].astype(F32)
                v = jnp.concatenate([v, jnp.zeros_like(v)], axis=1)
            shift = ((xs - lf) * band) % full
            if shift:
                v = pltpu.roll(v, shift, 1)
            frame = jnp.where(lane // band == xs, v, frame)
        for dw in range(3):
            if dw == 0:
                v = jnp.where(col < COLS - 1, pltpu.roll(frame, full - 1, 1), 0.0)
            elif dw == 2:
                v = jnp.where(col > 0, pltpu.roll(frame, 1, 1), 0.0)
            else:
                v = frame
            for dh in range(3):
                if dh == 0:
                    s = jnp.where(line < full // COLS - 1, pltpu.roll(v, full - COLS, 1), 0.0)
                elif dh == 2:
                    s = jnp.where(line > 0, pltpu.roll(v, COLS, 1), 0.0)
                else:
                    s = v
                q = dh * 3 + dw
                taps_ref[f % 2, q * block : (q + 1) * block, :] = s.astype(B16)

    build(0)
    for copy in copies[8:]:
        copy.wait()
    for f in range(10):
        if f < 9:
            build(f + 1)
        for dt in range(3):
            if 0 <= f - 2 + dt < 8:
                scale = keep_ref[dt, f : f + 1, :1]
                acc_ref[dt, : 9 * block] += scale * dot(taps_ref[f % 2], xs_ref[f - 2 + dt])
    direct = table_ref[c, :, :lanes]
    high = hsum.astype(B16)
    low = (hsum - high.astype(F32)).astype(B16)
    acc_ref[0, 9 * block : 9 * block + hblock] = dot(high, direct) + dot(low, direct)
    loss = jnp.broadcast_to(loss[:, :1], (8, lanes))
    top = loss.astype(B16).astype(F32)
    mid = (loss - top).astype(B16).astype(F32)
    acc_ref[1, 9 * block : 9 * block + 8] = top
    acc_ref[1, 9 * block + 8 : 9 * block + 16] = mid
    acc_ref[1, 9 * block + 16 : 9 * block + 24] = loss - top - mid
    rows = sends[0].shape[1]
    ystep = lanes // ny
    for dt in range(3):
        out_ref[...] = jnp.transpose(acc_ref[dt], (1, 0))
        for d, ref in enumerate(sends):
            to = lax.rem(y + d, ny)
            ref[dt] = out_ref[pl.ds(pl.multiple_of(to * ystep, 8), rows), :].astype(ref.dtype)


def add_kernel(ny, nz, run, *refs):
    gets, (keep_ref, send_ref, sum_ref, part_ref) = refs[:ny], refs[ny:]
    total = gets[0][...]
    for ref in gets[1:]:
        total = total + ref[...].astype(F32)
    chunk = sum_ref.shape[3]
    for i in range(sum_ref.shape[0]):
        sum_ref[i] = total[:, :, i * chunk : (i + 1) * chunk]
    part_ref[...] = jnp.zeros(part_ref.shape, F32)
    step = part_ref.shape[1] // 3
    for z in range(nz):
        for dt in range(3):
            for i in range(sum_ref.shape[0]):
                part_ref[z, dt * step : dt * step + run, i * chunk : (i + 1) * chunk] = sum_ref[
                    i, dt, pl.ds(z, run, stride=nz), :
                ]
    side = lax.rem(place(nz)[3], 2)
    for m in range(nz // 2):
        keep_ref[m] = part_ref[2 * m + side]
        send_ref[m] = part_ref[2 * m + 1 - side].astype(B16)


def pair_kernel(nz, keep_ref, got_ref, *refs):
    sends, sum_ref = refs[:-1], refs[-1]
    sum_ref[...] = keep_ref[...] + got_ref[...].astype(F32)
    m = lax.div(place(nz)[3], 2)
    for d, ref in enumerate(sends):
        ref[...] = sum_ref[lax.rem(m + d, nz // 2)].astype(ref.dtype)


def last_kernel(count, *refs):
    parts, (weight_ref, head_ref, loss_ref) = refs[:count], refs[count:]
    total = parts[0][...]
    for ref in parts[1:]:
        total = total + ref[...].astype(F32)
    run, _, block = weight_ref.shape
    step = total.shape[0] // 3
    for dt in range(3):
        for q in range(9):
            weight_ref[:, dt * 9 + q, :] = total[dt * step : dt * step + run, q * block : (q + 1) * block]
    base = 9 * block
    head_ref[...] = total[:run, base : base + head_ref.shape[1]]
    loss = total[step : step + 1, base : base + 1]
    loss = loss + total[step : step + 1, base + 8 : base + 9]
    loss_ref[...] = loss + total[step : step + 1, base + 16 : base + 17]


def body(frames, conv_weight, head_weight, clip_len):
    nf, nrow, ncol, chans = frames.shape
    band = nrow * ncol
    cells = nf * band
    count = lax.axis_size("tm")
    ny = 4 if count == 64 else 2
    nz = count // 2 // ny
    run = chans // count
    chip = 2 * nf
    shape = jax.ShapeDtypeStruct

    def index(yy, zz, cc):
        return ((yy % ny) * nz + zz % nz) * 2 + cc

    every = [(yy, zz, cc) for yy in range(ny) for zz in range(nz) for cc in range(2)]

    def over_core(v):
        return lax.ppermute(v, "tm", [(i, i ^ 1) for i in range(count)])

    def over_chip(v, d):
        return lax.ppermute(v, "tm", [(i, (i + 2 * d) % count) for i in range(count)])

    def over_x(v, d):
        return lax.ppermute(v, "space", [(i, (i + d) % 4) for i in range(4)])

    def over_y(v, d):
        return lax.ppermute(v, "tm", [(index(a, b, e), index(a + d, b, e)) for a, b, e in every])

    def over_z(v, d):
        return lax.ppermute(v, "tm", [(index(a, b, e), index(a, b + d, e)) for a, b, e in every])

    table = half_table(chans, run, ny, nz)
    lanes = table.shape[2]
    table = np.concatenate([table, table[::-1]], axis=2)
    table = jnp.asarray(table, B16)
    flat = frames.reshape(nf, band, chans)
    edge = shape((nf, ncol, chans), B16)
    top, bot = call(first_kernel, [edge, edge], name="first")(flat)
    top, bot = (
        lax.ppermute(bot, "space", [(i, i + 1) for i in range(3)]),
        lax.ppermute(top, "space", [(i + 1, i) for i in range(3)]),
    )
    flat, top, bot = lax.optimization_barrier((flat, top, bot))
    flats = [flat] + [over_x(flat, d) for d in (1, 2, 3)]
    ends = call(ends_kernel, shape((2, band + 2 * ncol, chans), B16), name="ends")(flat, top, bot)
    ends = lax.ppermute(ends, "tm", [(i, i + 1) for i in range(count - 1)])

    whole = lambda *dims: pl.BlockSpec(dims, lambda i: (0,) * len(dims))
    zlat = head_weight.shape[1]
    hblock = zlat // 4
    block = chans // 4
    message = shape((32 + block, cells), B16)
    latent, *mine_d = call(
        forward_kernel,
        [shape((cells, zlat), F32)] + [message] * 4,
        [
            pltpu.VMEM((cells, chans), F32),
            pltpu.VMEM(((nf + 2) * band, 9 * chans), B16),
            pltpu.VMEM((chans, cells), B16),
            pltpu.VMEM((nf, zlat, chans), F32),
            pltpu.VMEM((3, 9 * chans, chans), B16),
            pltpu.SemaphoreType.DMA((3,)),
        ],
        grid=(1,),
        in_specs=[smem()]
        + [whole(*v.shape) for v in (flat, ends, top, bot)]
        + [pl.BlockSpec(memory_space=pl.ANY), whole(zlat, chans)],
        out_specs=[whole(cells, zlat)] + [whole(*message.shape)] * 4,
        name="forward",
    )(clip_len, flat, ends, top, bot, conv_weight.reshape(3, 9 * chans, chans), head_weight.T)
    mine_d, flats = lax.optimization_barrier((mine_d, flats))
    mine_d = [mine_d[0]] + [over_x(mine_d[d], d) for d in (1, 2, 3)]
    chosen = shape((4, 4 * band, lanes), B16)
    spec = pl.BlockSpec((1, 4 * band, lanes), lambda i: (i, 0, 0))
    xown, xoth = call(
        choose_kernel,
        [chosen, chosen],
        [pltpu.VMEM((4 * band, chans), B16)],
        grid=(4,),
        in_specs=[pl.BlockSpec((1, band, chans), lambda i: (i, 0, 0))] * 4 + [whole(*table.shape)],
        out_specs=[spec, spec],
        name="choose",
    )(*flats, table)
    mine_d, xoth = lax.optimization_barrier((mine_d, xoth))
    core_d = [over_core(v) for v in mine_d]
    xoth = over_core(xoth)

    front = pl.BlockSpec((message.shape[0], 2 * band), lambda i: (0, 0))
    kchip, tail = call(
        clip_kernel,
        [shape((chip, 128), F32), shape((4, block, 2 * band), B16)],
        grid=(1,),
        in_specs=[front] * 8,
        out_specs=[whole(chip, 128), whole(4, block, 2 * band)],
        name="clip",
    )(*mine_d, *core_d)
    tail = over_chip(tail, -1)
    triple = jnp.stack([over_chip(kchip, 1), kchip, over_chip(kchip, -1)])
    left, right = over_chip(triple, 2), over_chip(triple, -2)

    rows = run * nz
    wrow = 9 * block + 32
    sends = call(
        functools.partial(weight_kernel, ny, nz, float(4 * band)),
        [shape((3, rows, wrow), F32)] + [shape((3, rows, wrow), B16)] * (ny - 1),
        [
            pltpu.VMEM((2, 4) + message.shape, B16),
            pltpu.VMEM((2, 9 * block, 4 * band), B16),
            pltpu.VMEM((3, wrow, lanes), F32),
            pltpu.VMEM((lanes, wrow), F32),
            pltpu.VMEM((8, 4 * band, lanes), B16),
            pltpu.VMEM((2 * chip, 128), F32),
            pltpu.VMEM((3, 2 * chip, 128), F32),
            pltpu.SemaphoreType.DMA((3, 4)),
        ],
        in_specs=[smem()] + [vmem()] * 4 + [pl.BlockSpec(memory_space=pl.ANY)] * 10 + [vmem()],
        name="weight",
    )(clip_len, left, kchip, right, tail, *mine_d, *core_d, xown, xoth, table)
    gets = [sends[0]] + [over_y(sends[d], d) for d in range(1, ny)]
    step = wide(run)
    chunk = 128 if wrow % 128 == 0 else wrow
    half = shape((nz // 2, 3 * step, wrow), F32)
    kept, sent = call(
        functools.partial(add_kernel, ny, nz, run),
        [half, shape(half.shape, B16)],
        [pltpu.VMEM((wrow // chunk, 3, rows, chunk), F32), pltpu.VMEM((nz, 3 * step, wrow), F32)],
        name="add",
    )(*gets)
    sent = lax.ppermute(sent, "tm", [(index(a, b, e), index(a, b ^ 1, e)) for a, b, e in every])
    parts = call(
        functools.partial(pair_kernel, nz),
        [shape((3 * step, wrow), F32)] + [shape((3 * step, wrow), B16)] * (nz // 2 - 1),
        [pltpu.VMEM(half.shape, F32)],
        name="pair",
    )(kept, sent)
    parts = [parts[0]] + [over_z(parts[d], 2 * d) for d in range(1, nz // 2)]
    weight_grad, head_grad, loss = call(
        functools.partial(last_kernel, nz // 2),
        [shape((run, 27, block), F32), shape((run, hblock), F32), shape((1, 1), F32)],
        name="last",
    )(*parts)
    return latent.reshape(nf, nrow, ncol, zlat), loss[0, 0], weight_grad.transpose(1, 0, 2), head_grad


def solution(mesh):
    in_specs = (P("tm", "space", None, None), P(), P(), P())
    out_specs = (P("tm", "space", None, None), P(), P(None, "tm", "space"), P("tm", "space"))
    return jax.shard_map(body, mesh=mesh, in_specs=in_specs, out_specs=out_specs, check_vma=False)
```

```python
import functools

import jax
import jax.numpy as jnp
import numpy as np
from jax import lax
from jax.experimental import pallas as pl
from jax.experimental.pallas import tpu as pltpu
from jax.sharding import PartitionSpec as P

F32 = jnp.float32
B16 = jnp.bfloat16
COLS = 24
LIMIT = 56 * 1024 * 1024
NT = (((1,), (1,)), ((), ()))
TN = (((0,), (0,)), ((), ()))


def dot(a, b, dims=None):
    if dims is None:
        return jnp.dot(a, b, preferred_element_type=F32)
    return lax.dot_general(a, b, dims, preferred_element_type=F32)


def call(kernel, outs, scratch=(), **kw):
    params = pltpu.CompilerParams(vmem_limit_bytes=LIMIT)
    return pl.pallas_call(kernel, out_shape=outs, scratch_shapes=list(scratch), compiler_params=params, **kw)


def smem():
    return pl.BlockSpec(memory_space=pltpu.SMEM)


def vmem():
    return pl.BlockSpec(memory_space=pltpu.VMEM)


def place(nz):
    t = lax.axis_index("tm")
    k = lax.div(t, 2)
    return lax.rem(t, 2), lax.axis_index("space"), lax.div(k, nz), lax.rem(k, nz), k


def half_table(chans, run, ny, nz):
    lane = np.arange(chans // 2)
    block = wide(run) * nz
    spot = (lane // run // nz) * block + (lane % run) * nz + lane // run % nz
    table = np.zeros((2, chans, ny * block), np.float32)
    for core in range(2):
        table[core, (lane // run) * 2 * run + core * run + lane % run, spot] = 1
    return table


def wide(run):
    return -(-run // 8) * 8


def first_kernel(x_ref, top_ref, bot_ref):
    nf, band, chans = x_ref.shape
    for f in range(nf):
        wide_frame = x_ref[f].astype(F32)
        top_ref[f] = wide_frame[:COLS].astype(B16)
        bot_ref[f] = wide_frame[band - COLS :].astype(B16)


def frame_of(top, mid, bot):
    return jnp.concatenate([top.astype(F32), mid.astype(F32), bot.astype(F32)], axis=0)


def ends_kernel(x_ref, top_ref, bot_ref, ends_ref):
    nf = x_ref.shape[0]
    for f in range(2):
        g = nf - 2 + f
        ends_ref[f] = frame_of(top_ref[g], x_ref[g], bot_ref[g]).astype(B16)


def choose_kernel(f0, f1, f2, f3, table_ref, own_ref, oth_ref, wide_ref):
    c, x = lax.rem(lax.axis_index("tm"), 2), lax.axis_index("space")
    band = f0.shape[1]

    for d, ref in enumerate((f0, f1, f2, f3)):
        wide_ref[pl.ds(pl.multiple_of(lax.rem(x - d + 4, 4) * band, band), band)] = ref[0]
    both = dot(wide_ref[...], table_ref[c]).astype(B16)
    lanes = own_ref.shape[2]
    own_ref[0] = both[:, :lanes]
    oth_ref[0] = both[:, lanes:]


def forward_kernel(len_ref, x_ref, ends_ref, top_ref, bot_ref, w_ref, hw_ref,
                   lat_ref, d0, d1, d2, d3, pre_ref, wide_ref, turned_ref, head_ref, held_ref, sem):
    nf, band, chans = x_ref.shape
    rows = band + 2 * COLS
    loads = [pltpu.make_async_copy(w_ref.at[dt], held_ref.at[dt], sem.at[dt]) for dt in range(3)]
    for load in loads:
        load.start()
    col = lax.rem(lax.broadcasted_iota(jnp.int32, (rows, 1), 0), COLS)

    def build(f):
        if f < 2:
            v = ends_ref[f].astype(F32)
        else:
            v = frame_of(top_ref[f - 2], x_ref[f - 2], bot_ref[f - 2])
        for dw in range(3):
            if dw == 0:
                s = jnp.where(col > 0, pltpu.roll(v, 1, 0), 0.0)
            elif dw == 2:
                s = jnp.where(col < COLS - 1, pltpu.roll(v, rows - 1, 0), 0.0)
            else:
                s = v
            for dh in range(3):
                q = dh * 3 + dw
                wide_ref[f * band : (f + 1) * band, q * chans : (q + 1) * chans] = s[
                    dh * COLS : dh * COLS + band
                ].astype(B16)

    t, xs = lax.axis_index("tm"), lax.axis_index("space")
    pos = [jnp.int32(0)] * nf
    start = jnp.int32(0)
    for j in range(len_ref.shape[0]):
        for f in range(nf):
            pos[f] = jnp.where(t * nf + f >= start, t * nf + f - start, pos[f])
        start = start + len_ref[j]
    for f in range(nf):
        build(f)
    for dt in range(3):
        if dt:
            build(nf - 1 + dt)
        loads[dt].wait()
        part = dot(wide_ref[dt * band : (dt + nf) * band, :], held_ref[dt])
        for f in range(nf):
            keep = jnp.where(pos[f] >= 2 - dt, 1.0, 0.0)
            piece = keep * part[f * band : (f + 1) * band]
            if dt == 0:
                pre_ref[f * band : (f + 1) * band] = piece
            else:
                pre_ref[f * band : (f + 1) * band] += piece

    zdim = lat_ref.shape[1] // 2
    row = lax.broadcasted_iota(jnp.int32, (16, 128), 0)
    kf = jnp.zeros((16, 128), F32)
    for f in range(nf):
        at = slice(f * band, (f + 1) * band)
        pre = pre_ref[at]
        sig = 1.0 / (1.0 + jnp.exp(-pre))
        act = (pre * sig).astype(B16)
        lat = dot(act, hw_ref[...], NT)
        lat_ref[at] = lat
        lane = lax.broadcasted_iota(jnp.int32, lat.shape, 1)
        grow = jnp.exp(lat) - 1.0
        term = jnp.where(lane < zdim, lat * lat, grow - lat)
        kf = jnp.where(lax.rem(row, nf) == f, 0.5 * jnp.sum(term), kf)
        dlat = jnp.where(lane < zdim, lat, 0.5 * grow).astype(B16)
        dact = dot(dlat, hw_ref[...])
        pre_ref[at] = (dact * sig * (1.0 + pre * (1.0 - sig))).astype(B16).astype(F32)
        head_ref[f] = dot(dlat, act, TN)
    high = kf.astype(B16).astype(F32)
    mid = (kf - high).astype(B16).astype(F32)
    kf = jnp.where(row < nf, high, jnp.where(row < 2 * nf, mid, jnp.where(row < 3 * nf, kf - high - mid, 0.0)))
    turned_ref[...] = jnp.transpose(pre_ref[...], (1, 0)).astype(B16)
    block = chans // 4
    hblock = 2 * zdim // 4
    for d, ref in enumerate((d0, d1, d2, d3)):
        to = lax.rem(xs + d, 4)
        ref[:16, :128] = kf.astype(B16)
        ref[:16, 128:] = jnp.zeros((16, ref.shape[1] - 128), B16)
        ref[32:] = turned_ref[pl.ds(pl.multiple_of(to * block, block), block), :]
        heads = [head_ref[f, pl.ds(pl.multiple_of(to * hblock, hblock), hblock), :] for f in range(nf)]
        pad = ref.shape[1] - 2 * chans
        if pad:
            heads = [jnp.concatenate([h, jnp.zeros((hblock, pad // 2), F32)], axis=1) for h in heads]
        both = jnp.concatenate(
            [jnp.concatenate(heads[:2], axis=1), jnp.concatenate(heads[2:], axis=1)], axis=0
        )
        ref[16:32] = both.astype(B16)


def clip_kernel(*refs):
    c, x = lax.rem(lax.axis_index("tm"), 2), lax.axis_index("space")
    given, (sums_ref, tail_ref) = (refs[:4], refs[4:8]), refs[8:]
    sums = []
    for four in given:
        v = four[0][:16, :128].astype(F32)
        for ref in four[1:]:
            v = v + ref[:16, :128].astype(F32)
        sums.append(v[:4] + v[4:8] + v[8:12])
    for core in range(2):

        @pl.when(c == core)
        def _():
            sums_ref[...] = jnp.concatenate([sums[core], sums[1 - core]], axis=0)
            for d in range(4):
                tail_ref[lax.rem(x - d + 4, 4)] = given[core][d][32:, :]


def weight_kernel(ny, nz, per_frame, len_ref, left_ref, mid_ref, right_ref, next_ref, a0, a1, a2, a3, b0, b1, b2, b3,
                  x_ref, xo_ref, table_ref, *refs):
    sends, (held_ref, taps_ref, acc_ref, out_ref, xs_ref, g_ref, keep_ref, sem) = refs[:ny], refs[ny:]
    c, x, y, _, k = place(nz)
    copies = []
    for core, given, s in ((c, (a0, a1, a2, a3), 0), (1 - c, (b0, b1, b2, b3), 1)):
        for d, ref in enumerate(given):
            copies.append(pltpu.make_async_copy(ref, held_ref.at[core, lax.rem(x - d + 4, 4)], sem.at[s, d]))
    for core, ref, s in ((c, x_ref, 0), (1 - c, xo_ref, 1)):
        copies.append(pltpu.make_async_copy(ref, xs_ref.at[pl.ds(4 * core, 4)], sem.at[2, s]))
    for copy in copies:
        copy.start()
    full = x_ref.shape[1]
    band = full // 4
    block = taps_ref.shape[1] // 9
    chans = table_ref.shape[1]
    lanes = acc_ref.shape[2]
    hblock = 8
    half = full // 2
    window = jnp.concatenate(
        [left_ref[0], left_ref[1], left_ref[2], mid_ref[...], right_ref[0], right_ref[1], right_ref[2]], axis=0
    )
    chip = mid_ref.shape[0]
    wids = chip * (k - 3) + lax.broadcasted_iota(jnp.int32, window.shape, 0)
    ids = chip * k + lax.broadcasted_iota(jnp.int32, g_ref.shape, 0)
    total = jnp.zeros(g_ref.shape, F32)
    lens = jnp.ones(g_ref.shape, F32)
    pos = jnp.full(g_ref.shape, -1, jnp.int32)
    start = jnp.int32(0)
    for j in range(len_ref.shape[0]):
        size = len_ref[j]
        inside = jnp.where((wids >= start) & (wids < start + size), window, 0.0)
        mine = (ids >= start) & (ids < start + size)
        total = jnp.where(mine, jnp.sum(inside, axis=0, keepdims=True), total)
        lens = jnp.where(mine, size.astype(F32), lens)
        pos = jnp.where(mine, ids - start, pos)
        start = start + size
    gain = lens / (lens * per_frame + total)
    g_ref[...] = gain
    for dt in range(3):
        keep_ref[dt] = jnp.where(pos >= 2 - dt, gain, 0.0)
    row = lax.broadcasted_iota(jnp.int32, g_ref.shape, 0)
    loss = jnp.where((pos == 0) & (row < chip), lens * jnp.log1p(total / (lens * per_frame)), 0.0)
    loss = jnp.sum(loss, axis=0, keepdims=True)
    hsum = jnp.zeros((hblock, chans), F32)
    for copy in copies[:8]:
        copy.wait()
    for core in range(2):
        for xs in range(4):
            tail = held_ref[core, xs, 16:32, :].astype(F32)
            for f in range(4):
                part = tail[(f // 2) * hblock : (f // 2 + 1) * hblock, (f % 2) * half : (f % 2) * half + chans]
                hsum = hsum + g_ref[core * 4 + f : core * 4 + f + 1, :1] * part
    acc_ref[...] = jnp.zeros(acc_ref.shape, F32)
    lane = lax.broadcasted_iota(jnp.int32, (1, full), 1)
    col = lax.rem(lane, COLS)
    line = lane // COLS

    def build(f):
        core, lf = f // 4 % 2, f % 4
        frame = jnp.zeros((block, full), F32)
        for xs in range(4):
            if f < 8:
                v = held_ref[core, xs, 32:, :].astype(F32)
            else:
                v = next_ref[xs].astype(F32)
                v = jnp.concatenate([v, jnp.zeros_like(v)], axis=1)
            shift = ((xs - lf) * band) % full
            if shift:
                v = pltpu.roll(v, shift, 1)
            frame = jnp.where(lane // band == xs, v, frame)
        for dw in range(3):
            if dw == 0:
                v = jnp.where(col < COLS - 1, pltpu.roll(frame, full - 1, 1), 0.0)
            elif dw == 2:
                v = jnp.where(col > 0, pltpu.roll(frame, 1, 1), 0.0)
            else:
                v = frame
            for dh in range(3):
                if dh == 0:
                    s = jnp.where(line < full // COLS - 1, pltpu.roll(v, full - COLS, 1), 0.0)
                elif dh == 2:
                    s = jnp.where(line > 0, pltpu.roll(v, COLS, 1), 0.0)
                else:
                    s = v
                q = dh * 3 + dw
                taps_ref[f % 2, q * block : (q + 1) * block, :] = s.astype(B16)

    build(0)
    for copy in copies[8:]:
        copy.wait()
    for f in range(10):
        if f < 9:
            build(f + 1)
        for dt in range(3):
            if 0 <= f - 2 + dt < 8:
                scale = keep_ref[dt, f : f + 1, :1]
                acc_ref[dt, : 9 * block] += scale * dot(taps_ref[f % 2], xs_ref[f - 2 + dt])
    direct = table_ref[c, :, :lanes]
    high = hsum.astype(B16)
    low = (hsum - high.astype(F32)).astype(B16)
    acc_ref[0, 9 * block : 9 * block + hblock] = dot(high, direct) + dot(low, direct)
    loss = jnp.broadcast_to(loss[:, :1], (8, lanes))
    top = loss.astype(B16).astype(F32)
    mid = (loss - top).astype(B16).astype(F32)
    acc_ref[1, 9 * block : 9 * block + 8] = top
    acc_ref[1, 9 * block + 8 : 9 * block + 16] = mid
    acc_ref[1, 9 * block + 16 : 9 * block + 24] = loss - top - mid
    rows = sends[0].shape[1]
    ystep = lanes // ny
    for dt in range(3):
        out_ref[...] = jnp.transpose(acc_ref[dt], (1, 0))
        for d, ref in enumerate(sends):
            to = lax.rem(y + d, ny)
            ref[dt] = out_ref[pl.ds(pl.multiple_of(to * ystep, 8), rows), :].astype(ref.dtype)


def add_kernel(ny, nz, run, *refs):
    gets, (keep_ref, send_ref, sum_ref, part_ref) = refs[:ny], refs[ny:]
    total = gets[0][...]
    for ref in gets[1:]:
        total = total + ref[...].astype(F32)
    chunk = sum_ref.shape[3]
    for i in range(sum_ref.shape[0]):
        sum_ref[i] = total[:, :, i * chunk : (i + 1) * chunk]
    part_ref[...] = jnp.zeros(part_ref.shape, F32)
    step = part_ref.shape[1] // 3
    for z in range(nz):
        for dt in range(3):
            for i in range(sum_ref.shape[0]):
                part_ref[z, dt * step : dt * step + run, i * chunk : (i + 1) * chunk] = sum_ref[
                    i, dt, pl.ds(z, run, stride=nz), :
                ]
    side = lax.rem(place(nz)[3], 2)
    for m in range(nz // 2):
        keep_ref[m] = part_ref[2 * m + side]
        send_ref[m] = part_ref[2 * m + 1 - side].astype(B16)


def pair_kernel(nz, keep_ref, got_ref, *refs):
    sends, sum_ref = refs[:-1], refs[-1]
    sum_ref[...] = keep_ref[...] + got_ref[...].astype(F32)
    m = lax.div(place(nz)[3], 2)
    for d, ref in enumerate(sends):
        ref[...] = sum_ref[lax.rem(m + d, nz // 2)].astype(ref.dtype)


def last_kernel(count, *refs):
    parts, (weight_ref, head_ref, loss_ref) = refs[:count], refs[count:]
    total = parts[0][...]
    for ref in parts[1:]:
        total = total + ref[...].astype(F32)
    run, _, block = weight_ref.shape
    step = total.shape[0] // 3
    for dt in range(3):
        for q in range(9):
            weight_ref[:, dt * 9 + q, :] = total[dt * step : dt * step + run, q * block : (q + 1) * block]
    base = 9 * block
    head_ref[...] = total[:run, base : base + head_ref.shape[1]]
    loss = total[step : step + 1, base : base + 1]
    loss = loss + total[step : step + 1, base + 8 : base + 9]
    loss_ref[...] = loss + total[step : step + 1, base + 16 : base + 17]


def body(frames, conv_weight, head_weight, clip_len):
    nf, nrow, ncol, chans = frames.shape
    band = nrow * ncol
    cells = nf * band
    count = lax.axis_size("tm")
    ny = 4 if count == 64 else 2
    nz = count // 2 // ny
    run = chans // count
    chip = 2 * nf
    shape = jax.ShapeDtypeStruct

    def index(yy, zz, cc):
        return ((yy % ny) * nz + zz % nz) * 2 + cc

    every = [(yy, zz, cc) for yy in range(ny) for zz in range(nz) for cc in range(2)]

    def over_core(v):
        return lax.ppermute(v, "tm", [(i, i ^ 1) for i in range(count)])

    def over_chip(v, d):
        return lax.ppermute(v, "tm", [(i, (i + 2 * d) % count) for i in range(count)])

    def over_x(v, d):
        return lax.ppermute(v, "space", [(i, (i + d) % 4) for i in range(4)])

    def over_y(v, d):
        return lax.ppermute(v, "tm", [(index(a, b, e), index(a + d, b, e)) for a, b, e in every])

    def over_z(v, d):
        return lax.ppermute(v, "tm", [(index(a, b, e), index(a, b + d, e)) for a, b, e in every])

    table = half_table(chans, run, ny, nz)
    lanes = table.shape[2]
    table = np.concatenate([table, table[::-1]], axis=2)
    table = jnp.asarray(table, B16)
    flat = frames.reshape(nf, band, chans)
    edge = shape((nf, ncol, chans), B16)
    top, bot = call(first_kernel, [edge, edge], name="first")(flat)
    top, bot = (
        lax.ppermute(bot, "space", [(i, i + 1) for i in range(3)]),
        lax.ppermute(top, "space", [(i + 1, i) for i in range(3)]),
    )
    flat, top, bot = lax.optimization_barrier((flat, top, bot))
    flats = [flat] + [over_x(flat, d) for d in (1, 2, 3)]
    ends = call(ends_kernel, shape((2, band + 2 * ncol, chans), B16), name="ends")(flat, top, bot)
    ends = lax.ppermute(ends, "tm", [(i, i + 1) for i in range(count - 1)])

    whole = lambda *dims: pl.BlockSpec(dims, lambda i: (0,) * len(dims))
    zlat = head_weight.shape[1]
    hblock = zlat // 4
    block = chans // 4
    message = shape((32 + block, cells), B16)
    latent, *mine_d = call(
        forward_kernel,
        [shape((cells, zlat), F32)] + [message] * 4,
        [
            pltpu.VMEM((cells, chans), F32),
            pltpu.VMEM(((nf + 2) * band, 9 * chans), B16),
            pltpu.VMEM((chans, cells), B16),
            pltpu.VMEM((nf, zlat, chans), F32),
            pltpu.VMEM((3, 9 * chans, chans), B16),
            pltpu.SemaphoreType.DMA((3,)),
        ],
        grid=(1,),
        in_specs=[smem()]
        + [whole(*v.shape) for v in (flat, ends, top, bot)]
        + [pl.BlockSpec(memory_space=pl.ANY), whole(zlat, chans)],
        out_specs=[whole(cells, zlat)] + [whole(*message.shape)] * 4,
        name="forward",
    )(clip_len, flat, ends, top, bot, conv_weight.reshape(3, 9 * chans, chans), head_weight.T)
    mine_d, flats = lax.optimization_barrier((mine_d, flats))
    mine_d = [mine_d[0]] + [over_x(mine_d[d], d) for d in (1, 2, 3)]
    chosen = shape((4, 4 * band, lanes), B16)
    spec = pl.BlockSpec((1, 4 * band, lanes), lambda i: (i, 0, 0))
    xown, xoth = call(
        choose_kernel,
        [chosen, chosen],
        [pltpu.VMEM((4 * band, chans), B16)],
        grid=(4,),
        in_specs=[pl.BlockSpec((1, band, chans), lambda i: (i, 0, 0))] * 4 + [whole(*table.shape)],
        out_specs=[spec, spec],
        name="choose",
    )(*flats, table)
    mine_d, xoth = lax.optimization_barrier((mine_d, xoth))
    core_d = [over_core(v) for v in mine_d]
    xoth = over_core(xoth)

    front = pl.BlockSpec((message.shape[0], 2 * band), lambda i: (0, 0))
    kchip, tail = call(
        clip_kernel,
        [shape((chip, 128), F32), shape((4, block, 2 * band), B16)],
        grid=(1,),
        in_specs=[front] * 8,
        out_specs=[whole(chip, 128), whole(4, block, 2 * band)],
        name="clip",
    )(*mine_d, *core_d)
    before, after = over_chip(kchip, 1), over_chip(kchip, -1)
    tail, before, after = lax.optimization_barrier((tail, before, after))
    tail = over_chip(tail, -1)
    triple = jnp.stack([before, kchip, after])
    left, right = over_chip(triple, 2), over_chip(triple, -2)

    rows = run * nz
    wrow = 9 * block + 32
    sends = call(
        functools.partial(weight_kernel, ny, nz, float(4 * band)),
        [shape((3, rows, wrow), F32)] + [shape((3, rows, wrow), B16)] * (ny - 1),
        [
            pltpu.VMEM((2, 4) + message.shape, B16),
            pltpu.VMEM((2, 9 * block, 4 * band), B16),
            pltpu.VMEM((3, wrow, lanes), F32),
            pltpu.VMEM((lanes, wrow), F32),
            pltpu.VMEM((8, 4 * band, lanes), B16),
            pltpu.VMEM((2 * chip, 128), F32),
            pltpu.VMEM((3, 2 * chip, 128), F32),
            pltpu.SemaphoreType.DMA((3, 4)),
        ],
        in_specs=[smem()] + [vmem()] * 4 + [pl.BlockSpec(memory_space=pl.ANY)] * 10 + [vmem()],
        name="weight",
    )(clip_len, left, kchip, right, tail, *mine_d, *core_d, xown, xoth, table)
    gets = [sends[0]] + [over_y(sends[d], d) for d in range(1, ny)]
    step = wide(run)
    chunk = 128 if wrow % 128 == 0 else wrow
    half = shape((nz // 2, 3 * step, wrow), F32)
    kept, sent = call(
        functools.partial(add_kernel, ny, nz, run),
        [half, shape(half.shape, B16)],
        [pltpu.VMEM((wrow // chunk, 3, rows, chunk), F32), pltpu.VMEM((nz, 3 * step, wrow), F32)],
        name="add",
    )(*gets)
    sent = lax.ppermute(sent, "tm", [(index(a, b, e), index(a, b ^ 1, e)) for a, b, e in every])
    parts = call(
        functools.partial(pair_kernel, nz),
        [shape((3 * step, wrow), F32)] + [shape((3 * step, wrow), B16)] * (nz // 2 - 1),
        [pltpu.VMEM(half.shape, F32)],
        name="pair",
    )(kept, sent)
    parts = [parts[0]] + [over_z(parts[d], 2 * d) for d in range(1, nz // 2)]
    weight_grad, head_grad, loss = call(
        functools.partial(last_kernel, nz // 2),
        [shape((run, 27, block), F32), shape((run, hblock), F32), shape((1, 1), F32)],
        name="last",
    )(*parts)
    return latent.reshape(nf, nrow, ncol, zlat), loss[0, 0], weight_grad.transpose(1, 0, 2), head_grad


def solution(mesh):
    in_specs = (P("tm", "space", None, None), P(), P(), P())
    out_specs = (P("tm", "space", None, None), P(), P(None, "tm", "space"), P("tm", "space"))
    return jax.shard_map(body, mesh=mesh, in_specs=in_specs, out_specs=out_specs, check_vma=False)
```

```python
import functools

import jax
import jax.numpy as jnp
import numpy as np
from jax import lax
from jax.experimental import pallas as pl
from jax.experimental.pallas import tpu as pltpu
from jax.sharding import PartitionSpec as P

F32 = jnp.float32
B16 = jnp.bfloat16
COLS = 24
LIMIT = 56 * 1024 * 1024
NT = (((1,), (1,)), ((), ()))
TN = (((0,), (0,)), ((), ()))


def dot(a, b, dims=None):
    if dims is None:
        return jnp.dot(a, b, preferred_element_type=F32)
    return lax.dot_general(a, b, dims, preferred_element_type=F32)


def call(kernel, outs, scratch=(), **kw):
    params = pltpu.CompilerParams(vmem_limit_bytes=LIMIT)
    return pl.pallas_call(kernel, out_shape=outs, scratch_shapes=list(scratch), compiler_params=params, **kw)


def smem():
    return pl.BlockSpec(memory_space=pltpu.SMEM)


def vmem():
    return pl.BlockSpec(memory_space=pltpu.VMEM)


def place(nz):
    t = lax.axis_index("tm")
    k = lax.div(t, 2)
    return lax.rem(t, 2), lax.axis_index("space"), lax.div(k, nz), lax.rem(k, nz), k


def half_table(chans, run, ny, nz):
    lane = np.arange(chans // 2)
    block = wide(run) * nz
    spot = (lane // run // nz) * block + (lane % run) * nz + lane // run % nz
    table = np.zeros((2, chans, ny * block), np.float32)
    for core in range(2):
        table[core, (lane // run) * 2 * run + core * run + lane % run, spot] = 1
    return table


def wide(run):
    return -(-run // 8) * 8


def first_kernel(x_ref, top_ref, bot_ref):
    nf, band, chans = x_ref.shape
    for f in range(nf):
        wide_frame = x_ref[f].astype(F32)
        top_ref[f] = wide_frame[:COLS].astype(B16)
        bot_ref[f] = wide_frame[band - COLS :].astype(B16)


def frame_of(top, mid, bot):
    return jnp.concatenate([top.astype(F32), mid.astype(F32), bot.astype(F32)], axis=0)


def ends_kernel(x_ref, top_ref, bot_ref, ends_ref):
    nf = x_ref.shape[0]
    for f in range(2):
        g = nf - 2 + f
        ends_ref[f] = frame_of(top_ref[g], x_ref[g], bot_ref[g]).astype(B16)


def choose_kernel(f0, f1, f2, f3, table_ref, own_ref, oth_ref, wide_ref):
    c, x = lax.rem(lax.axis_index("tm"), 2), lax.axis_index("space")
    band = f0.shape[1]

    for d, ref in enumerate((f0, f1, f2, f3)):
        wide_ref[pl.ds(pl.multiple_of(lax.rem(x - d + 4, 4) * band, band), band)] = ref[0]
    both = dot(wide_ref[...], table_ref[c]).astype(B16)
    lanes = own_ref.shape[2]
    own_ref[0] = both[:, :lanes]
    oth_ref[0] = both[:, lanes:]


def forward_kernel(len_ref, x_ref, ends_ref, top_ref, bot_ref, w_ref, hw_ref,
                   lat_ref, d0, d1, d2, d3, pre_ref, wide_ref, turned_ref, head_ref, held_ref, sem):
    nf, band, chans = x_ref.shape
    rows = band + 2 * COLS
    loads = [pltpu.make_async_copy(w_ref.at[dt], held_ref.at[dt], sem.at[dt]) for dt in range(3)]
    for load in loads:
        load.start()
    col = lax.rem(lax.broadcasted_iota(jnp.int32, (rows, 1), 0), COLS)

    def build(f):
        if f < 2:
            v = ends_ref[f].astype(F32)
        else:
            v = frame_of(top_ref[f - 2], x_ref[f - 2], bot_ref[f - 2])
        for dw in range(3):
            if dw == 0:
                s = jnp.where(col > 0, pltpu.roll(v, 1, 0), 0.0)
            elif dw == 2:
                s = jnp.where(col < COLS - 1, pltpu.roll(v, rows - 1, 0), 0.0)
            else:
                s = v
            for dh in range(3):
                q = dh * 3 + dw
                wide_ref[f * band : (f + 1) * band, q * chans : (q + 1) * chans] = s[
                    dh * COLS : dh * COLS + band
                ].astype(B16)

    t, xs = lax.axis_index("tm"), lax.axis_index("space")
    pos = [jnp.int32(0)] * nf
    start = jnp.int32(0)
    for j in range(len_ref.shape[0]):
        for f in range(nf):
            pos[f] = jnp.where(t * nf + f >= start, t * nf + f - start, pos[f])
        start = start + len_ref[j]
    for f in range(nf):
        build(f)
    for dt in range(3):
        if dt:
            build(nf - 1 + dt)
        loads[dt].wait()
        part = dot(wide_ref[dt * band : (dt + nf) * band, :], held_ref[dt])
        for f in range(nf):
            keep = jnp.where(pos[f] >= 2 - dt, 1.0, 0.0)
            piece = keep * part[f * band : (f + 1) * band]
            if dt == 0:
                pre_ref[f * band : (f + 1) * band] = piece
            else:
                pre_ref[f * band : (f + 1) * band] += piece

    zdim = lat_ref.shape[1] // 2
    row = lax.broadcasted_iota(jnp.int32, (16, 128), 0)
    kf = jnp.zeros((16, 128), F32)
    for f in range(nf):
        at = slice(f * band, (f + 1) * band)
        pre = pre_ref[at]
        sig = 1.0 / (1.0 + jnp.exp(-pre))
        act = (pre * sig).astype(B16)
        lat = dot(act, hw_ref[...], NT)
        lat_ref[at] = lat
        lane = lax.broadcasted_iota(jnp.int32, lat.shape, 1)
        grow = jnp.exp(lat) - 1.0
        term = jnp.where(lane < zdim, lat * lat, grow - lat)
        kf = jnp.where(lax.rem(row, nf) == f, 0.5 * jnp.sum(term), kf)
        dlat = jnp.where(lane < zdim, lat, 0.5 * grow).astype(B16)
        dact = dot(dlat, hw_ref[...])
        pre_ref[at] = (dact * sig * (1.0 + pre * (1.0 - sig))).astype(B16).astype(F32)
        head_ref[f] = dot(dlat, act, TN)
    high = kf.astype(B16).astype(F32)
    mid = (kf - high).astype(B16).astype(F32)
    kf = jnp.where(row < nf, high, jnp.where(row < 2 * nf, mid, jnp.where(row < 3 * nf, kf - high - mid, 0.0)))
    turned_ref[...] = jnp.transpose(pre_ref[...], (1, 0)).astype(B16)
    block = chans // 4
    hblock = 2 * zdim // 4
    for d, ref in enumerate((d0, d1, d2, d3)):
        to = lax.rem(xs + d, 4)
        ref[:16, :128] = kf.astype(B16)
        ref[:16, 128:] = jnp.zeros((16, ref.shape[1] - 128), B16)
        ref[32:] = turned_ref[pl.ds(pl.multiple_of(to * block, block), block), :]
        heads = [head_ref[f, pl.ds(pl.multiple_of(to * hblock, hblock), hblock), :] for f in range(nf)]
        pad = ref.shape[1] - 2 * chans
        if pad:
            heads = [jnp.concatenate([h, jnp.zeros((hblock, pad // 2), F32)], axis=1) for h in heads]
        both = jnp.concatenate(
            [jnp.concatenate(heads[:2], axis=1), jnp.concatenate(heads[2:], axis=1)], axis=0
        )
        ref[16:32] = both.astype(B16)


def tail_kernel(a0, a1, a2, a3, out_ref):
    x = lax.axis_index("space")
    for d, ref in enumerate((a0, a1, a2, a3)):
        out_ref[lax.rem(x - d + 4, 4)] = ref[32:, :]


def clip_kernel(*refs):
    c = lax.rem(lax.axis_index("tm"), 2)
    given, sums_ref = (refs[:4], refs[4:8]), refs[8]
    sums = []
    for four in given:
        v = four[0][...].astype(F32)
        for ref in four[1:]:
            v = v + ref[...].astype(F32)
        sums.append(v[:4] + v[4:8] + v[8:12])
    for core in range(2):

        @pl.when(c == core)
        def _():
            sums_ref[...] = jnp.concatenate([sums[core], sums[1 - core]], axis=0)


def weight_kernel(ny, nz, per_frame, len_ref, left_ref, mid_ref, right_ref, next_ref, more_ref, a0, a1, a2, a3, b0, b1, b2, b3,
                  x_ref, xo_ref, table_ref, *refs):
    sends, (held_ref, taps_ref, acc_ref, out_ref, xs_ref, g_ref, keep_ref, sem) = refs[:ny], refs[ny:]
    c, x, y, _, k = place(nz)
    copies = []
    for core, given, s in ((c, (a0, a1, a2, a3), 0), (1 - c, (b0, b1, b2, b3), 1)):
        for d, ref in enumerate(given):
            copies.append(pltpu.make_async_copy(ref, held_ref.at[core, lax.rem(x - d + 4, 4)], sem.at[s, d]))
    for core, ref, s in ((c, x_ref, 0), (1 - c, xo_ref, 1)):
        copies.append(pltpu.make_async_copy(ref, xs_ref.at[pl.ds(4 * core, 4)], sem.at[2, s]))
    for copy in copies:
        copy.start()
    full = x_ref.shape[1]
    band = full // 4
    block = taps_ref.shape[1] // 9
    chans = table_ref.shape[1]
    lanes = acc_ref.shape[2]
    hblock = 8
    half = full // 2
    window = jnp.concatenate(
        [left_ref[0], left_ref[1], left_ref[2], mid_ref[...], right_ref[0], right_ref[1], right_ref[2]], axis=0
    )
    chip = mid_ref.shape[0]
    wids = chip * (k - 3) + lax.broadcasted_iota(jnp.int32, window.shape, 0)
    ids = chip * k + lax.broadcasted_iota(jnp.int32, g_ref.shape, 0)
    total = jnp.zeros(g_ref.shape, F32)
    lens = jnp.ones(g_ref.shape, F32)
    pos = jnp.full(g_ref.shape, -1, jnp.int32)
    start = jnp.int32(0)
    for j in range(len_ref.shape[0]):
        size = len_ref[j]
        inside = jnp.where((wids >= start) & (wids < start + size), window, 0.0)
        mine = (ids >= start) & (ids < start + size)
        total = jnp.where(mine, jnp.sum(inside, axis=0, keepdims=True), total)
        lens = jnp.where(mine, size.astype(F32), lens)
        pos = jnp.where(mine, ids - start, pos)
        start = start + size
    gain = lens / (lens * per_frame + total)
    g_ref[...] = gain
    for dt in range(3):
        keep_ref[dt] = jnp.where(pos >= 2 - dt, gain, 0.0)
    row = lax.broadcasted_iota(jnp.int32, g_ref.shape, 0)
    loss = jnp.where((pos == 0) & (row < chip), lens * jnp.log1p(total / (lens * per_frame)), 0.0)
    loss = jnp.sum(loss, axis=0, keepdims=True)
    hsum = jnp.zeros((hblock, chans), F32)
    for copy in copies[:8]:
        copy.wait()
    for core in range(2):
        for xs in range(4):
            tail = held_ref[core, xs, 16:32, :].astype(F32)
            for f in range(4):
                part = tail[(f // 2) * hblock : (f // 2 + 1) * hblock, (f % 2) * half : (f % 2) * half + chans]
                hsum = hsum + g_ref[core * 4 + f : core * 4 + f + 1, :1] * part
    acc_ref[...] = jnp.zeros(acc_ref.shape, F32)
    lane = lax.broadcasted_iota(jnp.int32, (1, full), 1)
    col = lax.rem(lane, COLS)
    line = lane // COLS

    def build(f):
        core, lf = f // 4 % 2, f % 4
        frame = jnp.zeros((block, full), F32)
        for xs in range(4):
            if f < 8:
                v = held_ref[core, xs, 32:, :].astype(F32)
            else:
                v = next_ref[xs].astype(F32) + more_ref[xs].astype(F32)
                v = jnp.concatenate([v, jnp.zeros_like(v)], axis=1)
            shift = ((xs - lf) * band) % full
            if shift:
                v = pltpu.roll(v, shift, 1)
            frame = jnp.where(lane // band == xs, v, frame)
        for dw in range(3):
            if dw == 0:
                v = jnp.where(col < COLS - 1, pltpu.roll(frame, full - 1, 1), 0.0)
            elif dw == 2:
                v = jnp.where(col > 0, pltpu.roll(frame, 1, 1), 0.0)
            else:
                v = frame
            for dh in range(3):
                if dh == 0:
                    s = jnp.where(line < full // COLS - 1, pltpu.roll(v, full - COLS, 1), 0.0)
                elif dh == 2:
                    s = jnp.where(line > 0, pltpu.roll(v, COLS, 1), 0.0)
                else:
                    s = v
                q = dh * 3 + dw
                taps_ref[f % 2, q * block : (q + 1) * block, :] = s.astype(B16)

    build(0)
    for copy in copies[8:]:
        copy.wait()
    for f in range(10):
        if f < 9:
            build(f + 1)
        for dt in range(3):
            if 0 <= f - 2 + dt < 8:
                scale = keep_ref[dt, f : f + 1, :1]
                acc_ref[dt, : 9 * block] += scale * dot(taps_ref[f % 2], xs_ref[f - 2 + dt])
    direct = table_ref[c, :, :lanes]
    high = hsum.astype(B16)
    low = (hsum - high.astype(F32)).astype(B16)
    acc_ref[0, 9 * block : 9 * block + hblock] = dot(high, direct) + dot(low, direct)
    loss = jnp.broadcast_to(loss[:, :1], (8, lanes))
    top = loss.astype(B16).astype(F32)
    mid = (loss - top).astype(B16).astype(F32)
    acc_ref[1, 9 * block : 9 * block + 8] = top
    acc_ref[1, 9 * block + 8 : 9 * block + 16] = mid
    acc_ref[1, 9 * block + 16 : 9 * block + 24] = loss - top - mid
    rows = sends[0].shape[1]
    ystep = lanes // ny
    for dt in range(3):
        out_ref[...] = jnp.transpose(acc_ref[dt], (1, 0))
        for d, ref in enumerate(sends):
            to = lax.rem(y + d, ny)
            ref[dt] = out_ref[pl.ds(pl.multiple_of(to * ystep, 8), rows), :].astype(ref.dtype)


def add_kernel(ny, nz, run, *refs):
    gets, (keep_ref, send_ref, sum_ref, part_ref) = refs[:ny], refs[ny:]
    total = gets[0][...]
    for ref in gets[1:]:
        total = total + ref[...].astype(F32)
    chunk = sum_ref.shape[3]
    for i in range(sum_ref.shape[0]):
        sum_ref[i] = total[:, :, i * chunk : (i + 1) * chunk]
    part_ref[...] = jnp.zeros(part_ref.shape, F32)
    step = part_ref.shape[1] // 3
    for z in range(nz):
        for dt in range(3):
            for i in range(sum_ref.shape[0]):
                part_ref[z, dt * step : dt * step + run, i * chunk : (i + 1) * chunk] = sum_ref[
                    i, dt, pl.ds(z, run, stride=nz), :
                ]
    side = lax.rem(place(nz)[3], 2)
    for m in range(nz // 2):
        keep_ref[m] = part_ref[2 * m + side]
        send_ref[m] = part_ref[2 * m + 1 - side].astype(B16)


def pair_kernel(nz, keep_ref, got_ref, *refs):
    sends, sum_ref = refs[:-1], refs[-1]
    sum_ref[...] = keep_ref[...] + got_ref[...].astype(F32)
    m = lax.div(place(nz)[3], 2)
    for d, ref in enumerate(sends):
        ref[...] = sum_ref[lax.rem(m + d, nz // 2)].astype(ref.dtype)


def last_kernel(count, *refs):
    parts, (weight_ref, head_ref, loss_ref) = refs[:count], refs[count:]
    total = parts[0][...]
    for ref in parts[1:]:
        total = total + ref[...].astype(F32)
    run, _, block = weight_ref.shape
    step = total.shape[0] // 3
    for dt in range(3):
        for q in range(9):
            weight_ref[:, dt * 9 + q, :] = total[dt * step : dt * step + run, q * block : (q + 1) * block]
    base = 9 * block
    head_ref[...] = total[:run, base : base + head_ref.shape[1]]
    loss = total[step : step + 1, base : base + 1]
    loss = loss + total[step : step + 1, base + 8 : base + 9]
    loss_ref[...] = loss + total[step : step + 1, base + 16 : base + 17]


def body(frames, conv_weight, head_weight, clip_len):
    nf, nrow, ncol, chans = frames.shape
    band = nrow * ncol
    cells = nf * band
    count = lax.axis_size("tm")
    ny = 4 if count == 64 else 2
    nz = count // 2 // ny
    run = chans // count
    chip = 2 * nf
    shape = jax.ShapeDtypeStruct

    def index(yy, zz, cc):
        return ((yy % ny) * nz + zz % nz) * 2 + cc

    every = [(yy, zz, cc) for yy in range(ny) for zz in range(nz) for cc in range(2)]

    def over_core(v):
        return lax.ppermute(v, "tm", [(i, i ^ 1) for i in range(count)])

    def over_chip(v, d):
        return lax.ppermute(v, "tm", [(i, (i + 2 * d) % count) for i in range(count)])

    def over_x(v, d):
        return lax.ppermute(v, "space", [(i, (i + d) % 4) for i in range(4)])

    def over_y(v, d):
        return lax.ppermute(v, "tm", [(index(a, b, e), index(a + d, b, e)) for a, b, e in every])

    def over_z(v, d):
        return lax.ppermute(v, "tm", [(index(a, b, e), index(a, b + d, e)) for a, b, e in every])

    table = half_table(chans, run, ny, nz)
    lanes = table.shape[2]
    table = np.concatenate([table, table[::-1]], axis=2)
    table = jnp.asarray(table, B16)
    flat = frames.reshape(nf, band, chans)
    edge = shape((nf, ncol, chans), B16)
    top, bot = call(first_kernel, [edge, edge], name="first")(flat)
    top, bot = (
        lax.ppermute(bot, "space", [(i, i + 1) for i in range(3)]),
        lax.ppermute(top, "space", [(i + 1, i) for i in range(3)]),
    )
    flat, top, bot = lax.optimization_barrier((flat, top, bot))
    flats = [flat] + [over_x(flat, d) for d in (1, 2, 3)]
    ends = call(ends_kernel, shape((2, band + 2 * ncol, chans), B16), name="ends")(flat, top, bot)
    ends = lax.ppermute(ends, "tm", [(i, i + 1) for i in range(count - 1)])

    whole = lambda *dims: pl.BlockSpec(dims, lambda i: (0,) * len(dims))
    zlat = head_weight.shape[1]
    hblock = zlat // 4
    block = chans // 4
    message = shape((32 + block, cells), B16)
    latent, *mine_d = call(
        forward_kernel,
        [shape((cells, zlat), F32)] + [message] * 4,
        [
            pltpu.VMEM((cells, chans), F32),
            pltpu.VMEM(((nf + 2) * band, 9 * chans), B16),
            pltpu.VMEM((chans, cells), B16),
            pltpu.VMEM((nf, zlat, chans), F32),
            pltpu.VMEM((3, 9 * chans, chans), B16),
            pltpu.SemaphoreType.DMA((3,)),
        ],
        grid=(1,),
        in_specs=[smem()]
        + [whole(*v.shape) for v in (flat, ends, top, bot)]
        + [pl.BlockSpec(memory_space=pl.ANY), whole(zlat, chans)],
        out_specs=[whole(cells, zlat)] + [whole(*message.shape)] * 4,
        name="forward",
    )(clip_len, flat, ends, top, bot, conv_weight.reshape(3, 9 * chans, chans), head_weight.T)
    mine_d, flats = lax.optimization_barrier((mine_d, flats))
    mine_d = [mine_d[0]] + [over_x(mine_d[d], d) for d in (1, 2, 3)]
    chosen = shape((4, 4 * band, lanes), B16)
    spec = pl.BlockSpec((1, 4 * band, lanes), lambda i: (i, 0, 0))
    xown, xoth = call(
        choose_kernel,
        [chosen, chosen],
        [pltpu.VMEM((4 * band, chans), B16)],
        grid=(4,),
        in_specs=[pl.BlockSpec((1, band, chans), lambda i: (i, 0, 0))] * 4 + [whole(*table.shape)],
        out_specs=[spec, spec],
        name="choose",
    )(*flats, table)
    mine_d, xoth = lax.optimization_barrier((mine_d, xoth))
    core_d = [over_core(v) for v in mine_d]
    xoth = over_core(xoth)

    front = pl.BlockSpec((message.shape[0], 2 * band), lambda i: (0, 0))
    tail = call(
        tail_kernel,
        shape((4, block, 2 * band), B16),
        grid=(1,),
        in_specs=[front] * 4,
        out_specs=whole(4, block, 2 * band),
        name="tail",
    )(*mine_d)
    tail = lax.ppermute(tail, "tm", [(i, i - 2) for i in range(2, count, 2)])
    tail, core_d = lax.optimization_barrier((tail, core_d))
    other = lax.ppermute(tail, "tm", [(i, i + 1) for i in range(0, count, 2)])
    corner = pl.BlockSpec((16, 128), lambda i: (0, 0))
    kchip = call(
        clip_kernel,
        shape((chip, 128), F32),
        grid=(1,),
        in_specs=[corner] * 8,
        out_specs=whole(chip, 128),
        name="clip",
    )(*mine_d, *core_d)
    before, after = over_chip(kchip, 1), over_chip(kchip, -1)
    triple = jnp.stack([before, kchip, after])
    left, right = over_chip(triple, 2), over_chip(triple, -2)

    rows = run * nz
    wrow = 9 * block + 32
    sends = call(
        functools.partial(weight_kernel, ny, nz, float(4 * band)),
        [shape((3, rows, wrow), F32)] + [shape((3, rows, wrow), B16)] * (ny - 1),
        [
            pltpu.VMEM((2, 4) + message.shape, B16),
            pltpu.VMEM((2, 9 * block, 4 * band), B16),
            pltpu.VMEM((3, wrow, lanes), F32),
            pltpu.VMEM((lanes, wrow), F32),
            pltpu.VMEM((8, 4 * band, lanes), B16),
            pltpu.VMEM((2 * chip, 128), F32),
            pltpu.VMEM((3, 2 * chip, 128), F32),
            pltpu.SemaphoreType.DMA((3, 4)),
        ],
        in_specs=[smem()] + [vmem()] * 5 + [pl.BlockSpec(memory_space=pl.ANY)] * 10 + [vmem()],
        name="weight",
    )(clip_len, left, kchip, right, tail, other, *mine_d, *core_d, xown, xoth, table)
    gets = [sends[0]] + [over_y(sends[d], d) for d in range(1, ny)]
    step = wide(run)
    chunk = 128 if wrow % 128 == 0 else wrow
    half = shape((nz // 2, 3 * step, wrow), F32)
    kept, sent = call(
        functools.partial(add_kernel, ny, nz, run),
        [half, shape(half.shape, B16)],
        [pltpu.VMEM((wrow // chunk, 3, rows, chunk), F32), pltpu.VMEM((nz, 3 * step, wrow), F32)],
        name="add",
    )(*gets)
    sent = lax.ppermute(sent, "tm", [(index(a, b, e), index(a, b ^ 1, e)) for a, b, e in every])
    parts = call(
        functools.partial(pair_kernel, nz),
        [shape((3 * step, wrow), F32)] + [shape((3 * step, wrow), B16)] * (nz // 2 - 1),
        [pltpu.VMEM(half.shape, F32)],
        name="pair",
    )(kept, sent)
    parts = [parts[0]] + [over_z(parts[d], 2 * d) for d in range(1, nz // 2)]
    weight_grad, head_grad, loss = call(
        functools.partial(last_kernel, nz // 2),
        [shape((run, 27, block), F32), shape((run, hblock), F32), shape((1, 1), F32)],
        name="last",
    )(*parts)
    return latent.reshape(nf, nrow, ncol, zlat), loss[0, 0], weight_grad.transpose(1, 0, 2), head_grad


def solution(mesh):
    in_specs = (P("tm", "space", None, None), P(), P(), P())
    out_specs = (P("tm", "space", None, None), P(), P(None, "tm", "space"), P("tm", "space"))
    return jax.shard_map(body, mesh=mesh, in_specs=in_specs, out_specs=out_specs, check_vma=False)
```

```python
import functools

import jax
import jax.numpy as jnp
import numpy as np
from jax import lax
from jax.experimental import pallas as pl
from jax.experimental.pallas import tpu as pltpu
from jax.sharding import PartitionSpec as P

F32 = jnp.float32
B16 = jnp.bfloat16
COLS = 24
LIMIT = 56 * 1024 * 1024
NT = (((1,), (1,)), ((), ()))
TN = (((0,), (0,)), ((), ()))


def dot(a, b, dims=None):
    if dims is None:
        return jnp.dot(a, b, preferred_element_type=F32)
    return lax.dot_general(a, b, dims, preferred_element_type=F32)


def call(kernel, outs, scratch=(), **kw):
    params = pltpu.CompilerParams(vmem_limit_bytes=LIMIT)
    return pl.pallas_call(kernel, out_shape=outs, scratch_shapes=list(scratch), compiler_params=params, **kw)


def smem():
    return pl.BlockSpec(memory_space=pltpu.SMEM)


def vmem():
    return pl.BlockSpec(memory_space=pltpu.VMEM)


def place(nz):
    t = lax.axis_index("tm")
    k = lax.div(t, 2)
    return lax.rem(t, 2), lax.axis_index("space"), lax.div(k, nz), lax.rem(k, nz), k


def half_table(chans, run, ny, nz):
    lane = np.arange(chans // 2)
    block = wide(run) * nz
    spot = (lane // run // nz) * block + (lane % run) * nz + lane // run % nz
    table = np.zeros((2, chans, ny * block), np.float32)
    for core in range(2):
        table[core, (lane // run) * 2 * run + core * run + lane % run, spot] = 1
    return table


def wide(run):
    return -(-run // 8) * 8


def first_kernel(x_ref, top_ref, bot_ref):
    nf, band, chans = x_ref.shape
    for f in range(nf):
        wide_frame = x_ref[f].astype(F32)
        top_ref[f] = wide_frame[:COLS].astype(B16)
        bot_ref[f] = wide_frame[band - COLS :].astype(B16)


def frame_of(top, mid, bot):
    return jnp.concatenate([top.astype(F32), mid.astype(F32), bot.astype(F32)], axis=0)


def ends_kernel(x_ref, top_ref, bot_ref, ends_ref):
    nf = x_ref.shape[0]
    for f in range(2):
        g = nf - 2 + f
        ends_ref[f] = frame_of(top_ref[g], x_ref[g], bot_ref[g]).astype(B16)


def choose_kernel(f0, f1, f2, f3, table_ref, own_ref, oth_ref, wide_ref):
    c, x = lax.rem(lax.axis_index("tm"), 2), lax.axis_index("space")
    band = f0.shape[1]

    for d, ref in enumerate((f0, f1, f2, f3)):
        wide_ref[pl.ds(pl.multiple_of(lax.rem(x - d + 4, 4) * band, band), band)] = ref[0]
    both = dot(wide_ref[...], table_ref[c]).astype(B16)
    lanes = own_ref.shape[2]
    own_ref[0] = both[:, :lanes]
    oth_ref[0] = both[:, lanes:]


def forward_kernel(len_ref, x_ref, ends_ref, top_ref, bot_ref, w_ref, hw_ref,
                   lat_ref, d0, d1, d2, d3, pre_ref, wide_ref, turned_ref, head_ref, held_ref, sem):
    nf, band, chans = x_ref.shape
    rows = band + 2 * COLS
    loads = [pltpu.make_async_copy(w_ref.at[dt], held_ref.at[dt], sem.at[dt]) for dt in range(3)]
    for load in loads:
        load.start()
    col = lax.rem(lax.broadcasted_iota(jnp.int32, (rows, 1), 0), COLS)

    def build(f):
        if f < 2:
            v = ends_ref[f].astype(F32)
        else:
            v = frame_of(top_ref[f - 2], x_ref[f - 2], bot_ref[f - 2])
        for dw in range(3):
            if dw == 0:
                s = jnp.where(col > 0, pltpu.roll(v, 1, 0), 0.0)
            elif dw == 2:
                s = jnp.where(col < COLS - 1, pltpu.roll(v, rows - 1, 0), 0.0)
            else:
                s = v
            for dh in range(3):
                q = dh * 3 + dw
                wide_ref[f * band : (f + 1) * band, q * chans : (q + 1) * chans] = s[
                    dh * COLS : dh * COLS + band
                ].astype(B16)

    t, xs = lax.axis_index("tm"), lax.axis_index("space")
    pos = [jnp.int32(0)] * nf
    start = jnp.int32(0)
    for j in range(len_ref.shape[0]):
        for f in range(nf):
            pos[f] = jnp.where(t * nf + f >= start, t * nf + f - start, pos[f])
        start = start + len_ref[j]
    for f in range(nf):
        build(f)
    for dt in range(3):
        if dt:
            build(nf - 1 + dt)
        loads[dt].wait()
        part = dot(wide_ref[dt * band : (dt + nf) * band, :], held_ref[dt])
        for f in range(nf):
            keep = jnp.where(pos[f] >= 2 - dt, 1.0, 0.0)
            piece = keep * part[f * band : (f + 1) * band]
            if dt == 0:
                pre_ref[f * band : (f + 1) * band] = piece
            else:
                pre_ref[f * band : (f + 1) * band] += piece

    zdim = lat_ref.shape[1] // 2
    row = lax.broadcasted_iota(jnp.int32, (16, 128), 0)
    kf = jnp.zeros((16, 128), F32)
    for f in range(nf):
        at = slice(f * band, (f + 1) * band)
        pre = pre_ref[at]
        sig = 1.0 / (1.0 + jnp.exp(-pre))
        act = (pre * sig).astype(B16)
        lat = dot(act, hw_ref[...], NT)
        lat_ref[at] = lat
        lane = lax.broadcasted_iota(jnp.int32, lat.shape, 1)
        grow = jnp.exp(lat) - 1.0
        term = jnp.where(lane < zdim, lat * lat, grow - lat)
        kf = jnp.where(lax.rem(row, nf) == f, 0.5 * jnp.sum(term), kf)
        dlat = jnp.where(lane < zdim, lat, 0.5 * grow).astype(B16)
        dact = dot(dlat, hw_ref[...])
        pre_ref[at] = (dact * sig * (1.0 + pre * (1.0 - sig))).astype(B16).astype(F32)
        head_ref[f] = dot(dlat, act, TN)
    high = kf.astype(B16).astype(F32)
    mid = (kf - high).astype(B16).astype(F32)
    kf = jnp.where(row < nf, high, jnp.where(row < 2 * nf, mid, jnp.where(row < 3 * nf, kf - high - mid, 0.0)))
    turned_ref[...] = jnp.transpose(pre_ref[...], (1, 0)).astype(B16)
    block = chans // 4
    hblock = 2 * zdim // 4
    for d, ref in enumerate((d0, d1, d2, d3)):
        to = lax.rem(xs + d, 4)
        ref[:16, :128] = kf.astype(B16)
        ref[:16, 128:] = jnp.zeros((16, ref.shape[1] - 128), B16)
        ref[32:] = turned_ref[pl.ds(pl.multiple_of(to * block, block), block), :]
        heads = [head_ref[f, pl.ds(pl.multiple_of(to * hblock, hblock), hblock), :] for f in range(nf)]
        pad = ref.shape[1] - 2 * chans
        if pad:
            heads = [jnp.concatenate([h, jnp.zeros((hblock, pad // 2), F32)], axis=1) for h in heads]
        both = jnp.concatenate(
            [jnp.concatenate(heads[:2], axis=1), jnp.concatenate(heads[2:], axis=1)], axis=0
        )
        ref[16:32] = both.astype(B16)


def clip_kernel(*refs):
    c, x = lax.rem(lax.axis_index("tm"), 2), lax.axis_index("space")
    given, (sums_ref, tail_ref) = (refs[:4], refs[4:8]), refs[8:]
    sums = []
    for four in given:
        v = four[0][:16, :128].astype(F32)
        for ref in four[1:]:
            v = v + ref[:16, :128].astype(F32)
        sums.append(v[:4] + v[4:8] + v[8:12])
    for core in range(2):

        @pl.when(c == core)
        def _():
            sums_ref[...] = jnp.concatenate([sums[core], sums[1 - core]], axis=0)
            for d in range(4):
                tail_ref[lax.rem(x - d + 4, 4)] = given[core][d][32:, :]


def weight_kernel(ny, nz, per_frame, len_ref, left_ref, mid_ref, right_ref, next_ref, a0, a1, a2, a3, b0, b1, b2, b3,
                  x_ref, xo_ref, table_ref, *refs):
    sends, (held_ref, taps_ref, acc_ref, out_ref, xs_ref, g_ref, keep_ref, sem) = refs[:ny], refs[ny:]
    c, x, y, _, k = place(nz)
    copies = []
    for core, given, s in ((c, (a0, a1, a2, a3), 0), (1 - c, (b0, b1, b2, b3), 1)):
        for d, ref in enumerate(given):
            copies.append(pltpu.make_async_copy(ref, held_ref.at[core, lax.rem(x - d + 4, 4)], sem.at[s, d]))
    for core, ref, s in ((c, x_ref, 0), (1 - c, xo_ref, 1)):
        copies.append(pltpu.make_async_copy(ref, xs_ref.at[pl.ds(4 * core, 4)], sem.at[2, s]))
    for copy in copies:
        copy.start()
    full = x_ref.shape[1]
    band = full // 4
    block = taps_ref.shape[1] // 9
    chans = table_ref.shape[1]
    lanes = acc_ref.shape[2]
    hblock = 8
    half = full // 2
    window = jnp.concatenate(
        [left_ref[0], left_ref[1], left_ref[2], mid_ref[...], right_ref[0], right_ref[1], right_ref[2]], axis=0
    )
    chip = mid_ref.shape[0]
    wids = chip * (k - 3) + lax.broadcasted_iota(jnp.int32, window.shape, 0)
    ids = chip * k + lax.broadcasted_iota(jnp.int32, g_ref.shape, 0)
    total = jnp.zeros(g_ref.shape, F32)
    lens = jnp.ones(g_ref.shape, F32)
    pos = jnp.full(g_ref.shape, -1, jnp.int32)
    start = jnp.int32(0)
    for j in range(len_ref.shape[0]):
        size = len_ref[j]
        inside = jnp.where((wids >= start) & (wids < start + size), window, 0.0)
        mine = (ids >= start) & (ids < start + size)
        total = jnp.where(mine, jnp.sum(inside, axis=0, keepdims=True), total)
        lens = jnp.where(mine, size.astype(F32), lens)
        pos = jnp.where(mine, ids - start, pos)
        start = start + size
    gain = lens / (lens * per_frame + total)
    g_ref[...] = gain
    for dt in range(3):
        keep_ref[dt] = jnp.where(pos >= 2 - dt, gain, 0.0)
    row = lax.broadcasted_iota(jnp.int32, g_ref.shape, 0)
    loss = jnp.where((pos == 0) & (row < chip), lens * jnp.log1p(total / (lens * per_frame)), 0.0)
    loss = jnp.sum(loss, axis=0, keepdims=True)
    hsum = jnp.zeros((hblock, chans), F32)
    for copy in copies[:8]:
        copy.wait()
    for core in range(2):
        for xs in range(4):
            tail = held_ref[core, xs, 16:32, :].astype(F32)
            for f in range(4):
                part = tail[(f // 2) * hblock : (f // 2 + 1) * hblock, (f % 2) * half : (f % 2) * half + chans]
                hsum = hsum + g_ref[core * 4 + f : core * 4 + f + 1, :1] * part
    acc_ref[...] = jnp.zeros(acc_ref.shape, F32)
    lane = lax.broadcasted_iota(jnp.int32, (1, full), 1)
    col = lax.rem(lane, COLS)
    line = lane // COLS

    def build(f):
        core, lf = f // 4 % 2, f % 4
        frame = jnp.zeros((block, full), F32)
        for xs in range(4):
            if f < 8:
                v = held_ref[core, xs, 32:, :].astype(F32)
            else:
                v = next_ref[xs].astype(F32)
                v = jnp.concatenate([v, jnp.zeros_like(v)], axis=1)
            shift = ((xs - lf) * band) % full
            if shift:
                v = pltpu.roll(v, shift, 1)
            frame = jnp.where(lane // band == xs, v, frame)
        for dw in range(3):
            if dw == 0:
                v = jnp.where(col < COLS - 1, pltpu.roll(frame, full - 1, 1), 0.0)
            elif dw == 2:
                v = jnp.where(col > 0, pltpu.roll(frame, 1, 1), 0.0)
            else:
                v = frame
            for dh in range(3):
                if dh == 0:
                    s = jnp.where(line < full // COLS - 1, pltpu.roll(v, full - COLS, 1), 0.0)
                elif dh == 2:
                    s = jnp.where(line > 0, pltpu.roll(v, COLS, 1), 0.0)
                else:
                    s = v
                q = dh * 3 + dw
                taps_ref[f % 2, q * block : (q + 1) * block, :] = s.astype(B16)

    build(0)
    for copy in copies[8:]:
        copy.wait()
    for f in range(10):
        if f < 9:
            build(f + 1)
        for dt in range(3):
            if 0 <= f - 2 + dt < 8:
                scale = keep_ref[dt, f : f + 1, :1]
                acc_ref[dt, : 9 * block] += scale * dot(taps_ref[f % 2], xs_ref[f - 2 + dt])
    direct = table_ref[c, :, :lanes]
    high = hsum.astype(B16)
    low = (hsum - high.astype(F32)).astype(B16)
    acc_ref[0, 9 * block : 9 * block + hblock] = dot(high, direct) + dot(low, direct)
    loss = jnp.broadcast_to(loss[:, :1], (8, lanes))
    top = loss.astype(B16).astype(F32)
    mid = (loss - top).astype(B16).astype(F32)
    acc_ref[1, 9 * block : 9 * block + 8] = top
    acc_ref[1, 9 * block + 8 : 9 * block + 16] = mid
    acc_ref[1, 9 * block + 16 : 9 * block + 24] = loss - top - mid
    rows = sends[0].shape[1]
    ystep = lanes // ny
    for dt in range(3):
        out_ref[...] = jnp.transpose(acc_ref[dt], (1, 0))
        for d, ref in enumerate(sends):
            to = lax.rem(y + d, ny)
            ref[dt] = out_ref[pl.ds(pl.multiple_of(to * ystep, 8), rows), :].astype(ref.dtype)


def add_kernel(ny, nz, run, *refs):
    gets, sends, (sum_ref, part_ref) = refs[:ny], refs[ny : ny + nz], refs[ny + nz :]
    total = gets[0][...]
    for ref in gets[1:]:
        total = total + ref[...].astype(F32)
    chunk = sum_ref.shape[3]
    for i in range(sum_ref.shape[0]):
        sum_ref[i] = total[:, :, i * chunk : (i + 1) * chunk]
    part_ref[...] = jnp.zeros(part_ref.shape, F32)
    step = part_ref.shape[1] // 3
    for z in range(nz):
        for dt in range(3):
            for i in range(sum_ref.shape[0]):
                part_ref[z, dt * step : dt * step + run, i * chunk : (i + 1) * chunk] = sum_ref[
                    i, dt, pl.ds(z, run, stride=nz), :
                ]
    for d, ref in enumerate(sends):
        ref[...] = part_ref[lax.rem(place(nz)[3] + d, nz)].astype(ref.dtype)


def last_kernel(count, *refs):
    parts, (weight_ref, head_ref, loss_ref) = refs[:count], refs[count:]
    total = parts[0][...]
    for ref in parts[1:]:
        total = total + ref[...].astype(F32)
    run, _, block = weight_ref.shape
    step = total.shape[0] // 3
    for dt in range(3):
        for q in range(9):
            weight_ref[:, dt * 9 + q, :] = total[dt * step : dt * step + run, q * block : (q + 1) * block]
    base = 9 * block
    head_ref[...] = total[:run, base : base + head_ref.shape[1]]
    loss = total[step : step + 1, base : base + 1]
    loss = loss + total[step : step + 1, base + 8 : base + 9]
    loss_ref[...] = loss + total[step : step + 1, base + 16 : base + 17]


def body(frames, conv_weight, head_weight, clip_len):
    nf, nrow, ncol, chans = frames.shape
    band = nrow * ncol
    cells = nf * band
    count = lax.axis_size("tm")
    ny = 4 if count == 64 else 2
    nz = count // 2 // ny
    run = chans // count
    chip = 2 * nf
    shape = jax.ShapeDtypeStruct

    def index(yy, zz, cc):
        return ((yy % ny) * nz + zz % nz) * 2 + cc

    every = [(yy, zz, cc) for yy in range(ny) for zz in range(nz) for cc in range(2)]

    def over_core(v):
        return lax.ppermute(v, "tm", [(i, i ^ 1) for i in range(count)])

    def over_chip(v, d):
        return lax.ppermute(v, "tm", [(i, (i + 2 * d) % count) for i in range(count)])

    def over_x(v, d):
        return lax.ppermute(v, "space", [(i, (i + d) % 4) for i in range(4)])

    def over_y(v, d):
        return lax.ppermute(v, "tm", [(index(a, b, e), index(a + d, b, e)) for a, b, e in every])

    def over_z(v, d):
        return lax.ppermute(v, "tm", [(index(a, b, e), index(a, b + d, e)) for a, b, e in every])

    table = half_table(chans, run, ny, nz)
    lanes = table.shape[2]
    table = np.concatenate([table, table[::-1]], axis=2)
    table = jnp.asarray(table, B16)
    flat = frames.reshape(nf, band, chans)
    edge = shape((nf, ncol, chans), B16)
    top, bot = call(first_kernel, [edge, edge], name="first")(flat)
    top, bot = (
        lax.ppermute(bot, "space", [(i, i + 1) for i in range(3)]),
        lax.ppermute(top, "space", [(i + 1, i) for i in range(3)]),
    )
    flat, top, bot = lax.optimization_barrier((flat, top, bot))
    flats = [flat] + [over_x(flat, d) for d in (1, 2, 3)]
    ends = call(ends_kernel, shape((2, band + 2 * ncol, chans), B16), name="ends")(flat, top, bot)
    ends = lax.ppermute(ends, "tm", [(i, i + 1) for i in range(count - 1)])

    whole = lambda *dims: pl.BlockSpec(dims, lambda i: (0,) * len(dims))
    zlat = head_weight.shape[1]
    hblock = zlat // 4
    block = chans // 4
    message = shape((32 + block, cells), B16)
    latent, *mine_d = call(
        forward_kernel,
        [shape((cells, zlat), F32)] + [message] * 4,
        [
            pltpu.VMEM((cells, chans), F32),
            pltpu.VMEM(((nf + 2) * band, 9 * chans), B16),
            pltpu.VMEM((chans, cells), B16),
            pltpu.VMEM((nf, zlat, chans), F32),
            pltpu.VMEM((3, 9 * chans, chans), B16),
            pltpu.SemaphoreType.DMA((3,)),
        ],
        grid=(1,),
        in_specs=[smem()]
        + [whole(*v.shape) for v in (flat, ends, top, bot)]
        + [pl.BlockSpec(memory_space=pl.ANY), whole(zlat, chans)],
        out_specs=[whole(cells, zlat)] + [whole(*message.shape)] * 4,
        name="forward",
    )(clip_len, flat, ends, top, bot, conv_weight.reshape(3, 9 * chans, chans), head_weight.T)
    mine_d, flats = lax.optimization_barrier((mine_d, flats))
    mine_d = [mine_d[0]] + [over_x(mine_d[d], d) for d in (1, 2, 3)]
    chosen = shape((4, 4 * band, lanes), B16)
    spec = pl.BlockSpec((1, 4 * band, lanes), lambda i: (i, 0, 0))
    xown, xoth = call(
        choose_kernel,
        [chosen, chosen],
        [pltpu.VMEM((4 * band, chans), B16)],
        grid=(4,),
        in_specs=[pl.BlockSpec((1, band, chans), lambda i: (i, 0, 0))] * 4 + [whole(*table.shape)],
        out_specs=[spec, spec],
        name="choose",
    )(*flats, table)
    mine_d, xoth = lax.optimization_barrier((mine_d, xoth))
    core_d = [over_core(v) for v in mine_d]
    xoth = over_core(xoth)

    front = pl.BlockSpec((message.shape[0], 2 * band), lambda i: (0, 0))
    kchip, tail = call(
        clip_kernel,
        [shape((chip, 128), F32), shape((4, block, 2 * band), B16)],
        grid=(1,),
        in_specs=[front] * 8,
        out_specs=[whole(chip, 128), whole(4, block, 2 * band)],
        name="clip",
    )(*mine_d, *core_d)
    before, after = over_chip(kchip, 1), over_chip(kchip, -1)
    tail, before, after = lax.optimization_barrier((tail, before, after))
    tail = over_chip(tail, -1)
    triple = jnp.stack([before, kchip, after])
    left, right = over_chip(triple, 2), over_chip(triple, -2)

    rows = run * nz
    wrow = 9 * block + 32
    sends = call(
        functools.partial(weight_kernel, ny, nz, float(4 * band)),
        [shape((3, rows, wrow), F32)] + [shape((3, rows, wrow), B16)] * (ny - 1),
        [
            pltpu.VMEM((2, 4) + message.shape, B16),
            pltpu.VMEM((2, 9 * block, 4 * band), B16),
            pltpu.VMEM((3, wrow, lanes), F32),
            pltpu.VMEM((lanes, wrow), F32),
            pltpu.VMEM((8, 4 * band, lanes), B16),
            pltpu.VMEM((2 * chip, 128), F32),
            pltpu.VMEM((3, 2 * chip, 128), F32),
            pltpu.SemaphoreType.DMA((3, 4)),
        ],
        in_specs=[smem()] + [vmem()] * 4 + [pl.BlockSpec(memory_space=pl.ANY)] * 10 + [vmem()],
        name="weight",
    )(clip_len, left, kchip, right, tail, *mine_d, *core_d, xown, xoth, table)
    gets = [sends[0]] + [over_y(sends[d], d) for d in range(1, ny)]
    step = wide(run)
    chunk = 128 if wrow % 128 == 0 else wrow
    parts = call(
        functools.partial(add_kernel, ny, nz, run),
        [shape((3 * step, wrow), F32)] + [shape((3 * step, wrow), B16)] * (nz - 1),
        [pltpu.VMEM((wrow // chunk, 3, rows, chunk), F32), pltpu.VMEM((nz, 3 * step, wrow), F32)],
        name="add",
    )(*gets)
    parts = [parts[0]] + [over_z(parts[d], d) for d in range(1, nz)]
    weight_grad, head_grad, loss = call(
        functools.partial(last_kernel, nz),
        [shape((run, 27, block), F32), shape((run, hblock), F32), shape((1, 1), F32)],
        name="last",
    )(*parts)
    return latent.reshape(nf, nrow, ncol, zlat), loss[0, 0], weight_grad.transpose(1, 0, 2), head_grad


def solution(mesh):
    in_specs = (P("tm", "space", None, None), P(), P(), P())
    out_specs = (P("tm", "space", None, None), P(), P(None, "tm", "space"), P("tm", "space"))
    return jax.shard_map(body, mesh=mesh, in_specs=in_specs, out_specs=out_specs, check_vma=False)
```
